32 devices in a mesh: dp: 8 (over z, y), seq: 4 (over x, core).
Axes of the slice: x: 2, y: 2, z: 4, core: 2. Of those that a mesh axis runs over, the one named last changes fastest.
Arguments:
- frames: bfloat16 [8, 2048, 1024], P('dp', 'seq'), may hold values from -6 to 6
- cotangent: bfloat16 [8, 2048, 1024], P('dp', 'seq'), may hold values from -6 to 6
- lengths: int32 [8, 17], P('dp'), may hold values from 0 to 250, as said below
- attend_weight: bfloat16 [1024, 3072], replicated, may hold values from -0.1875 to 0.1875
- output_weight: bfloat16 [1024, 1024], replicated, may hold values from -0.75 to 0.75
- expand_weight: bfloat16 [1024, 8192], replicated, may hold values from -0.1875 to 0.1875
- shrink_weight: bfloat16 [4096, 1024], replicated, may hold values from -0.09375 to 0.09375
- norm_gains: float32 [2, 1024], replicated, may hold values from 0.25 to 1.75
- norm_biases: float32 [2, 1024], replicated, may hold values from -3 to 3
- layer_scales: float32 [2, 1024], replicated, may hold values from 0.25 to 1.75
Outputs:
- activations: bfloat16 [8, 2048, 1024], P('dp', 'seq')
- input_gradient: bfloat16 [8, 2048, 1024], P('dp', 'seq')
- attend_gradient: float32 [1024, 3072], P('dp')
- output_gradient: float32 [1024, 1024], P('dp')
- expand_gradient: float32 [1024, 8192], P('dp')
- shrink_gradient: float32 [4096, 1024], P(None, 'dp')
- gains_gradient: float32 [2, 1024], P(None, 'dp')
- biases_gradient: float32 [2, 1024], P(None, 'dp')
- scales_gradient: float32 [2, 1024], P(None, 'dp')
The draws below stay inside these ranges and needn't reach their ends.
Inputs may be any that keep to these rules, and one draw needn't show every extreme that they name: In each stream the first clip has 250 frames and each later one 250 or 125, except the last nonempty clip, which ends at the stream's last frame and may be shorter; the lengths sum to 2048, and the entries after the last nonempty clip are 0.
All inputs are finite; a program needn't handle non-finite values.
Results may differ from the reference program's by a relative error of at most 0.019.
Values may be sent and summed in bfloat16 or wider, within the bound.
No kernel may reach another device: no remote copies, remote signals or barrier semaphores. Data moves between devices by JAX's collectives and lax.ppermute only.
A program may use at most 256 MiB of HBM per device.

```python
import math
import jax
import jax.numpy as jnp
from jax import lax

D = 1024
HEADS = 16
HEAD_DIM = 64
FF = 4096
WINDOW = 128
CLIP_LONG = 250
CLIP_SHORT = 125
STREAMS = 8
STREAM_LEN = 2048
CLIPS = 17


def draw_lengths(key, part):
    key = jax.random.fold_in(key, 7)
    picks = jax.random.randint(key, (STREAMS, CLIPS), 0, 2)
    column = jnp.arange(CLIPS, dtype=jnp.int32)[None, :]
    picks = jnp.where(column == 0, 1, picks)
    wanted = jnp.where(picks == 1, CLIP_LONG, CLIP_SHORT).astype(jnp.int32)
    ends = jnp.cumsum(wanted, axis=1)
    starts = ends - wanted
    clipped = jnp.minimum(ends, STREAM_LEN) - starts
    return jnp.maximum(clipped, 0).astype(jnp.int32)


def shard_levels(own_key, extent, shards, smallest, high):
    def one(axis_at, shards_of):
        draws = jax.random.uniform(jax.random.fold_in(jax.random.fold_in(own_key, 6), axis_at), (shards_of,), jnp.float32, smallest / len(shards), high / len(shards))
        return jnp.repeat(jnp.exp(draws), extent[axis_at] // shards_of).reshape((-1,) + (1,) * (len(extent) - axis_at - 1))

    level = one(*shards[0])
    for cut in shards[1:]:
        level = level * one(*cut)
    return level


def scatter_about(key, shape, scale, bound, shards=(), kind=jnp.bfloat16):
    gain = shard_levels(key, shape, shards, -0.22, 0.18) if shards else 1.0
    array = jax.random.normal(key, shape, jnp.float32) * scale * gain
    return jnp.minimum(jnp.maximum(array, -bound), bound).astype(kind)


def setup_inputs(seed: int = 0) -> dict:
    keys = jax.random.split(jax.random.key(seed), 11)
    frames = scatter_about(keys[0], (STREAMS, STREAM_LEN, D), 1.0, 6.0, ((0, 8), (1, 4)))
    cotangent = scatter_about(keys[1], (STREAMS, STREAM_LEN, D), 1.0, 6.0, ((0, 8), (1, 4)))
    lengths = draw_lengths(jax.random.fold_in(keys[10], 71), 0)
    attend_weight = scatter_about(keys[3], (D, 3 * D), D ** -0.5, 0.1875)
    output_weight = scatter_about(keys[4], (D, D), (D // 16) ** -0.5, 0.75)
    expand_weight = scatter_about(keys[5], (D, 2 * FF), D ** -0.5, 0.1875)
    shrink_weight = scatter_about(keys[6], (FF, D), FF ** -0.5, 0.09375)
    norm_gains = jnp.clip(1.0 + 0.15 * jax.random.normal(keys[7], (2, D), jnp.float32), 0.25, 1.75)
    norm_biases = scatter_about(keys[8], (2, D), 0.5, 3.0, (), jnp.float32)
    layer_scales = jnp.clip(1.0 + 0.15 * jax.random.normal(keys[9], (2, D), jnp.float32), 0.25, 1.75)
    return {"frames": frames, "cotangent": cotangent, "lengths": lengths, "attend_weight": attend_weight, "output_weight": output_weight, "expand_weight": expand_weight, "shrink_weight": shrink_weight, "norm_gains": norm_gains, "norm_biases": norm_biases, "layer_scales": layer_scales}


highest = lax.Precision.HIGHEST

@jax.custom_vjp
def low(v):
    return lax.optimization_barrier(v.astype(jnp.bfloat16)).astype(jnp.float32)

@jax.custom_vjp
def low_back(v):
    return v

def low_keep(v):
    return (low(v), None)

def low_pass(kept, grad):
    return (grad,)

def back_keep(v):
    return (v, None)

def back_low(kept, grad):
    return (low(grad),)
low.defvjp(low_keep, low_pass)
low_back.defvjp(back_keep, back_low)

def both_round(value):
    return low(low_back(value))

def layer_norm(values, gain_row, bias_row):
    row_mean = lax.optimization_barrier(jnp.mean(values, axis=-1, keepdims=True))
    centered = values - row_mean
    variance = lax.optimization_barrier(jnp.mean(centered * centered, axis=-1, keepdims=True))
    return centered * lax.rsqrt(variance + 1e-05) * gain_row + bias_row

def rotary_tables(positions):
    half_width = HEAD_DIM // 2
    inverse_freq = jnp.exp(jnp.arange(half_width, dtype=jnp.float32) * (-2.0 * math.log(10000.0) / HEAD_DIM))
    angles = positions.astype(jnp.float32)[..., None] * inverse_freq
    return (jnp.cos(angles), jnp.sin(angles))

def rotate(values, cosine_table, sine_table):
    half_width = values.shape[-1] // 2
    first_half = values[..., :half_width]
    second_half = values[..., half_width:]
    return jnp.concatenate([first_half * cosine_table - second_half * sine_table, second_half * cosine_table + first_half * sine_table], axis=-1)

def attention(queries, keys_rot, values, clip_id):
    block_rows = math.gcd(STREAM_LEN, 512)
    block_count = STREAM_LEN // block_rows
    key_span = block_rows + 2 * WINDOW
    padding = ((WINDOW, WINDOW), (0, 0), (0, 0))
    keys_pad = jnp.pad(keys_rot, padding)
    values_pad = jnp.pad(values, padding)
    clip_pad = jnp.pad(clip_id, (WINDOW, WINDOW), constant_values=-1)
    row_ids = jnp.arange(block_rows, dtype=jnp.int32)[:, None]
    col_ids = jnp.arange(key_span, dtype=jnp.int32)[None, :]
    offset = col_ids - WINDOW - row_ids

    def one_block(block_index):
        first_row = block_index * block_rows
        query_block = lax.dynamic_slice_in_dim(queries, first_row, block_rows, 0)
        key_block = lax.dynamic_slice_in_dim(keys_pad, first_row, key_span, 0)
        value_block = lax.dynamic_slice_in_dim(values_pad, first_row, key_span, 0)
        query_clip = lax.dynamic_slice_in_dim(clip_id, first_row, block_rows, 0)
        key_clip = lax.dynamic_slice_in_dim(clip_pad, first_row, key_span, 0)
        allowed = (jnp.abs(offset) <= WINDOW) & (query_clip[:, None] == key_clip[None, :])
        scores = low_back(jnp.einsum('qhd,khd->hqk', query_block, key_block, precision=highest) * HEAD_DIM ** (-0.5))
        scores = jnp.where(allowed[None], scores, -1e+30)
        row_max = lax.optimization_barrier(jnp.max(scores, axis=-1, keepdims=True))
        weights = jnp.exp(scores - row_max)
        weights = weights / lax.optimization_barrier(jnp.sum(weights, axis=-1, keepdims=True))
        mixed_heads = jnp.einsum('hqk,khd->qhd', low(weights), value_block, precision=highest)
        return mixed_heads.reshape(block_rows, D)
    blocks = lax.map(jax.checkpoint(one_block), jnp.arange(block_count, dtype=jnp.int32))
    return blocks.reshape(STREAM_LEN, D)

def stream_forward(stream_in, clip_lengths, attend_weight, output_weight, expand_weight, shrink_weight, norm_gains, norm_biases, layer_scales):
    frame_ids = jnp.arange(STREAM_LEN, dtype=jnp.int32)
    starts = jnp.cumsum(clip_lengths) - clip_lengths
    inside = frame_ids[:, None] >= starts[None, :]
    clip_id = lax.optimization_barrier(jnp.sum(inside.astype(jnp.int32), axis=1)) - 1
    clip_begin = lax.optimization_barrier(jnp.max(jnp.where(inside, starts[None, :], 0), axis=1))
    cosine_table, sine_table = rotary_tables(frame_ids - clip_begin)
    cosine_table = cosine_table[:, None, :]
    sine_table = sine_table[:, None, :]
    normed_one = low(layer_norm(stream_in, norm_gains[0], norm_biases[0]))
    projected = low_back(jnp.dot(normed_one, attend_weight, precision=highest))
    head_split = projected.reshape(STREAM_LEN, 3, HEADS, HEAD_DIM)
    queries = low(rotate(head_split[:, 0], cosine_table, sine_table))
    keys_rot = low(rotate(head_split[:, 1], cosine_table, sine_table))
    values = low(head_split[:, 2])
    mixed_heads = both_round(attention(queries, keys_rot, values, clip_id))
    attn_branch = low_back(jnp.dot(mixed_heads, output_weight, precision=highest))
    residual = stream_in + attn_branch * layer_scales[0]
    normed_two = low(layer_norm(residual, norm_gains[1], norm_biases[1]))
    gate_and_up = low_back(jnp.dot(normed_two, expand_weight, precision=highest))
    hidden = low(jax.nn.silu(gate_and_up[:, :FF]) * gate_and_up[:, FF:])
    mlp_branch = low_back(jnp.dot(hidden, shrink_weight, precision=highest))
    return residual + mlp_branch * layer_scales[1]

def reference(frames, cotangent, lengths, attend_weight, output_weight, expand_weight, shrink_weight, norm_gains, norm_biases, layer_scales):
    params = tuple((weight.astype(jnp.float32) for weight in (attend_weight, output_weight, expand_weight, shrink_weight, norm_gains, norm_biases, layer_scales)))

    def scan_step(totals, element):
        stream_in, grad_stream, clip_lengths = element

        def forward_all(layer_in, *weight_list):
            return stream_forward(layer_in, clip_lengths, *weight_list)
        result, pullback = jax.vjp(forward_all, stream_in.astype(jnp.float32), *params)
        gradients = pullback(grad_stream.astype(jnp.float32))
        totals = tuple((total + gradient for total, gradient in zip(totals, gradients[1:])))
        return (totals, (result.astype(jnp.bfloat16), gradients[0].astype(jnp.bfloat16)))
    initial = tuple((jnp.zeros(weight.shape, jnp.float32) for weight in params))
    totals, (results, input_grads) = lax.scan(scan_step, initial, (frames, cotangent, lengths))
    return (results, input_grads, totals[0], totals[1], totals[2], totals[3], totals[4], totals[5], totals[6])
```

```python
import functools
import math

import jax
import jax.numpy as jnp
from jax import lax
from jax.experimental import pallas as pl
from jax.experimental.pallas import tpu as pltpu
from jax.sharding import PartitionSpec as P

D = 1024
HEADS = 16
HEAD_DIM = 64
FF = 4096
WINDOW = 128
QUAD = 4 * HEAD_DIM
SLICES = 8
PART = FF // SLICES
HALF = PART // 2
EPS = 1e-05
BF = jnp.bfloat16
F32 = jnp.float32
VMEM_BYTES = 58 * 1024 * 1024


def dot_nn(a, b):
    return lax.dot_general(a, b, (((1,), (0,)), ((), ())), preferred_element_type=F32)


def dot_nt(a, b):
    return lax.dot_general(a, b, (((1,), (1,)), ((), ())), preferred_element_type=F32)


def dot_tn(a, b):
    return lax.dot_general(a, b, (((0,), (0,)), ((), ())), preferred_element_type=F32)


def params(**extra):
    return pltpu.CompilerParams(vmem_limit_bytes=VMEM_BYTES, **extra)


def cost(flops, size, transcendentals=0):
    return pl.CostEstimate(
        flops=int(flops), bytes_accessed=int(size), transcendentals=int(transcendentals)
    )


def whole(shape):
    return pl.BlockSpec(shape, lambda *_: (0,) * len(shape))


def norm_stats(values):
    centered = values - jnp.mean(values, axis=-1, keepdims=True)
    inverse = lax.rsqrt(jnp.mean(centered * centered, axis=-1, keepdims=True) + EPS)
    return (centered * inverse, inverse)


def norm_back(gradient, normed, inverse, gain_row):
    scaled = gradient * gain_row
    return inverse * (
        scaled
        - jnp.mean(scaled, axis=-1, keepdims=True)
        - normed * jnp.mean(scaled * normed, axis=-1, keepdims=True)
    )


def turn(values, cosine, sine, sign):
    lane = lax.broadcasted_iota(jnp.int32, (values.shape[0], 128), 1) % HEAD_DIM
    parts = []
    for group in range(values.shape[1] // 128):
        part = values[:, group * 128 : group * 128 + 128]
        swapped = jnp.where(
            lane < HEAD_DIM // 2, pltpu.roll(part, 96, 1), pltpu.roll(part, 32, 1)
        )
        if sign > 0:
            parts.append(part * cosine + swapped * sine)
        else:
            parts.append(part * cosine - swapped * sine)
    return jnp.concatenate(parts, axis=1)


def tables_kernel(info_ref, lengths_ref, cos_ref, sin_ref, bias_ref):
    wide = cos_ref.shape[0]
    rows = wide - 2 * WINDOW
    base = info_ref[0] * rows
    total = info_ref[1]
    frame = base - WINDOW + lax.broadcasted_iota(jnp.int32, (wide, 128), 0)
    query = base + lax.broadcasted_iota(jnp.int32, (8, rows), 1)
    key_clip = jnp.full((wide, 128), -1, jnp.int32)
    begin = jnp.zeros((wide, 128), jnp.int32)
    query_clip = jnp.full((8, rows), -1, jnp.int32)

    def step(entry, carry):
        start, key_clip, begin, query_clip = carry
        inside = frame >= start
        key_clip = key_clip + inside.astype(jnp.int32)
        begin = jnp.where(inside, start, begin)
        query_clip = query_clip + (query >= start).astype(jnp.int32)
        return (start + lengths_ref[0, entry], key_clip, begin, query_clip)

    _, key_clip, begin, query_clip = lax.fori_loop(
        0, lengths_ref.shape[1], step, (jnp.int32(0), key_clip, begin, query_clip)
    )
    key_clip = jnp.where((frame >= 0) & (frame < total), key_clip, -1)
    lane = lax.broadcasted_iota(jnp.int32, (wide, 128), 1)
    frequency = jnp.exp(
        (lane % (HEAD_DIM // 2)).astype(F32) * (-2.0 * math.log(10000.0) / HEAD_DIM)
    )
    angle = (frame - begin).astype(F32) * frequency
    sine = jnp.sin(angle)
    cos_ref[...] = jnp.cos(angle)
    sin_ref[...] = jnp.where(lane % HEAD_DIM < HEAD_DIM // 2, -sine, sine)
    span = 3 * WINDOW
    gap = lax.broadcasted_iota(jnp.int32, (span, 128), 0) - lax.broadcasted_iota(
        jnp.int32, (span, 128), 1
    )
    near = (gap >= 0) & (gap <= 2 * WINDOW)
    for block in range(rows // WINDOW):
        at = block * WINDOW
        same = key_clip[at : at + span] == query_clip[0:1, at : at + WINDOW]
        bias_ref[block] = jnp.where(near & same, 0.0, -1e30)


def tables_call(info, lengths, rows):
    wide = rows + 2 * WINDOW
    return pl.pallas_call(
        tables_kernel,
        out_shape=(
            jax.ShapeDtypeStruct((wide, 128), F32),
            jax.ShapeDtypeStruct((wide, 128), F32),
            jax.ShapeDtypeStruct((rows // WINDOW, 3 * WINDOW, 128), F32),
        ),
        in_specs=[
            pl.BlockSpec(memory_space=pltpu.SMEM),
            pl.BlockSpec(memory_space=pltpu.SMEM),
        ],
        compiler_params=params(),
        cost_estimate=cost(1e8, 2e6),
        name="tables",
    )(info, lengths)


def project_kernel(x_ref, gain_ref, shift_ref, cos_ref, sin_ref, weight_ref, a1_ref, out_ref):
    chunk = pl.program_id(0)
    rows = x_ref.shape[0]

    @pl.when(chunk == 0)
    def _():
        normed, _unused = norm_stats(x_ref[...].astype(F32))
        a1_ref[...] = (normed * gain_ref[0:1, :] + shift_ref[0:1, :]).astype(BF)

    projected = dot_nn(a1_ref[...], weight_ref[...])
    cosine = cos_ref[WINDOW : WINDOW + rows, :]
    sine = sin_ref[WINDOW : WINDOW + rows, :]

    @pl.when(chunk < 2)
    def _():
        out_ref[...] = (turn(projected, cosine, sine, 1) * HEAD_DIM**-0.5).astype(BF)

    @pl.when((chunk >= 2) & (chunk < 4))
    def _():
        out_ref[...] = turn(projected, cosine, sine, 1).astype(BF)

    @pl.when(chunk >= 4)
    def _():
        out_ref[...] = projected.astype(BF)


def project_call(x, gains, shifts, cosine, sine, weight):
    rows = x.shape[0]
    wide = cosine.shape[0]
    return pl.pallas_call(
        project_kernel,
        grid=(6,),
        out_shape=(
            jax.ShapeDtypeStruct((rows, D), BF),
            jax.ShapeDtypeStruct((rows, 3 * D), BF),
        ),
        in_specs=[
            whole((rows, D)),
            whole((2, D)),
            whole((2, D)),
            whole((wide, 128)),
            whole((wide, 128)),
            pl.BlockSpec((D, 512), lambda c: (0, c)),
        ],
        out_specs=(whole((rows, D)), pl.BlockSpec((rows, 512), lambda c: (0, c))),
        compiler_params=params(),
        cost_estimate=cost(2 * rows * D * 3 * D, 12e6),
        name="project",
    )(x, gains, shifts, cosine, sine, weight)


def rim_kernel(
    low_ref, high_ref, gain_ref, shift_ref, cos_ref, sin_ref, weight_ref, out_ref, a1_ref
):
    chunk = pl.program_id(0)
    wide = cos_ref.shape[0]

    @pl.when(chunk == 0)
    def _():
        for at, ref in ((0, low_ref), (WINDOW, high_ref)):
            normed, _unused = norm_stats(ref[...].astype(F32))
            a1_ref[at : at + WINDOW, :] = (
                normed * gain_ref[0:1, :] + shift_ref[0:1, :]
            ).astype(BF)

    projected = dot_nn(a1_ref[...], weight_ref[...])

    @pl.when(chunk < 2)
    def _():
        cosine = jnp.concatenate([cos_ref[:WINDOW, :], cos_ref[wide - WINDOW :, :]], axis=0)
        sine = jnp.concatenate([sin_ref[:WINDOW, :], sin_ref[wide - WINDOW :, :]], axis=0)
        out_ref[...] = turn(projected, cosine, sine, 1).astype(BF)

    @pl.when(chunk >= 2)
    def _():
        out_ref[...] = projected.astype(BF)


def rim_call(low, high, gains, shifts, cosine, sine, weight):
    wide = cosine.shape[0]
    return pl.pallas_call(
        rim_kernel,
        grid=(4,),
        out_shape=jax.ShapeDtypeStruct((2 * WINDOW, 2 * D), BF),
        in_specs=[
            whole((WINDOW, D)),
            whole((WINDOW, D)),
            whole((2, D)),
            whole((2, D)),
            whole((wide, 128)),
            whole((wide, 128)),
            pl.BlockSpec((D, 512), lambda c: (0, c + 2)),
        ],
        out_specs=pl.BlockSpec((2 * WINDOW, 512), lambda c: (0, c)),
        scratch_shapes=[pltpu.VMEM((2 * WINDOW, D), BF)],
        compiler_params=params(),
        cost_estimate=cost(2 * 256 * D * 2 * D, 6e6),
        name="rim",
    )(low, high, gains, shifts, cosine, sine, weight)


def stacked(block):
    owner = lax.broadcasted_iota(jnp.int32, block.shape, 1) // HEAD_DIM
    zero = jnp.zeros_like(block)
    return jnp.concatenate([jnp.where(owner == head, block, zero) for head in range(4)], axis=0)


def attend_kernel(
    q_ref,
    k_ref,
    v_ref,
    rim_k_ref,
    rim_v_ref,
    bias_ref,
    weight_ref,
    x_ref,
    gain_ref,
    shift_ref,
    scale_ref,
    o_ref,
    lse_ref,
    x1_ref,
    attn_ref,
    a2_ref,
    keys,
    values_t,
    mixed_t,
    total,
):
    quad = pl.program_id(0)
    rows = q_ref.shape[0]
    keys[0:WINDOW, :] = rim_k_ref[0:WINDOW, :]
    keys[WINDOW : WINDOW + rows, :] = k_ref[...]
    keys[WINDOW + rows :, :] = rim_k_ref[WINDOW:, :]
    values_t[:, 0:WINDOW] = rim_v_ref[0:WINDOW, :].T
    values_t[:, WINDOW : WINDOW + rows] = v_ref[...].T
    values_t[:, WINDOW + rows :] = rim_v_ref[WINDOW:, :].T
    for block in range(rows // WINDOW):
        at = block * WINDOW
        queries = stacked(q_ref[at : at + WINDOW, :])
        scores = dot_nt(keys[at : at + 3 * WINDOW, :], queries)
        bias = bias_ref[block]
        scores = scores + jnp.concatenate([bias] * 4, axis=1)
        top = jnp.max(scores, axis=0, keepdims=True)
        weights = jnp.exp(scores - top)
        total_row = jnp.sum(weights, axis=0, keepdims=True)
        weights = (weights * (1.0 / total_row)).astype(BF)
        log_row = top + jnp.log(total_row)
        for head in range(4):
            lanes = slice(head * WINDOW, head * WINDOW + WINDOW)
            lse_ref[0, head : head + 1, at : at + WINDOW] = log_row[:, lanes]
            feature = slice(head * HEAD_DIM, head * HEAD_DIM + HEAD_DIM)
            mixed_t[feature, at : at + WINDOW] = dot_nn(
                values_t[feature, at : at + 3 * WINDOW], weights[:, lanes]
            )
    mixed = mixed_t[...].T.astype(BF)
    o_ref[...] = mixed
    branch = dot_nn(mixed, weight_ref[...])

    @pl.when(quad == 0)
    def _():
        total[...] = branch

    @pl.when(quad > 0)
    def _():
        total[...] += branch

    @pl.when(quad == HEADS // 4 - 1)
    def _():
        attn = total[...]
        residual = x_ref[...].astype(F32) + attn * scale_ref[0:1, :]
        normed, _unused = norm_stats(residual)
        x1_ref[...] = residual
        attn_ref[...] = attn.astype(BF)
        a2_ref[...] = (normed * gain_ref[1:2, :] + shift_ref[1:2, :]).astype(BF)


def attend_call(qkv, rim, bias, weight, x, gains, shifts, scales):
    rows = x.shape[0]
    wide = rows + 2 * WINDOW
    row_spec = whole((rows, D))
    return pl.pallas_call(
        attend_kernel,
        grid=(HEADS // 4,),
        out_shape=(
            jax.ShapeDtypeStruct((rows, D), BF),
            jax.ShapeDtypeStruct((HEADS // 4, 8, rows), F32),
            jax.ShapeDtypeStruct((rows, D), F32),
            jax.ShapeDtypeStruct((rows, D), BF),
            jax.ShapeDtypeStruct((rows, D), BF),
        ),
        in_specs=[
            pl.BlockSpec((rows, QUAD), lambda h: (0, h)),
            pl.BlockSpec((rows, QUAD), lambda h: (0, h + 4)),
            pl.BlockSpec((rows, QUAD), lambda h: (0, h + 8)),
            pl.BlockSpec((2 * WINDOW, QUAD), lambda h: (0, h)),
            pl.BlockSpec((2 * WINDOW, QUAD), lambda h: (0, h + 4)),
            whole(bias.shape),
            pl.BlockSpec((QUAD, D), lambda h: (h, 0)),
            row_spec,
            whole((2, D)),
            whole((2, D)),
            whole((2, D)),
        ],
        out_specs=(
            pl.BlockSpec((rows, QUAD), lambda h: (0, h)),
            pl.BlockSpec((1, 8, rows), lambda h: (h, 0, 0)),
            row_spec,
            row_spec,
            row_spec,
        ),
        scratch_shapes=[
            pltpu.VMEM((wide, QUAD), BF),
            pltpu.VMEM((QUAD, wide), BF),
            pltpu.VMEM((QUAD, rows), F32),
            pltpu.VMEM((rows, D), F32),
        ],
        compiler_params=params(),
        cost_estimate=cost(8e9, 14e6, 3e6),
        name="attend",
    )(qkv, qkv, qkv, rim, rim, bias, weight, x, gains, shifts, scales)


def gated(gate, up, grad_hidden):
    sigmoid = 0.5 * jnp.tanh(0.5 * gate) + 0.5
    swish = gate * sigmoid
    hidden = swish * up
    grad_gate = grad_hidden * up * (sigmoid + swish * (1.0 - sigmoid))
    grad_up = grad_hidden * swish
    return (hidden.astype(BF), grad_gate.astype(BF), grad_up.astype(BF))


def feed_kernel(
    a2_ref,
    dy_ref,
    x1_ref,
    attn_ref,
    gain_ref,
    scale_ref,
    gate_w_ref,
    up_w_ref,
    shrink_w_ref,
    act_ref,
    dx1_ref,
    dattn_ref,
    small_ref,
    branch_grad,
    mlp,
    back,
):
    chunk = pl.program_id(0)

    @pl.when(chunk == 0)
    def _():
        branch_grad[...] = (dy_ref[...].astype(F32) * scale_ref[1:2, :]).astype(BF)

    a2 = a2_ref[...]
    gate = dot_nn(a2, gate_w_ref[...])
    up = dot_nn(a2, up_w_ref[...])
    grad_hidden = dot_nt(branch_grad[...], shrink_w_ref[...])
    hidden, grad_gate, grad_up = gated(gate, up, grad_hidden)
    branch = dot_nn(hidden, shrink_w_ref[...])
    back_part = dot_nt(grad_gate, gate_w_ref[...]) + dot_nt(grad_up, up_w_ref[...])

    @pl.when(chunk == 0)
    def _():
        mlp[...] = branch
        back[...] = back_part

    @pl.when(chunk > 0)
    def _():
        mlp[...] += branch
        back[...] += back_part

    @pl.when(chunk == pl.num_programs(0) - 1)
    def _():
        residual = x1_ref[...]
        grad_result = dy_ref[...].astype(F32)
        branch = mlp[...]
        act_ref[...] = (residual + branch * scale_ref[1:2, :]).astype(BF)
        small_ref[0:1, :] = jnp.sum(grad_result * branch, axis=0, keepdims=True)
        grad_normed = back[...]
        normed, inverse = norm_stats(residual)
        small_ref[1:2, :] = jnp.sum(grad_normed * normed, axis=0, keepdims=True)
        small_ref[2:3, :] = jnp.sum(grad_normed, axis=0, keepdims=True)
        grad_residual = grad_result + norm_back(grad_normed, normed, inverse, gain_ref[1:2, :])
        dx1_ref[...] = grad_residual
        small_ref[3:4, :] = jnp.sum(
            grad_residual * attn_ref[...].astype(F32), axis=0, keepdims=True
        )
        small_ref[4:8, :] = jnp.zeros((4, D), F32)
        dattn_ref[...] = (grad_residual * scale_ref[0:1, :]).astype(BF)


def feed_call(a2, dy, x1, attn, gains, scales, expand, shrink):
    rows = a2.shape[0]
    size = 512
    count = FF // size
    row_spec = whole((rows, D))
    return pl.pallas_call(
        feed_kernel,
        grid=(count,),
        out_shape=(
            jax.ShapeDtypeStruct((rows, D), BF),
            jax.ShapeDtypeStruct((rows, D), F32),
            jax.ShapeDtypeStruct((rows, D), BF),
            jax.ShapeDtypeStruct((8, D), F32),
        ),
        in_specs=[
            row_spec,
            row_spec,
            row_spec,
            row_spec,
            whole((2, D)),
            whole((2, D)),
            pl.BlockSpec((D, size), lambda f: (0, f)),
            pl.BlockSpec((D, size), lambda f: (0, f + count)),
            pl.BlockSpec((size, D), lambda f: (f, 0)),
        ],
        out_specs=(row_spec, row_spec, row_spec, whole((8, D))),
        scratch_shapes=[
            pltpu.VMEM((rows, D), BF),
            pltpu.VMEM((rows, D), F32),
            pltpu.VMEM((rows, D), F32),
        ],
        compiler_params=params(),
        cost_estimate=cost(2 * rows * D * FF * 6, 36e6, rows * FF),
        name="feed",
    )(a2, dy, x1, attn, gains, scales, expand, expand, shrink)


def slice_kernel(pieces, outer, info_ref, *refs):
    a2_refs = refs[: len(pieces)]
    dy_refs = refs[len(pieces) : 2 * len(pieces)]
    scale_ref, gate_w_ref, up_w_ref, shrink_w_ref = refs[2 * len(pieces) : 2 * len(pieces) + 4]
    send_ref, keep_ref, a2_all, dy_all, acc, acc_shrink, sems = refs[2 * len(pieces) + 4 :]
    rows = a2_all.shape[1]
    groups = a2_all.shape[0]
    for number, (slot, first, size) in enumerate(pieces):
        for kind, (sources, held) in enumerate(((a2_refs, a2_all), (dy_refs, dy_all))):
            pltpu.make_async_copy(
                sources[number],
                held.at[slot, pl.ds(first, size), :],
                sems.at[kind, slot],
            ).start()
    acc[...] = jnp.zeros_like(acc)
    acc_shrink[...] = jnp.zeros_like(acc_shrink)

    def step(slot, _):
        for kind, held in enumerate((a2_all, dy_all)):
            pltpu.make_async_copy(held.at[slot], held.at[slot], sems.at[kind, slot]).wait()
        a2 = a2_all[slot]
        branch_grad = (dy_all[slot].astype(F32) * scale_ref[1:2, :]).astype(BF)
        gate = dot_nn(a2, gate_w_ref[...])
        up = dot_nn(a2, up_w_ref[...])
        grad_hidden = dot_nt(branch_grad, shrink_w_ref[...])
        hidden, grad_gate, grad_up = gated(gate, up, grad_hidden)
        acc[...] += dot_tn(a2, jnp.concatenate([grad_gate, grad_up], axis=1))
        acc_shrink[...] += dot_tn(branch_grad, hidden)
        return 0

    lax.fori_loop(0, groups, step, 0)
    mine = info_ref[1]
    span = D // (2 * outer)
    for at in range(outer):
        for target, bit in ((send_ref, 1 - mine), (keep_ref, mine)):
            first = pl.multiple_of(at * 2 * span + bit * span, span)
            target[at, :, : 2 * HALF] = acc[pl.ds(first, span), :].astype(BF)
            target[at, :, 2 * HALF :] = acc_shrink[pl.ds(first, span), :].astype(BF)


def slice_call(info, a2_list, dy_list, scales, expand, shrink, rows, outer):
    pieces = []
    slot, first = 0, 0
    for piece in a2_list:
        pieces.append((slot, first, piece.shape[0]))
        first += piece.shape[0]
        if first == rows:
            slot, first = slot + 1, 0
    groups = slot
    span = D // (2 * outer)
    hbm = pl.BlockSpec(memory_space=pl.ANY)
    result = jax.ShapeDtypeStruct((outer, span, 3 * HALF), BF)
    out_spec = pl.BlockSpec((outer, span, 3 * HALF), lambda i, info: (0, 0, 0))
    return pl.pallas_call(
        functools.partial(slice_kernel, tuple(pieces), outer),
        grid_spec=pltpu.PrefetchScalarGridSpec(
            num_scalar_prefetch=1,
            grid=(1,),
            in_specs=[hbm] * (2 * len(pieces))
            + [
                pl.BlockSpec((2, D), lambda i, info: (0, 0)),
                pl.BlockSpec((D, HALF), lambda i, info: (0, info[0])),
                pl.BlockSpec((D, HALF), lambda i, info: (0, info[0] + FF // HALF)),
                pl.BlockSpec((HALF, D), lambda i, info: (info[0], 0)),
            ],
            out_specs=(out_spec, out_spec),
            scratch_shapes=[
                pltpu.VMEM((groups, rows, D), BF),
                pltpu.VMEM((groups, rows, D), BF),
                pltpu.VMEM((D, 2 * HALF), F32),
                pltpu.VMEM((D, HALF), F32),
                pltpu.SemaphoreType.DMA((2, groups)),
            ],
        ),
        out_shape=(result, result),
        compiler_params=params(),
        cost_estimate=cost(2 * groups * rows * D * HALF * 6, 22e6, groups * rows * HALF),
        name="slice_grads",
    )(info, *a2_list, *dy_list, scales, expand, expand, shrink)


def attend_back_kernel(
    info_ref,
    q_ref,
    k_ref,
    v_ref,
    rim_k_ref,
    rim_v_ref,
    bias_ref,
    cos_ref,
    sin_ref,
    lse_ref,
    o_ref,
    dattn_ref,
    weight_ref,
    dq_ref,
    dk_ref,
    dv_ref,
    low_ref,
    high_ref,
    send_ref,
    keep_ref,
    keys,
    values,
    keys_t,
    grad_q_t,
    grad_k,
    grad_v,
):
    rows = q_ref.shape[0]
    for held, own, rim in ((keys, k_ref, rim_k_ref), (values, v_ref, rim_v_ref)):
        held[0:WINDOW, :] = rim[0:WINDOW, :]
        held[WINDOW : WINDOW + rows, :] = own[...]
        held[WINDOW + rows :, :] = rim[WINDOW:, :]
    keys_t[...] = keys[...].T
    dattn = dattn_ref[...]
    grad_mixed = dot_nt(dattn, weight_ref[...]).astype(BF)
    outer = dot_tn(o_ref[...], dattn).astype(BF)
    for core in range(2):

        @pl.when(info_ref[2] == core)
        def _():
            for half in range(2):
                for target, bit in ((keep_ref, core), (send_ref, 1 - core)):
                    first = (2 * half + bit) * QUAD
                    target[half] = outer[:, first : first + QUAD]

    grad_k[...] = jnp.zeros_like(grad_k)
    grad_v[...] = jnp.zeros_like(grad_v)
    for block in range(rows // WINDOW):
        at = block * WINDOW
        span = slice(at, at + 3 * WINDOW)
        queries = stacked(q_ref[at : at + WINDOW, :])
        grad_out = stacked(grad_mixed[at : at + WINDOW, :])
        scores = dot_nt(keys[span, :], queries)
        log_row = jnp.concatenate(
            [lse_ref[0, head : head + 1, at : at + WINDOW] for head in range(4)], axis=1
        )
        bias = bias_ref[block]
        weights = jnp.exp(scores + jnp.concatenate([bias] * 4, axis=1) - log_row)
        grad_weights = dot_nt(values[span, :], grad_out)
        weighted = weights * grad_weights
        grad_scores = weighted - weights * jnp.sum(weighted, axis=0, keepdims=True)
        grad_scores = grad_scores.astype(BF)
        grad_v[span, :] += dot_nn(weights.astype(BF), grad_out)
        grad_k[span, :] += dot_nn(grad_scores, queries)
        for head in range(4):
            feature = slice(head * HEAD_DIM, head * HEAD_DIM + HEAD_DIM)
            grad_q_t[feature, at : at + WINDOW] = dot_nn(
                keys_t[feature, span], grad_scores[:, head * WINDOW : head * WINDOW + WINDOW]
            )
    own = slice(WINDOW, WINDOW + rows)
    cosine, sine = cos_ref[...], sin_ref[...]
    dq_ref[...] = turn(
        grad_q_t[...].T * HEAD_DIM**-0.5, cosine[own, :], sine[own, :], -1
    ).astype(BF)
    turned = turn(grad_k[...], cosine, sine, -1).astype(BF)
    grad_values = grad_v[...].astype(BF)
    dk_ref[...] = turned[own, :]
    dv_ref[...] = grad_values[own, :]
    low_ref[0] = turned[:WINDOW, :]
    low_ref[1] = grad_values[:WINDOW, :]
    high_ref[0] = turned[WINDOW + rows :, :]
    high_ref[1] = grad_values[WINDOW + rows :, :]


def attend_back_call(info, qkv, rim, bias, cosine, sine, lse, o, dattn, weight):
    rows = o.shape[0]
    wide = rows + 2 * WINDOW
    row_shape = jax.ShapeDtypeStruct((rows, D), BF)
    rim_shape = jax.ShapeDtypeStruct((2, WINDOW, D), BF)
    grad_shape = jax.ShapeDtypeStruct((2, D, QUAD), BF)
    row_spec = pl.BlockSpec((rows, QUAD), lambda h, info: (0, h))
    rim_spec = pl.BlockSpec((2, WINDOW, QUAD), lambda h, info: (0, 0, h))
    grad_spec = pl.BlockSpec((2, QUAD, QUAD), lambda h, info: (0, h, 0))
    return pl.pallas_call(
        attend_back_kernel,
        grid_spec=pltpu.PrefetchScalarGridSpec(
            num_scalar_prefetch=1,
            grid=(HEADS // 4,),
            in_specs=[
                row_spec,
                pl.BlockSpec((rows, QUAD), lambda h, info: (0, h + 4)),
                pl.BlockSpec((rows, QUAD), lambda h, info: (0, h + 8)),
                pl.BlockSpec((2 * WINDOW, QUAD), lambda h, info: (0, h)),
                pl.BlockSpec((2 * WINDOW, QUAD), lambda h, info: (0, h + 4)),
                whole(bias.shape),
                whole((wide, 128)),
                whole((wide, 128)),
                pl.BlockSpec((1, 8, rows), lambda h, info: (h, 0, 0)),
                row_spec,
                whole((rows, D)),
                pl.BlockSpec((QUAD, D), lambda h, info: (h, 0)),
            ],
            out_specs=(row_spec, row_spec, row_spec, rim_spec, rim_spec, grad_spec, grad_spec),
            scratch_shapes=[
                pltpu.VMEM((wide, QUAD), BF),
                pltpu.VMEM((wide, QUAD), BF),
                pltpu.VMEM((QUAD, wide), BF),
                pltpu.VMEM((QUAD, rows), F32),
                pltpu.VMEM((wide, QUAD), F32),
                pltpu.VMEM((wide, QUAD), F32),
            ],
        ),
        out_shape=(
            row_shape,
            row_shape,
            row_shape,
            rim_shape,
            rim_shape,
            grad_shape,
            grad_shape,
        ),
        compiler_params=params(),
        cost_estimate=cost(2e10, 20e6, 3e6),
        name="attend_back",
    )(info, qkv, qkv, qkv, rim, rim, bias, cosine, sine, lse, o, dattn, weight)


def project_back_kernel(
    info_ref,
    dq_ref,
    dk_ref,
    dv_ref,
    low_ref,
    high_ref,
    a1_ref,
    x_ref,
    dx1_ref,
    gain_ref,
    weight_ref,
    grad_ref,
    small_ref,
    send_ref,
    keep_ref,
    part,
    back,
):
    chunk = pl.program_id(0)
    rows = dq_ref.shape[0]
    lanes = pl.ds(pl.multiple_of((chunk % 2) * 512, 512), 512)

    @pl.when(chunk < 2)
    def _():
        part[...] = dq_ref[:, lanes]

    for kind, ref in ((0, dk_ref), (1, dv_ref)):

        @pl.when(chunk // 2 == kind + 1)
        def _():
            part[WINDOW : rows - WINDOW, :] = ref[WINDOW : rows - WINDOW, lanes]
            for at, rim in ((0, low_ref), (rows - WINDOW, high_ref)):
                part[at : at + WINDOW, :] = (
                    ref[at : at + WINDOW, lanes].astype(F32) + rim[kind, :, lanes].astype(F32)
                ).astype(BF)

    grad_part = part[...]
    back_part = dot_nt(grad_part, weight_ref[...])

    @pl.when(chunk == 0)
    def _():
        back[...] = back_part

    @pl.when(chunk > 0)
    def _():
        back[...] += back_part

    outer = dot_tn(a1_ref[...], grad_part).astype(BF)
    for core in range(2):

        @pl.when(info_ref[2] == core)
        def _():
            keep_ref[0, 0] = outer[:, core * QUAD : core * QUAD + QUAD]
            send_ref[0, 0] = outer[:, (1 - core) * QUAD : (1 - core) * QUAD + QUAD]

    @pl.when(chunk == pl.num_programs(0) - 1)
    def _():
        grad_normed = back[...]
        normed, inverse = norm_stats(x_ref[...].astype(F32))
        small_ref[0:1, :] = jnp.sum(grad_normed * normed, axis=0, keepdims=True)
        small_ref[1:2, :] = jnp.sum(grad_normed, axis=0, keepdims=True)
        small_ref[2:8, :] = jnp.zeros((6, D), F32)
        grad_ref[...] = (
            dx1_ref[...] + norm_back(grad_normed, normed, inverse, gain_ref[0:1, :])
        ).astype(BF)


def project_back_call(info, dq, dk, dv, low, high, a1, x, dx1, gains, weight):
    rows = x.shape[0]
    row_spec = whole((rows, D))
    rim_spec = whole((2, WINDOW, D))
    grad_shape = jax.ShapeDtypeStruct((3, 2, D, QUAD), BF)
    grad_spec = pl.BlockSpec((1, 1, D, QUAD), lambda c, info: (c // 2, c % 2, 0, 0))
    return pl.pallas_call(
        project_back_kernel,
        grid_spec=pltpu.PrefetchScalarGridSpec(
            num_scalar_prefetch=1,
            grid=(6,),
            in_specs=[
                row_spec,
                row_spec,
                row_spec,
                rim_spec,
                rim_spec,
                row_spec,
                row_spec,
                row_spec,
                whole((2, D)),
                pl.BlockSpec((D, 512), lambda c, info: (0, c)),
            ],
            out_specs=(row_spec, whole((8, D)), grad_spec, grad_spec),
            scratch_shapes=[pltpu.VMEM((rows, 512), BF), pltpu.VMEM((rows, D), F32)],
        ),
        out_shape=(
            jax.ShapeDtypeStruct((rows, D), BF),
            jax.ShapeDtypeStruct((8, D), F32),
            grad_shape,
            grad_shape,
        ),
        compiler_params=params(),
        cost_estimate=cost(4 * rows * D * 3 * D, 22e6),
        name="project_back",
    )(info, dq, dk, dv, low, high, a1, x, dx1, gains, weight)


def place_kernel(count, info_ref, *refs):
    first, second = refs[:count], refs[count : 2 * count]
    expand_ref, shrink_ref = refs[2 * count :]
    slot = info_ref[0]
    for flip in range(count):
        unit = slot ^ flip
        for half, ref in ((0, first[flip]), (1, second[flip])):
            at = unit * PART + half * HALF
            expand_ref[:, pl.ds(pl.multiple_of(at, HALF), HALF)] = ref[:, :HALF].astype(F32)
            expand_ref[:, pl.ds(pl.multiple_of(FF + at, HALF), HALF)] = ref[
                :, HALF : 2 * HALF
            ].astype(F32)
            shrink_ref[pl.ds(pl.multiple_of(at, HALF), HALF), :] = ref[:, 2 * HALF :].astype(F32).T


def place_call(info, first, second):
    rows = first[0].shape[0]
    vmem = pl.BlockSpec(memory_space=pltpu.VMEM)
    return pl.pallas_call(
        functools.partial(place_kernel, len(first)),
        in_specs=[pl.BlockSpec(memory_space=pltpu.SMEM)] + [vmem] * (2 * len(first)),
        out_shape=(
            jax.ShapeDtypeStruct((rows, 2 * FF), F32),
            jax.ShapeDtypeStruct((FF, rows), F32),
        ),
        compiler_params=params(),
        cost_estimate=cost(1e6, 10e6),
        name="place_feed",
    )(info, *first, *second)


def place_attend_kernel(count, info_ref, *refs):
    attend_ref, output_ref = refs[count:]
    slot = info_ref[0]
    for flip in range(count):
        at = (slot ^ flip) * QUAD
        for block in range(4):
            value = refs[flip][block].astype(F32)
            if block < 3:
                attend_ref[:, pl.ds(pl.multiple_of(block * D + at, QUAD), QUAD)] = value
            else:
                output_ref[:, pl.ds(pl.multiple_of(at, QUAD), QUAD)] = value


def place_attend_call(info, pieces):
    rows = pieces[0].shape[1]
    vmem = pl.BlockSpec(memory_space=pltpu.VMEM)
    return pl.pallas_call(
        functools.partial(place_attend_kernel, len(pieces)),
        in_specs=[pl.BlockSpec(memory_space=pltpu.SMEM)] + [vmem] * len(pieces),
        out_shape=(
            jax.ShapeDtypeStruct((rows, 3 * D), F32),
            jax.ShapeDtypeStruct((rows, D), F32),
        ),
        compiler_params=params(),
        cost_estimate=cost(1e6, 4e6),
        name="place_attend",
    )(info, *pieces)


def add_up(terms):
    total = terms[0].astype(F32)
    for term in terms[1:]:
        total = total + term.astype(F32)
    return total


class Links:
    def __init__(self):
        self.dp_size = lax.axis_size("dp")
        self.seq_size = lax.axis_size("seq")
        self.dp = lax.axis_index("dp")
        self.seq = lax.axis_index("seq")
        self.dp_bits = self.dp_size.bit_length() - 1
        self.seq_bits = self.seq_size.bit_length() - 1

    def swap(self, value, axis, bit):
        size = self.dp_size if axis == "dp" else self.seq_size
        return lax.ppermute(value, axis, [(i, i ^ (1 << bit)) for i in range(size)])

    def bit(self, axis, bit):
        return ((self.dp if axis == "dp" else self.seq) >> bit) & 1

    def halve(self, terms, names, name):
        dim = names.index(name)
        mine = self.bit(*name)
        other = add_up(
            [lax.dynamic_index_in_dim(term, 1 - mine, dim, keepdims=False) for term in terms]
        ).astype(BF)
        got = self.swap(other, *name)
        kept = [lax.dynamic_index_in_dim(term, mine, dim, keepdims=False) for term in terms]
        return (kept + [got], names[:dim] + names[dim + 1 :])

    def reduce(self, terms, names, order):
        for name in order:
            terms, names = self.halve(terms, names, name)
        total = add_up(terms)
        for bit in range(2, self.seq_bits):
            total = total + self.swap(total.astype(BF), "seq", bit).astype(F32)
        return total.astype(BF)


def body(
    frames,
    cotangent,
    lengths,
    attend_weight,
    output_weight,
    expand_weight,
    shrink_weight,
    norm_gains,
    norm_biases,
    layer_scales,
):
    rows = frames.shape[1]
    links = Links()
    x = frames.reshape(rows, D)
    dy = cotangent.reshape(rows, D)
    core = links.bit("seq", 0)
    member = links.seq & 3
    slot = links.bit("dp", 0) * 4 + member
    block_rows = D // links.dp_size

    def shifted(value, steps):
        count = links.seq_size
        pairs = [(i, i + steps) for i in range(count) if 0 <= i + steps < count]
        return lax.ppermute(value, "seq", pairs)

    def gathered(value):
        over_x = links.swap(value, "seq", 1)
        over_y = links.swap(value, "dp", 0)
        top = links.swap(over_x[: rows // 2], "dp", 0)
        bottom = links.swap(over_y[rows // 2 :], "seq", 1)
        mine = [value, over_x, over_y, top, bottom]
        return mine + [links.swap(piece, "seq", 0) for piece in mine]

    low_frames = shifted(x[rows - WINDOW :], 1)
    high_frames = shifted(x[:WINDOW], -1)
    dy_pieces = gathered(dy)

    table_info = jnp.stack([links.seq, jnp.int32(links.seq_size * rows)]).astype(jnp.int32)
    cosine, sine, bias = tables_call(table_info, lengths, rows)
    a1, qkv = project_call(x, norm_gains, norm_biases, cosine, sine, attend_weight)
    rim = rim_call(low_frames, high_frames, norm_gains, norm_biases, cosine, sine, attend_weight)
    o, lse, x1, attn, a2 = attend_call(
        qkv, rim, bias, output_weight, x, norm_gains, norm_biases, layer_scales
    )
    a2_pieces = gathered(a2)
    act, dx1, dattn, small_feed = feed_call(
        a2, dy, x1, attn, norm_gains, layer_scales, expand_weight, shrink_weight
    )

    zero = jnp.int32(0)
    info = jnp.stack([zero, zero, core]).astype(jnp.int32)
    dq, dk, dv, low, high, out_send, out_keep = attend_back_call(
        info, qkv, rim, bias, cosine, sine, lse, o, dattn, output_weight
    )
    from_low = shifted(high, 1)
    from_high = shifted(low, -1)
    input_gradient, small_first, qkv_send, qkv_keep = project_back_call(
        info, dq, dk, dv, from_low, from_high, a1, x, dx1, norm_gains, attend_weight
    )

    outer = links.dp_size // 4
    high_bits = [("dp", bit) for bit in range(links.dp_bits - 1, -1, -1)]
    feed_done = []
    for half in range(2):
        slice_info = jnp.stack([slot * 2 + half, links.bit("dp", 1)]).astype(jnp.int32)
        send, keep = slice_call(
            slice_info, a2_pieces, dy_pieces, layer_scales, expand_weight, shrink_weight, rows, outer
        )
        got = links.swap(send, "dp", 1)
        shape = (2,) * (links.dp_bits - 2) + (2, block_rows, 3 * HALF)
        names = [name for name in high_bits if name[1] != 1]
        order = [("dp", bit) for bit in range(2, links.dp_bits)]
        total = links.reduce([keep.reshape(shape), got.reshape(shape)], names, order)
        mine = links.bit("dp", 0)
        pieces = [lax.dynamic_index_in_dim(total, mine, 0, keepdims=False)]
        pieces.append(
            links.swap(lax.dynamic_index_in_dim(total, 1 - mine, 0, keepdims=False), "dp", 0)
        )
        over_x = [links.swap(piece, "seq", 1) for piece in pieces]
        four = pieces + over_x
        over_core = [links.swap(piece, "seq", 0) for piece in four]
        order_of = [0, 4, 2, 6, 1, 5, 3, 7]
        eight = four + over_core
        feed_done.append([eight[order_of.index(flip)] for flip in range(8)])
    slot_info = slot.reshape(1).astype(jnp.int32)
    expand_grad, shrink_grad = place_call(slot_info, feed_done[0], feed_done[1])

    def piece_of(array):
        return array.reshape((2,) + (2,) * links.dp_bits + (block_rows, QUAD))

    names = [("seq", 1)] + high_bits
    over_x = ("seq", 1)
    over_y = ("dp", 0)
    over_z = [("dp", bit) for bit in range(1, links.dp_bits)]
    orders = [
        [over_x, over_y] + over_z,
        [over_y, over_x] + over_z,
        over_z + [over_x, over_y],
        [over_x, over_y] + over_z,
    ]
    qkv_got = links.swap(qkv_send, "seq", 0)
    out_got = links.swap(out_send, "seq", 0)
    done = []
    for block in range(4):
        if block < 3:
            terms = [piece_of(qkv_keep[block]), piece_of(qkv_got[block])]
        else:
            terms = [piece_of(out_keep), piece_of(out_got)]
        done.append(links.reduce(terms, names, orders[block]))
    stack = jnp.stack(done)
    across = links.swap(stack, "seq", 1)
    four = [stack, None, across, None]
    four[1] = links.swap(stack, "seq", 0)
    four[3] = links.swap(across, "seq", 0)
    attend_grad, output_grad = place_attend_call(member.reshape(1).astype(jnp.int32), four)

    small = jnp.concatenate([small_feed[:4], small_first[:2], jnp.zeros((2, D), F32)], axis=0)
    for axis, count in (("seq", links.seq_bits), ("dp", links.dp_bits)):
        for bit in range(count):
            small = small + links.swap(small, axis, bit)
    small = lax.dynamic_slice_in_dim(small, links.dp * block_rows, block_rows, axis=1)
    gains_grad = jnp.stack([small[4], small[1]])
    biases_grad = jnp.stack([small[5], small[2]])
    scales_grad = jnp.stack([small[3], small[0]])
    return (
        act.reshape(frames.shape),
        input_gradient.reshape(frames.shape),
        attend_grad,
        output_grad,
        expand_grad,
        shrink_grad,
        gains_grad,
        biases_grad,
        scales_grad,
    )


def solution(mesh):
    in_specs = (
        P("dp", "seq", None),
        P("dp", "seq", None),
        P("dp", None),
        P(),
        P(),
        P(),
        P(),
        P(),
        P(),
        P(),
    )
    out_specs = (
        P("dp", "seq", None),
        P("dp", "seq", None),
        P("dp", None),
        P("dp", None),
        P("dp", None),
        P(None, "dp"),
        P(None, "dp"),
        P(None, "dp"),
        P(None, "dp"),
    )
    return jax.shard_map(body, mesh=mesh, in_specs=in_specs, out_specs=out_specs, check_vma=False)
```

```python
import functools
import math

import jax
import jax.numpy as jnp
from jax import lax
from jax.experimental import pallas as pl
from jax.experimental.pallas import tpu as pltpu
from jax.sharding import PartitionSpec as P

D = 1024
HEADS = 16
HEAD_DIM = 64
FF = 4096
WINDOW = 128
QUAD = 4 * HEAD_DIM
SLICES = 8
PART = FF // SLICES
HALF = PART // 2
EPS = 1e-05
BF = jnp.bfloat16
F32 = jnp.float32
VMEM_BYTES = 58 * 1024 * 1024


def dot_nn(a, b):
    return lax.dot_general(a, b, (((1,), (0,)), ((), ())), preferred_element_type=F32)


def dot_nt(a, b):
    return lax.dot_general(a, b, (((1,), (1,)), ((), ())), preferred_element_type=F32)


def dot_tn(a, b):
    return lax.dot_general(a, b, (((0,), (0,)), ((), ())), preferred_element_type=F32)


def params(**extra):
    return pltpu.CompilerParams(vmem_limit_bytes=VMEM_BYTES, **extra)


def cost(flops, size, transcendentals=0):
    return pl.CostEstimate(
        flops=int(flops), bytes_accessed=int(size), transcendentals=int(transcendentals)
    )


def whole(shape):
    return pl.BlockSpec(shape, lambda *_: (0,) * len(shape))


def norm_stats(values):
    centered = values - jnp.mean(values, axis=-1, keepdims=True)
    inverse = lax.rsqrt(jnp.mean(centered * centered, axis=-1, keepdims=True) + EPS)
    return (centered * inverse, inverse)


def norm_back(gradient, normed, inverse, gain_row):
    scaled = gradient * gain_row
    return inverse * (
        scaled
        - jnp.mean(scaled, axis=-1, keepdims=True)
        - normed * jnp.mean(scaled * normed, axis=-1, keepdims=True)
    )


def turn(values, cosine, sine, sign):
    lane = lax.broadcasted_iota(jnp.int32, (values.shape[0], 128), 1) % HEAD_DIM
    parts = []
    for group in range(values.shape[1] // 128):
        part = values[:, group * 128 : group * 128 + 128]
        swapped = jnp.where(
            lane < HEAD_DIM // 2, pltpu.roll(part, 96, 1), pltpu.roll(part, 32, 1)
        )
        if sign > 0:
            parts.append(part * cosine + swapped * sine)
        else:
            parts.append(part * cosine - swapped * sine)
    return jnp.concatenate(parts, axis=1)


def tables_kernel(info_ref, lengths_ref, cos_ref, sin_ref, bias_ref):
    wide = cos_ref.shape[0]
    rows = wide - 2 * WINDOW
    base = info_ref[0] * rows
    total = info_ref[1]
    frame = base - WINDOW + lax.broadcasted_iota(jnp.int32, (wide, 128), 0)
    query = base + lax.broadcasted_iota(jnp.int32, (8, rows), 1)
    key_clip = jnp.full((wide, 128), -1, jnp.int32)
    begin = jnp.zeros((wide, 128), jnp.int32)
    query_clip = jnp.full((8, rows), -1, jnp.int32)

    def step(entry, carry):
        start, key_clip, begin, query_clip = carry
        inside = frame >= start
        key_clip = key_clip + inside.astype(jnp.int32)
        begin = jnp.where(inside, start, begin)
        query_clip = query_clip + (query >= start).astype(jnp.int32)
        return (start + lengths_ref[0, entry], key_clip, begin, query_clip)

    _, key_clip, begin, query_clip = lax.fori_loop(
        0, lengths_ref.shape[1], step, (jnp.int32(0), key_clip, begin, query_clip)
    )
    key_clip = jnp.where((frame >= 0) & (frame < total), key_clip, -1)
    lane = lax.broadcasted_iota(jnp.int32, (wide, 128), 1)
    frequency = jnp.exp(
        (lane % (HEAD_DIM // 2)).astype(F32) * (-2.0 * math.log(10000.0) / HEAD_DIM)
    )
    angle = (frame - begin).astype(F32) * frequency
    sine = jnp.sin(angle)
    cos_ref[...] = jnp.cos(angle)
    sin_ref[...] = jnp.where(lane % HEAD_DIM < HEAD_DIM // 2, -sine, sine)
    span = 3 * WINDOW
    gap = lax.broadcasted_iota(jnp.int32, (span, 128), 0) - lax.broadcasted_iota(
        jnp.int32, (span, 128), 1
    )
    near = (gap >= 0) & (gap <= 2 * WINDOW)
    for block in range(rows // WINDOW):
        at = block * WINDOW
        same = key_clip[at : at + span] == query_clip[0:1, at : at + WINDOW]
        bias_ref[block] = jnp.where(near & same, 0.0, -1e30)


def tables_call(info, lengths, rows):
    wide = rows + 2 * WINDOW
    return pl.pallas_call(
        tables_kernel,
        out_shape=(
            jax.ShapeDtypeStruct((wide, 128), F32),
            jax.ShapeDtypeStruct((wide, 128), F32),
            jax.ShapeDtypeStruct((rows // WINDOW, 3 * WINDOW, 128), F32),
        ),
        in_specs=[
            pl.BlockSpec(memory_space=pltpu.SMEM),
            pl.BlockSpec(memory_space=pltpu.SMEM),
        ],
        compiler_params=params(),
        cost_estimate=cost(1e8, 2e6),
        name="tables",
    )(info, lengths)


def project_kernel(x_ref, gain_ref, shift_ref, cos_ref, sin_ref, weight_ref, a1_ref, out_ref):
    chunk = pl.program_id(0)
    rows = x_ref.shape[0]

    @pl.when(chunk == 0)
    def _():
        normed, _unused = norm_stats(x_ref[...].astype(F32))
        a1_ref[...] = (normed * gain_ref[0:1, :] + shift_ref[0:1, :]).astype(BF)

    projected = dot_nn(a1_ref[...], weight_ref[...])
    cosine = cos_ref[WINDOW : WINDOW + rows, :]
    sine = sin_ref[WINDOW : WINDOW + rows, :]

    @pl.when(chunk < 2)
    def _():
        out_ref[...] = (turn(projected, cosine, sine, 1) * HEAD_DIM**-0.5).astype(BF)

    @pl.when((chunk >= 2) & (chunk < 4))
    def _():
        out_ref[...] = turn(projected, cosine, sine, 1).astype(BF)

    @pl.when(chunk >= 4)
    def _():
        out_ref[...] = projected.astype(BF)


def project_call(x, gains, shifts, cosine, sine, weight):
    rows = x.shape[0]
    wide = cosine.shape[0]
    return pl.pallas_call(
        project_kernel,
        grid=(6,),
        out_shape=(
            jax.ShapeDtypeStruct((rows, D), BF),
            jax.ShapeDtypeStruct((rows, 3 * D), BF),
        ),
        in_specs=[
            whole((rows, D)),
            whole((2, D)),
            whole((2, D)),
            whole((wide, 128)),
            whole((wide, 128)),
            pl.BlockSpec((D, 512), lambda c: (0, c)),
        ],
        out_specs=(whole((rows, D)), pl.BlockSpec((rows, 512), lambda c: (0, c))),
        compiler_params=params(),
        cost_estimate=cost(2 * rows * D * 3 * D, 12e6),
        name="project",
    )(x, gains, shifts, cosine, sine, weight)


def rim_kernel(
    low_ref, high_ref, gain_ref, shift_ref, cos_ref, sin_ref, weight_ref, out_ref, a1_ref
):
    chunk = pl.program_id(0)
    wide = cos_ref.shape[0]

    @pl.when(chunk == 0)
    def _():
        for at, ref in ((0, low_ref), (WINDOW, high_ref)):
            normed, _unused = norm_stats(ref[...].astype(F32))
            a1_ref[at : at + WINDOW, :] = (
                normed * gain_ref[0:1, :] + shift_ref[0:1, :]
            ).astype(BF)

    projected = dot_nn(a1_ref[...], weight_ref[...])

    @pl.when(chunk < 2)
    def _():
        cosine = jnp.concatenate([cos_ref[:WINDOW, :], cos_ref[wide - WINDOW :, :]], axis=0)
        sine = jnp.concatenate([sin_ref[:WINDOW, :], sin_ref[wide - WINDOW :, :]], axis=0)
        out_ref[...] = turn(projected, cosine, sine, 1).astype(BF)

    @pl.when(chunk >= 2)
    def _():
        out_ref[...] = projected.astype(BF)


def rim_call(low, high, gains, shifts, cosine, sine, weight):
    wide = cosine.shape[0]
    return pl.pallas_call(
        rim_kernel,
        grid=(4,),
        out_shape=jax.ShapeDtypeStruct((2 * WINDOW, 2 * D), BF),
        in_specs=[
            whole((WINDOW, D)),
            whole((WINDOW, D)),
            whole((2, D)),
            whole((2, D)),
            whole((wide, 128)),
            whole((wide, 128)),
            pl.BlockSpec((D, 512), lambda c: (0, c + 2)),
        ],
        out_specs=pl.BlockSpec((2 * WINDOW, 512), lambda c: (0, c)),
        scratch_shapes=[pltpu.VMEM((2 * WINDOW, D), BF)],
        compiler_params=params(),
        cost_estimate=cost(2 * 256 * D * 2 * D, 6e6),
        name="rim",
    )(low, high, gains, shifts, cosine, sine, weight)


def stacked(block):
    owner = lax.broadcasted_iota(jnp.int32, block.shape, 1) // HEAD_DIM
    zero = jnp.zeros_like(block)
    return jnp.concatenate([jnp.where(owner == head, block, zero) for head in range(4)], axis=0)


def attend_kernel(
    q_ref,
    k_ref,
    v_ref,
    rim_k_ref,
    rim_v_ref,
    bias_ref,
    weight_ref,
    x_ref,
    gain_ref,
    shift_ref,
    scale_ref,
    o_ref,
    lse_ref,
    x1_ref,
    attn_ref,
    a2_ref,
    keys,
    values_t,
    mixed_t,
    total,
):
    quad = pl.program_id(0)
    rows = q_ref.shape[0]
    keys[0:WINDOW, :] = rim_k_ref[0:WINDOW, :]
    keys[WINDOW : WINDOW + rows, :] = k_ref[...]
    keys[WINDOW + rows :, :] = rim_k_ref[WINDOW:, :]
    values_t[:, 0:WINDOW] = rim_v_ref[0:WINDOW, :].T
    values_t[:, WINDOW : WINDOW + rows] = v_ref[...].T
    values_t[:, WINDOW + rows :] = rim_v_ref[WINDOW:, :].T
    for block in range(rows // WINDOW):
        at = block * WINDOW
        queries = stacked(q_ref[at : at + WINDOW, :])
        scores = dot_nt(keys[at : at + 3 * WINDOW, :], queries)
        bias = bias_ref[block]
        scores = scores + jnp.concatenate([bias] * 4, axis=1)
        top = jnp.max(scores, axis=0, keepdims=True)
        weights = jnp.exp(scores - top)
        total_row = jnp.sum(weights, axis=0, keepdims=True)
        weights = (weights * (1.0 / total_row)).astype(BF)
        log_row = top + jnp.log(total_row)
        for head in range(4):
            lanes = slice(head * WINDOW, head * WINDOW + WINDOW)
            lse_ref[0, head : head + 1, at : at + WINDOW] = log_row[:, lanes]
            feature = slice(head * HEAD_DIM, head * HEAD_DIM + HEAD_DIM)
            mixed_t[feature, at : at + WINDOW] = dot_nn(
                values_t[feature, at : at + 3 * WINDOW], weights[:, lanes]
            )
    mixed = mixed_t[...].T.astype(BF)
    o_ref[...] = mixed
    branch = dot_nn(mixed, weight_ref[...])

    @pl.when(quad == 0)
    def _():
        total[...] = branch

    @pl.when(quad > 0)
    def _():
        total[...] += branch

    @pl.when(quad == HEADS // 4 - 1)
    def _():
        attn = total[...]
        residual = x_ref[...].astype(F32) + attn * scale_ref[0:1, :]
        normed, _unused = norm_stats(residual)
        x1_ref[...] = residual
        attn_ref[...] = attn.astype(BF)
        a2_ref[...] = (normed * gain_ref[1:2, :] + shift_ref[1:2, :]).astype(BF)


def attend_call(qkv, rim, bias, weight, x, gains, shifts, scales):
    rows = x.shape[0]
    wide = rows + 2 * WINDOW
    row_spec = whole((rows, D))
    return pl.pallas_call(
        attend_kernel,
        grid=(HEADS // 4,),
        out_shape=(
            jax.ShapeDtypeStruct((rows, D), BF),
            jax.ShapeDtypeStruct((HEADS // 4, 8, rows), F32),
            jax.ShapeDtypeStruct((rows, D), F32),
            jax.ShapeDtypeStruct((rows, D), BF),
            jax.ShapeDtypeStruct((rows, D), BF),
        ),
        in_specs=[
            pl.BlockSpec((rows, QUAD), lambda h: (0, h)),
            pl.BlockSpec((rows, QUAD), lambda h: (0, h + 4)),
            pl.BlockSpec((rows, QUAD), lambda h: (0, h + 8)),
            pl.BlockSpec((2 * WINDOW, QUAD), lambda h: (0, h)),
            pl.BlockSpec((2 * WINDOW, QUAD), lambda h: (0, h + 4)),
            whole(bias.shape),
            pl.BlockSpec((QUAD, D), lambda h: (h, 0)),
            row_spec,
            whole((2, D)),
            whole((2, D)),
            whole((2, D)),
        ],
        out_specs=(
            pl.BlockSpec((rows, QUAD), lambda h: (0, h)),
            pl.BlockSpec((1, 8, rows), lambda h: (h, 0, 0)),
            row_spec,
            row_spec,
            row_spec,
        ),
        scratch_shapes=[
            pltpu.VMEM((wide, QUAD), BF),
            pltpu.VMEM((QUAD, wide), BF),
            pltpu.VMEM((QUAD, rows), F32),
            pltpu.VMEM((rows, D), F32),
        ],
        compiler_params=params(),
        cost_estimate=cost(8e9, 14e6, 3e6),
        name="attend",
    )(qkv, qkv, qkv, rim, rim, bias, weight, x, gains, shifts, scales)


def gated(gate, up, grad_hidden):
    sigmoid = 0.5 * jnp.tanh(0.5 * gate) + 0.5
    swish = gate * sigmoid
    hidden = swish * up
    grad_gate = grad_hidden * up * (sigmoid + swish * (1.0 - sigmoid))
    grad_up = grad_hidden * swish
    return (hidden.astype(BF), grad_gate.astype(BF), grad_up.astype(BF))


def feed_kernel(
    a2_ref,
    dy_ref,
    x1_ref,
    attn_ref,
    gain_ref,
    scale_ref,
    gate_w_ref,
    up_w_ref,
    shrink_w_ref,
    act_ref,
    dx1_ref,
    dattn_ref,
    small_ref,
    branch_grad,
    mlp,
    back,
):
    chunk = pl.program_id(0)

    @pl.when(chunk == 0)
    def _():
        branch_grad[...] = (dy_ref[...].astype(F32) * scale_ref[1:2, :]).astype(BF)

    a2 = a2_ref[...]
    gate = dot_nn(a2, gate_w_ref[...])
    up = dot_nn(a2, up_w_ref[...])
    grad_hidden = dot_nt(branch_grad[...], shrink_w_ref[...])
    hidden, grad_gate, grad_up = gated(gate, up, grad_hidden)
    branch = dot_nn(hidden, shrink_w_ref[...])
    back_part = dot_nt(grad_gate, gate_w_ref[...]) + dot_nt(grad_up, up_w_ref[...])

    @pl.when(chunk == 0)
    def _():
        mlp[...] = branch
        back[...] = back_part

    @pl.when(chunk > 0)
    def _():
        mlp[...] += branch
        back[...] += back_part

    @pl.when(chunk == pl.num_programs(0) - 1)
    def _():
        residual = x1_ref[...]
        grad_result = dy_ref[...].astype(F32)
        branch = mlp[...]
        act_ref[...] = (residual + branch * scale_ref[1:2, :]).astype(BF)
        small_ref[0:1, :] = jnp.sum(grad_result * branch, axis=0, keepdims=True)
        grad_normed = back[...]
        normed, inverse = norm_stats(residual)
        small_ref[1:2, :] = jnp.sum(grad_normed * normed, axis=0, keepdims=True)
        small_ref[2:3, :] = jnp.sum(grad_normed, axis=0, keepdims=True)
        grad_residual = grad_result + norm_back(grad_normed, normed, inverse, gain_ref[1:2, :])
        dx1_ref[...] = grad_residual
        small_ref[3:4, :] = jnp.sum(
            grad_residual * attn_ref[...].astype(F32), axis=0, keepdims=True
        )
        small_ref[4:8, :] = jnp.zeros((4, D), F32)
        dattn_ref[...] = (grad_residual * scale_ref[0:1, :]).astype(BF)


def feed_call(a2, dy, x1, attn, gains, scales, expand, shrink):
    rows = a2.shape[0]
    size = 512
    count = FF // size
    row_spec = whole((rows, D))
    return pl.pallas_call(
        feed_kernel,
        grid=(count,),
        out_shape=(
            jax.ShapeDtypeStruct((rows, D), BF),
            jax.ShapeDtypeStruct((rows, D), F32),
            jax.ShapeDtypeStruct((rows, D), BF),
            jax.ShapeDtypeStruct((8, D), F32),
        ),
        in_specs=[
            row_spec,
            row_spec,
            row_spec,
            row_spec,
            whole((2, D)),
            whole((2, D)),
            pl.BlockSpec((D, size), lambda f: (0, f)),
            pl.BlockSpec((D, size), lambda f: (0, f + count)),
            pl.BlockSpec((size, D), lambda f: (f, 0)),
        ],
        out_specs=(row_spec, row_spec, row_spec, whole((8, D))),
        scratch_shapes=[
            pltpu.VMEM((rows, D), BF),
            pltpu.VMEM((rows, D), F32),
            pltpu.VMEM((rows, D), F32),
        ],
        compiler_params=params(),
        cost_estimate=cost(2 * rows * D * FF * 6, 36e6, rows * FF),
        name="feed",
    )(a2, dy, x1, attn, gains, scales, expand, expand, shrink)


def slice_kernel(pieces, outer, info_ref, *refs):
    a2_refs = refs[: len(pieces)]
    dy_refs = refs[len(pieces) : 2 * len(pieces)]
    scale_ref, gate_w_ref, up_w_ref, shrink_w_ref = refs[2 * len(pieces) : 2 * len(pieces) + 4]
    send_ref, keep_ref, a2_all, dm_all, inner, pair_w, result, sems = refs[
        2 * len(pieces) + 4 :
    ]
    size = gate_w_ref.shape[1]
    groups = 1 + max(slot for slot, _, _ in pieces)
    rows = a2_all.shape[0] // groups
    copies = [[] for _ in range(groups)]
    for number, (slot, first, count) in enumerate(pieces):
        for kind, (sources, held) in enumerate(((a2_refs, a2_all), (dy_refs, dm_all))):
            copies[slot].append(
                pltpu.make_async_copy(
                    sources[number],
                    held.at[pl.ds(slot * rows + first, count), :],
                    sems.at[kind, number],
                )
            )
    for slot in range(min(2, groups)):
        for copy in copies[slot]:
            copy.start()
    pair_w[:, :size] = gate_w_ref[...]
    pair_w[:, size:] = up_w_ref[...]
    scale = scale_ref[1:2, :]
    for slot in range(groups):
        if slot + 2 < groups:
            for copy in copies[slot + 2]:
                copy.start()
        for copy in copies[slot]:
            copy.wait()
        span = slice(slot * rows, slot * rows + rows)
        branch_grad = (dm_all[span, :].astype(F32) * scale).astype(BF)
        dm_all[span, :] = branch_grad
        pair = dot_nn(a2_all[span, :], pair_w[...])
        grad_hidden = dot_nt(branch_grad, shrink_w_ref[...])
        hidden, grad_gate, grad_up = gated(pair[:, :size], pair[:, size:], grad_hidden)
        inner[span, :size] = grad_gate
        inner[span, size : 2 * size] = grad_up
        inner[span, 2 * size :] = hidden
    result[:, : 2 * size] = dot_tn(a2_all[...], inner[:, : 2 * size]).astype(BF)
    result[:, 2 * size :] = dot_tn(dm_all[...], inner[:, 2 * size :]).astype(BF)
    mine = info_ref[1]
    span = D // (2 * outer)
    for at in range(outer):
        for target, bit in ((send_ref, 1 - mine), (keep_ref, mine)):
            first = pl.multiple_of(at * 2 * span + bit * span, span)
            target[at] = result[pl.ds(first, span), :]


def slice_call(info, size, a2_list, dy_list, scales, expand, shrink, rows, outer):
    pieces = []
    slot, first = 0, 0
    for piece in a2_list:
        pieces.append((slot, first, piece.shape[0]))
        first += piece.shape[0]
        if first == rows:
            slot, first = slot + 1, 0
    groups = slot
    span = D // (2 * outer)
    hbm = pl.BlockSpec(memory_space=pl.ANY)
    result = jax.ShapeDtypeStruct((outer, span, 3 * size), BF)
    out_spec = pl.BlockSpec((outer, span, 3 * size), lambda i, info: (0, 0, 0))
    return pl.pallas_call(
        functools.partial(slice_kernel, tuple(pieces), outer),
        grid_spec=pltpu.PrefetchScalarGridSpec(
            num_scalar_prefetch=1,
            grid=(1,),
            in_specs=[hbm] * (2 * len(pieces))
            + [
                pl.BlockSpec((2, D), lambda i, info: (0, 0)),
                pl.BlockSpec((D, size), lambda i, info: (0, info[0])),
                pl.BlockSpec((D, size), lambda i, info: (0, info[0] + FF // size)),
                pl.BlockSpec((size, D), lambda i, info: (info[0], 0)),
            ],
            out_specs=(out_spec, out_spec),
            scratch_shapes=[
                pltpu.VMEM((groups * rows, D), BF),
                pltpu.VMEM((groups * rows, D), BF),
                pltpu.VMEM((groups * rows, 3 * size), BF),
                pltpu.VMEM((D, 2 * size), BF),
                pltpu.VMEM((D, 3 * size), BF),
                pltpu.SemaphoreType.DMA((2, len(pieces))),
            ],
        ),
        out_shape=(result, result),
        compiler_params=params(),
        cost_estimate=cost(2 * groups * rows * D * size * 6, 22e6, groups * rows * size),
        name="slice_grads",
    )(info, *a2_list, *dy_list, scales, expand, expand, shrink)


def attend_back_kernel(
    q_ref,
    k_ref,
    v_ref,
    rim_k_ref,
    rim_v_ref,
    bias_ref,
    cos_ref,
    sin_ref,
    lse_ref,
    dattn_ref,
    weight_ref,
    dq_ref,
    dk_ref,
    dv_ref,
    low_ref,
    high_ref,
    keys,
    values,
    keys_t,
    grad_q_t,
    grad_k,
    grad_v,
):
    rows = q_ref.shape[0]
    for held, own, rim in ((keys, k_ref, rim_k_ref), (values, v_ref, rim_v_ref)):
        held[0:WINDOW, :] = rim[0:WINDOW, :]
        held[WINDOW : WINDOW + rows, :] = own[...]
        held[WINDOW + rows :, :] = rim[WINDOW:, :]
    keys_t[...] = keys[...].T
    dattn = dattn_ref[...]
    grad_mixed = dot_nt(dattn, weight_ref[...]).astype(BF)
    grad_k[...] = jnp.zeros_like(grad_k)
    grad_v[...] = jnp.zeros_like(grad_v)
    for block in range(rows // WINDOW):
        at = block * WINDOW
        span = slice(at, at + 3 * WINDOW)
        queries = stacked(q_ref[at : at + WINDOW, :])
        grad_out = stacked(grad_mixed[at : at + WINDOW, :])
        scores = dot_nt(keys[span, :], queries)
        log_row = jnp.concatenate(
            [lse_ref[0, head : head + 1, at : at + WINDOW] for head in range(4)], axis=1
        )
        bias = bias_ref[block]
        weights = jnp.exp(scores + jnp.concatenate([bias] * 4, axis=1) - log_row)
        grad_weights = dot_nt(values[span, :], grad_out)
        weighted = weights * grad_weights
        grad_scores = weighted - weights * jnp.sum(weighted, axis=0, keepdims=True)
        grad_scores = grad_scores.astype(BF)
        grad_v[span, :] += dot_nn(weights.astype(BF), grad_out)
        grad_k[span, :] += dot_nn(grad_scores, queries)
        for head in range(4):
            feature = slice(head * HEAD_DIM, head * HEAD_DIM + HEAD_DIM)
            grad_q_t[feature, at : at + WINDOW] = dot_nn(
                keys_t[feature, span], grad_scores[:, head * WINDOW : head * WINDOW + WINDOW]
            )
    own = slice(WINDOW, WINDOW + rows)
    cosine, sine = cos_ref[...], sin_ref[...]
    dq_ref[...] = turn(
        grad_q_t[...].T * HEAD_DIM**-0.5, cosine[own, :], sine[own, :], -1
    ).astype(BF)
    turned = turn(grad_k[...], cosine, sine, -1).astype(BF)
    grad_values = grad_v[...].astype(BF)
    dk_ref[...] = turned[own, :]
    dv_ref[...] = grad_values[own, :]
    low_ref[0] = turned[:WINDOW, :]
    low_ref[1] = grad_values[:WINDOW, :]
    high_ref[0] = turned[WINDOW + rows :, :]
    high_ref[1] = grad_values[WINDOW + rows :, :]


def attend_back_call(qkv, rim, bias, cosine, sine, lse, dattn, weight):
    rows = dattn.shape[0]
    wide = rows + 2 * WINDOW
    row_shape = jax.ShapeDtypeStruct((rows, D), BF)
    rim_shape = jax.ShapeDtypeStruct((2, WINDOW, D), BF)
    row_spec = pl.BlockSpec((rows, QUAD), lambda h: (0, h))
    rim_spec = pl.BlockSpec((2, WINDOW, QUAD), lambda h: (0, 0, h))
    return pl.pallas_call(
        attend_back_kernel,
        grid=(HEADS // 4,),
        in_specs=[
            row_spec,
            pl.BlockSpec((rows, QUAD), lambda h: (0, h + 4)),
            pl.BlockSpec((rows, QUAD), lambda h: (0, h + 8)),
            pl.BlockSpec((2 * WINDOW, QUAD), lambda h: (0, h)),
            pl.BlockSpec((2 * WINDOW, QUAD), lambda h: (0, h + 4)),
            whole(bias.shape),
            whole((wide, 128)),
            whole((wide, 128)),
            pl.BlockSpec((1, 8, rows), lambda h: (h, 0, 0)),
            whole((rows, D)),
            pl.BlockSpec((QUAD, D), lambda h: (h, 0)),
        ],
        out_specs=(row_spec, row_spec, row_spec, rim_spec, rim_spec),
        scratch_shapes=[
            pltpu.VMEM((wide, QUAD), BF),
            pltpu.VMEM((wide, QUAD), BF),
            pltpu.VMEM((QUAD, wide), BF),
            pltpu.VMEM((QUAD, rows), F32),
            pltpu.VMEM((wide, QUAD), F32),
            pltpu.VMEM((wide, QUAD), F32),
        ],
        out_shape=(row_shape, row_shape, row_shape, rim_shape, rim_shape),
        compiler_params=params(),
        cost_estimate=cost(2e10, 20e6, 3e6),
        name="attend_back",
    )(qkv, qkv, qkv, rim, rim, bias, cosine, sine, lse, dattn, weight)


def own_and_rims(target, ref, low_ref, high_ref, kind, lanes):
    rows = ref.shape[0]
    target[WINDOW : rows - WINDOW, :] = ref[WINDOW : rows - WINDOW, lanes]
    for at, rim in ((0, low_ref), (rows - WINDOW, high_ref)):
        target[at : at + WINDOW, :] = (
            ref[at : at + WINDOW, lanes].astype(F32) + rim[kind, :, lanes].astype(F32)
        ).astype(BF)


def split_by_core(info_ref, outer, keep_ref, send_ref):
    for core in range(2):

        @pl.when(info_ref[2] == core)
        def _():
            keep_ref[0, 0] = outer[:, core * QUAD : core * QUAD + QUAD]
            send_ref[0, 0] = outer[:, (1 - core) * QUAD : (1 - core) * QUAD + QUAD]


def weight_qo_kernel(info_ref, dq_ref, a1_ref, dattn_ref, o_ref, send_ref, keep_ref):
    for kind, (left, right) in enumerate(((a1_ref, dq_ref), (o_ref, dattn_ref))):

        @pl.when(pl.program_id(0) // 2 == kind)
        def _():
            outer = dot_tn(left[...], right[...]).astype(BF)
            split_by_core(info_ref, outer, keep_ref, send_ref)


def weight_qo_call(info, dq, a1, dattn, o):
    rows = a1.shape[0]
    grad_shape = jax.ShapeDtypeStruct((2, 2, D, QUAD), BF)
    grad_spec = pl.BlockSpec((1, 1, D, QUAD), lambda c, info: (c // 2, c % 2, 0, 0))
    return pl.pallas_call(
        weight_qo_kernel,
        grid_spec=pltpu.PrefetchScalarGridSpec(
            num_scalar_prefetch=1,
            grid=(4,),
            in_specs=[
                pl.BlockSpec((rows, 512), lambda c, info: (0, jnp.minimum(c, 1))),
                whole((rows, D)),
                pl.BlockSpec((rows, 512), lambda c, info: (0, jnp.maximum(c - 2, 0))),
                whole((rows, D)),
            ],
            out_specs=(grad_spec, grad_spec),
        ),
        out_shape=(grad_shape, grad_shape),
        compiler_params=params(),
        cost_estimate=cost(4 * rows * D * D, 8e6),
        name="weight_qo",
    )(info, dq, a1, dattn, o)


def weight_kv_kernel(
    info_ref, dk_ref, dv_ref, low_ref, high_ref, a1_ref, send_ref, keep_ref, part
):
    chunk = pl.program_id(0)
    lanes = pl.ds(pl.multiple_of((chunk % 2) * 512, 512), 512)
    for kind, ref in ((0, dk_ref), (1, dv_ref)):

        @pl.when(chunk // 2 == kind)
        def _():
            own_and_rims(part, ref, low_ref, high_ref, kind, lanes)

    outer = dot_tn(a1_ref[...], part[...]).astype(BF)
    split_by_core(info_ref, outer, keep_ref, send_ref)


def weight_kv_call(info, dk, dv, low, high, a1):
    rows = a1.shape[0]
    row_spec = whole((rows, D))
    rim_spec = whole((2, WINDOW, D))
    grad_shape = jax.ShapeDtypeStruct((2, 2, D, QUAD), BF)
    grad_spec = pl.BlockSpec((1, 1, D, QUAD), lambda c, info: (c // 2, c % 2, 0, 0))
    return pl.pallas_call(
        weight_kv_kernel,
        grid_spec=pltpu.PrefetchScalarGridSpec(
            num_scalar_prefetch=1,
            grid=(4,),
            in_specs=[row_spec, row_spec, rim_spec, rim_spec, row_spec],
            out_specs=(grad_spec, grad_spec),
            scratch_shapes=[pltpu.VMEM((rows, 512), BF)],
        ),
        out_shape=(grad_shape, grad_shape),
        compiler_params=params(),
        cost_estimate=cost(4 * rows * D * D, 8e6),
        name="weight_kv",
    )(info, dk, dv, low, high, a1)


def input_back_kernel(
    dq_ref,
    dk_ref,
    dv_ref,
    low_ref,
    high_ref,
    x_ref,
    dx1_ref,
    gain_ref,
    weight_ref,
    grad_ref,
    small_ref,
    part,
    back,
):
    chunk = pl.program_id(0)
    lanes = pl.ds(pl.multiple_of((chunk % 2) * 512, 512), 512)

    @pl.when(chunk < 2)
    def _():
        part[...] = dq_ref[:, lanes]

    for kind, ref in ((0, dk_ref), (1, dv_ref)):

        @pl.when(chunk // 2 == kind + 1)
        def _():
            own_and_rims(part, ref, low_ref, high_ref, kind, lanes)

    back_part = dot_nt(part[...], weight_ref[...])

    @pl.when(chunk == 0)
    def _():
        back[...] = back_part

    @pl.when(chunk > 0)
    def _():
        back[...] += back_part

    @pl.when(chunk == pl.num_programs(0) - 1)
    def _():
        grad_normed = back[...]
        normed, inverse = norm_stats(x_ref[...].astype(F32))
        small_ref[0:1, :] = jnp.sum(grad_normed * normed, axis=0, keepdims=True)
        small_ref[1:2, :] = jnp.sum(grad_normed, axis=0, keepdims=True)
        small_ref[2:8, :] = jnp.zeros((6, D), F32)
        grad_ref[...] = (
            dx1_ref[...] + norm_back(grad_normed, normed, inverse, gain_ref[0:1, :])
        ).astype(BF)


def input_back_call(dq, dk, dv, low, high, x, dx1, gains, weight):
    rows = x.shape[0]
    row_spec = whole((rows, D))
    rim_spec = whole((2, WINDOW, D))
    return pl.pallas_call(
        input_back_kernel,
        grid=(6,),
        in_specs=[
            row_spec,
            row_spec,
            row_spec,
            rim_spec,
            rim_spec,
            row_spec,
            row_spec,
            whole((2, D)),
            pl.BlockSpec((D, 512), lambda c: (0, c)),
        ],
        out_specs=(row_spec, whole((8, D))),
        scratch_shapes=[pltpu.VMEM((rows, 512), BF), pltpu.VMEM((rows, D), F32)],
        out_shape=(
            jax.ShapeDtypeStruct((rows, D), BF),
            jax.ShapeDtypeStruct((8, D), F32),
        ),
        compiler_params=params(),
        cost_estimate=cost(2 * rows * D * 3 * D, 14e6),
        name="input_back",
    )(dq, dk, dv, low, high, x, dx1, gains, weight)


def place_kernel(starts, count, info_ref, *refs):
    expand_ref, shrink_ref = refs[-2:]
    slot = info_ref[0]
    for number, start in enumerate(starts):
        for flip in range(count):
            ref = refs[number * count + flip]
            size = ref.shape[1] // 3
            at = (slot ^ flip) * PART + start
            expand_ref[:, pl.ds(pl.multiple_of(at, 128), size)] = ref[:, :size].astype(F32)
            expand_ref[:, pl.ds(pl.multiple_of(FF + at, 128), size)] = ref[
                :, size : 2 * size
            ].astype(F32)
            shrink_ref[pl.ds(pl.multiple_of(at, 128), size), :] = ref[:, 2 * size :].astype(F32).T


def place_call(info, starts, pieces):
    rows = pieces[0][0].shape[0]
    vmem = pl.BlockSpec(memory_space=pltpu.VMEM)
    flat = [piece for chunk in pieces for piece in chunk]
    return pl.pallas_call(
        functools.partial(place_kernel, starts, len(pieces[0])),
        in_specs=[pl.BlockSpec(memory_space=pltpu.SMEM)] + [vmem] * len(flat),
        out_shape=(
            jax.ShapeDtypeStruct((rows, 2 * FF), F32),
            jax.ShapeDtypeStruct((FF, rows), F32),
        ),
        compiler_params=params(),
        cost_estimate=cost(1e6, 10e6),
        name="place_feed",
    )(info, *flat)


def place_attend_kernel(count, info_ref, *refs):
    attend_ref, output_ref = refs[count:]
    slot = info_ref[0]
    for flip in range(count):
        at = (slot ^ flip) * QUAD
        for block in range(4):
            value = refs[flip][block].astype(F32)
            if block == 1:
                output_ref[:, pl.ds(pl.multiple_of(at, QUAD), QUAD)] = value
            else:
                column = max(block - 1, 0) * D + at
                attend_ref[:, pl.ds(pl.multiple_of(column, QUAD), QUAD)] = value


def place_attend_call(info, pieces):
    rows = pieces[0].shape[1]
    vmem = pl.BlockSpec(memory_space=pltpu.VMEM)
    return pl.pallas_call(
        functools.partial(place_attend_kernel, len(pieces)),
        in_specs=[pl.BlockSpec(memory_space=pltpu.SMEM)] + [vmem] * len(pieces),
        out_shape=(
            jax.ShapeDtypeStruct((rows, 3 * D), F32),
            jax.ShapeDtypeStruct((rows, D), F32),
        ),
        compiler_params=params(),
        cost_estimate=cost(1e6, 4e6),
        name="place_attend",
    )(info, *pieces)


def add_up(terms):
    total = terms[0].astype(F32)
    for term in terms[1:]:
        total = total + term.astype(F32)
    return total


class Links:
    def __init__(self):
        self.dp_size = lax.axis_size("dp")
        self.seq_size = lax.axis_size("seq")
        self.dp = lax.axis_index("dp")
        self.seq = lax.axis_index("seq")
        self.dp_bits = self.dp_size.bit_length() - 1
        self.seq_bits = self.seq_size.bit_length() - 1

    def swap(self, value, *names):
        flips = {"dp": 0, "seq": 0}
        for axis, bit in names:
            flips[axis] ^= 1 << bit
        pairs = []
        for dp in range(self.dp_size):
            for seq in range(self.seq_size):
                target = (dp ^ flips["dp"]) * self.seq_size + (seq ^ flips["seq"])
                pairs.append((dp * self.seq_size + seq, target))
        return lax.ppermute(value, ("dp", "seq"), pairs)

    def bit(self, name):
        return ((self.dp if name[0] == "dp" else self.seq) >> name[1]) & 1


CORE = ("seq", 0)
X = ("seq", 1)
Y = ("dp", 0)
Z = ("dp", 1)


def pick(value, dim, index):
    return lax.dynamic_index_in_dim(value, index, dim, keepdims=False)


def halve_flow(links, sets, names, order):
    for name in order:
        dim = 1 + names.index(name)
        mine = links.bit(name)
        other = [add_up([pick(term, dim, 1 - mine) for term in terms]) for terms in sets]
        other = other[0] if len(other) == 1 else jnp.concatenate(other, axis=0)
        got = yield links.swap(other.astype(BF), name)
        sets = [[pick(term, dim, mine) for term in terms] for terms in sets]
        first = 0
        for terms in sets:
            count = terms[0].shape[0]
            terms.append(got[first : first + count])
            first += count
        names = names[: dim - 1] + names[dim:]
    return sets


def total_flow(links, sets):
    total = [add_up(terms) for terms in sets]
    total = total[0] if len(total) == 1 else jnp.concatenate(total, axis=0)
    for bit in range(2, links.seq_bits):
        got = yield links.swap(total.astype(BF), ("seq", bit))
        total = total + got.astype(F32)
    return total.astype(BF)


def core_flow(links, send, keep, names, order, rows):
    got = yield links.swap(send, CORE)
    shape = (2, 2) + (2,) * links.dp_bits + (rows, QUAD)
    return (
        yield from halve_flow(links, [[keep.reshape(shape), got.reshape(shape)]], names, order)
    )


def attend_flow(links, sets, names, order):
    sets = yield from halve_flow(links, sets, names, order)
    total = yield from total_flow(links, sets)
    near, across = yield (links.swap(total, CORE), links.swap(total, X))
    far = yield links.swap(across, CORE)
    return [total, near, across, far]


def slice_flow(links, send, keep, rows):
    got = yield links.swap(send, Y)
    shape = (1,) + (2,) * (links.dp_bits - 1) + (rows, keep.shape[-1])
    names = [("dp", bit) for bit in range(links.dp_bits - 1, 0, -1)]
    order = [("dp", bit) for bit in range(2, links.dp_bits)]
    sets = yield from halve_flow(
        links, [[keep.reshape(shape), got.reshape(shape)]], names, order
    )
    total = yield from total_flow(links, sets)
    mine = links.bit(Z)
    own, other = pick(total[0], 0, mine), pick(total[0], 0, 1 - mine)
    over_x, over_z, over_both = yield (
        links.swap(own, X),
        links.swap(other, Z),
        links.swap(other, X, Z),
    )
    near = [own, over_x, over_z, over_both]
    far = yield tuple(links.swap(piece, CORE) for piece in near)
    return [(far if flip & 1 else near)[flip >> 1] for flip in range(8)]


def gather_flow(links, value):
    half = value.shape[0] // 2
    over_x, over_z, far = yield (
        links.swap(value, X),
        links.swap(value, Z),
        links.swap(value, CORE),
    )
    top = links.swap(over_x[:half], Z)
    bottom = links.swap(over_z[half:], X)
    rest = [links.swap(piece, CORE) for piece in (over_x, over_z)]
    top, bottom, *rest = yield (top, bottom, *rest)
    last = yield tuple(links.swap(piece, CORE) for piece in (top, bottom))
    return [value, over_x, over_z, top, bottom, far, *rest, *last]


def small_flow(links, value):
    groups = [(CORE, X), (Y, Z)]
    groups += [(("seq", bit),) for bit in range(2, links.seq_bits)]
    groups += [(("dp", bit),) for bit in range(2, links.dp_bits)]
    for group in groups:
        flips = [group] if len(group) == 1 else [group[:1], group[1:], group]
        arrived = yield tuple(links.swap(value, *flip) for flip in flips)
        value = value + sum(arrived[1:], arrived[0])
    return value


class Flow:
    def __init__(self, generator):
        self.generator = generator
        self.result = None
        self.waiting = next(generator)

    def resume(self, arrived):
        try:
            self.waiting = self.generator.send(arrived)
        except StopIteration as stop:
            self.waiting = None
            self.result = stop.value


def fence(flows, values=()):
    flows = [flow for flow in flows if flow.waiting is not None]
    arrived, values = lax.optimization_barrier(([flow.waiting for flow in flows], tuple(values)))
    for flow, waiting in zip(flows, arrived):
        flow.resume(waiting)
    return values


def finish(flows):
    while any(flow.waiting is not None for flow in flows):
        fence(flows)


def body(
    frames,
    cotangent,
    lengths,
    attend_weight,
    output_weight,
    expand_weight,
    shrink_weight,
    norm_gains,
    norm_biases,
    layer_scales,
):
    rows = frames.shape[1]
    links = Links()
    x = frames.reshape(rows, D)
    dy = cotangent.reshape(rows, D)
    member = links.seq & 3
    slot = links.bit(Z) * 4 + member
    block_rows = D // links.dp_size
    outer = links.dp_size // 2

    def shifted(value, steps):
        count = links.seq_size
        pairs = [(i, i + steps) for i in range(count) if 0 <= i + steps < count]
        return lax.ppermute(value, "seq", pairs)

    def shift_flow(low_edge, high_edge):
        pair = yield (shifted(high_edge, 1), shifted(low_edge, -1))
        return pair

    frames_rim = Flow(shift_flow(x[:WINDOW], x[rows - WINDOW :]))
    dy_flow = Flow(gather_flow(links, dy))
    table_info = jnp.stack([links.seq, jnp.int32(links.seq_size * rows)]).astype(jnp.int32)
    cosine, sine, bias = tables_call(table_info, lengths, rows)
    a1, qkv = project_call(x, norm_gains, norm_biases, cosine, sine, attend_weight)
    (qkv,) = fence([frames_rim], (qkv,))
    low_frames, high_frames = frames_rim.result
    rim = rim_call(low_frames, high_frames, norm_gains, norm_biases, cosine, sine, attend_weight)
    (rim,) = fence([dy_flow], (rim,))
    o, lse, x1, attn, a2 = attend_call(
        qkv, rim, bias, output_weight, x, norm_gains, norm_biases, layer_scales
    )
    (a2, x1) = fence([dy_flow], (a2, x1))
    a2_flow = Flow(gather_flow(links, a2))
    act, dx1, dattn, small_feed = feed_call(
        a2, dy, x1, attn, norm_gains, layer_scales, expand_weight, shrink_weight
    )
    (dattn,) = fence([dy_flow, a2_flow], (dattn,))
    core_info = jnp.stack([jnp.int32(0), jnp.int32(0), links.bit(CORE)]).astype(jnp.int32)
    high_bits = [("dp", bit) for bit in range(links.dp_bits - 1, -1, -1)]
    names = [X] + high_bits
    rest_names = high_bits[:-1]
    rest_order = [("dp", bit) for bit in range(1, links.dp_bits)]

    def slice_chunk(start, size, after):
        info = jnp.stack([(slot * PART + start) // size, links.bit(Y)]).astype(jnp.int32)
        info, after = lax.optimization_barrier((info, after))
        send, keep = slice_call(
            info,
            size,
            a2_flow.result,
            dy_flow.result,
            layer_scales,
            expand_weight,
            shrink_weight,
            rows,
            outer,
        )
        return send, keep

    chunks = [(0, 256), (256, 128), (384, 128)]
    slices = []

    dq, dk, dv, low, high = attend_back_call(
        qkv, rim, bias, cosine, sine, lse, dattn, output_weight
    )

    low, high, dq = fence([a2_flow], (low, high, dq))
    rim_flow = Flow(shift_flow(low, high))
    (dq,) = fence([a2_flow], (dq,))
    send, keep = slice_chunk(*chunks[0], dq)
    send, keep, dq = fence([rim_flow], (send, keep, dq))
    slices.append(Flow(slice_flow(links, send, keep, block_rows)))
    from_low, from_high = rim_flow.result
    kv_send, kv_keep = weight_kv_call(core_info, dk, dv, from_low, from_high, a1)
    kv_send, kv_keep, dq = lax.optimization_barrier((kv_send, kv_keep, dq))
    kv_flow = Flow(core_flow(links, kv_send, kv_keep, names, [Y, X], block_rows))
    qo_send, qo_keep = weight_qo_call(core_info, dq, a1, dattn, o)
    qo_send, qo_keep = fence([kv_flow, slices[0]], (qo_send, qo_keep))
    qo_flow = Flow(core_flow(links, qo_send, qo_keep, names, [X, Y], block_rows))
    (qo_keep,) = fence([qo_flow], (qo_keep,))
    send, keep = slice_chunk(*chunks[1], qo_keep)
    send, keep = fence([qo_flow, kv_flow, slices[0]], (send, keep))
    slices.append(Flow(slice_flow(links, send, keep, block_rows)))
    send, keep = slice_chunk(*chunks[2], keep)
    send, keep, dx1 = fence([qo_flow, kv_flow, *slices], (send, keep, dx1))
    attends = Flow(attend_flow(links, qo_flow.result + kv_flow.result, rest_names, rest_order))
    slices.append(Flow(slice_flow(links, send, keep, block_rows)))
    input_gradient, small_first = input_back_call(
        dq, dk, dv, from_low, from_high, x, dx1, norm_gains, attend_weight
    )
    (small_first,) = fence([attends, *slices], (small_first,))
    small = jnp.concatenate([small_feed[:4], small_first[:2], jnp.zeros((2, D), F32)], axis=0)
    small = Flow(small_flow(links, small))
    finish([attends, small, *slices])
    member_info = member.reshape(1).astype(jnp.int32)
    attend_grad, output_grad = place_attend_call(member_info, attends.result)
    expand_grad, shrink_grad = place_call(
        slot.reshape(1).astype(jnp.int32),
        tuple(start for start, _ in chunks),
        [flow.result for flow in slices],
    )
    small = lax.dynamic_slice_in_dim(small.result, links.dp * block_rows, block_rows, axis=1)
    gains_grad = jnp.stack([small[4], small[1]])
    biases_grad = jnp.stack([small[5], small[2]])
    scales_grad = jnp.stack([small[3], small[0]])
    return (
        act.reshape(frames.shape),
        input_gradient.reshape(frames.shape),
        attend_grad,
        output_grad,
        expand_grad,
        shrink_grad,
        gains_grad,
        biases_grad,
        scales_grad,
    )


def solution(mesh):
    in_specs = (
        P("dp", "seq", None),
        P("dp", "seq", None),
        P("dp", None),
        P(),
        P(),
        P(),
        P(),
        P(),
        P(),
        P(),
    )
    out_specs = (
        P("dp", "seq", None),
        P("dp", "seq", None),
        P("dp", None),
        P("dp", None),
        P("dp", None),
        P(None, "dp"),
        P(None, "dp"),
        P(None, "dp"),
        P(None, "dp"),
    )
    return jax.shard_map(body, mesh=mesh, in_specs=in_specs, out_specs=out_specs, check_vma=False)
```

```python
import functools
import math

import jax
import jax.numpy as jnp
from jax import lax
from jax.experimental import pallas as pl
from jax.experimental.pallas import tpu as pltpu
from jax.sharding import PartitionSpec as P

D = 1024
HEADS = 16
HEAD_DIM = 64
FF = 4096
WINDOW = 128
QUAD = 4 * HEAD_DIM
SLICES = 8
PART = FF // SLICES
HALF = PART // 2
EPS = 1e-05
BF = jnp.bfloat16
F32 = jnp.float32
VMEM_BYTES = 58 * 1024 * 1024


def dot_nn(a, b):
    return lax.dot_general(a, b, (((1,), (0,)), ((), ())), preferred_element_type=F32)


def dot_nt(a, b):
    return lax.dot_general(a, b, (((1,), (1,)), ((), ())), preferred_element_type=F32)


def dot_tn(a, b):
    return lax.dot_general(a, b, (((0,), (0,)), ((), ())), preferred_element_type=F32)


def params(**extra):
    return pltpu.CompilerParams(vmem_limit_bytes=VMEM_BYTES, **extra)


def cost(flops, size, transcendentals=0):
    return pl.CostEstimate(
        flops=int(flops), bytes_accessed=int(size), transcendentals=int(transcendentals)
    )


def whole(shape):
    return pl.BlockSpec(shape, lambda *_: (0,) * len(shape))


def norm_stats(values):
    centered = values - jnp.mean(values, axis=-1, keepdims=True)
    inverse = lax.rsqrt(jnp.mean(centered * centered, axis=-1, keepdims=True) + EPS)
    return (centered * inverse, inverse)


def norm_back(gradient, normed, inverse, gain_row):
    scaled = gradient * gain_row
    return inverse * (
        scaled
        - jnp.mean(scaled, axis=-1, keepdims=True)
        - normed * jnp.mean(scaled * normed, axis=-1, keepdims=True)
    )


def turn(values, cosine, sine, sign):
    lane = lax.broadcasted_iota(jnp.int32, (values.shape[0], 128), 1) % HEAD_DIM
    parts = []
    for group in range(values.shape[1] // 128):
        part = values[:, group * 128 : group * 128 + 128]
        swapped = jnp.where(
            lane < HEAD_DIM // 2, pltpu.roll(part, 96, 1), pltpu.roll(part, 32, 1)
        )
        if sign > 0:
            parts.append(part * cosine + swapped * sine)
        else:
            parts.append(part * cosine - swapped * sine)
    return jnp.concatenate(parts, axis=1)


def tables_kernel(info_ref, lengths_ref, cos_ref, sin_ref, bias_ref):
    wide = cos_ref.shape[0]
    rows = wide - 2 * WINDOW
    base = info_ref[0] * rows
    total = info_ref[1]
    frame = base - WINDOW + lax.broadcasted_iota(jnp.int32, (8, wide), 1)

    def step(entry, carry):
        start, clip, begin = carry
        inside = frame >= start
        clip = clip + inside.astype(jnp.int32)
        begin = jnp.where(inside, start, begin)
        return (start + lengths_ref[0, entry], clip, begin)

    _, clip, begin = lax.fori_loop(
        0,
        lengths_ref.shape[1],
        step,
        (jnp.int32(0), jnp.full((8, wide), -1, jnp.int32), jnp.zeros((8, wide), jnp.int32)),
    )
    query_clip = clip[0:1, WINDOW : WINDOW + rows].astype(F32)
    clip = jnp.where((frame >= 0) & (frame < total), clip, -1).astype(F32)
    place = (frame - begin).astype(F32)
    key_clip = jnp.broadcast_to(clip[0:1, :], (128, wide)).T
    half = HEAD_DIM // 2
    pack = 128 // half
    part = wide // pack
    packed = jnp.concatenate(
        [
            jnp.broadcast_to(place[0:1, at * part : at * part + part], (half, part))
            for at in range(pack)
        ],
        axis=0,
    ).T
    lane = lax.broadcasted_iota(jnp.int32, (part, 128), 1)
    frequency = jnp.exp((lane % half).astype(F32) * (-2.0 * math.log(10000.0) / HEAD_DIM))
    angle = packed * frequency
    sine, cosine = jnp.sin(angle), jnp.cos(angle)
    sign = jnp.where(lane % HEAD_DIM < half, -1.0, 1.0)
    for at in range(pack):
        for source, target, factor in ((cosine, cos_ref, None), (sine, sin_ref, sign)):
            value = pltpu.roll(source, (128 - at * half) % 128, 1) if at else source
            value = jnp.where(lane < half, value, 0.0)
            value = value + pltpu.roll(value, half, 1)
            value = value + pltpu.roll(value, 2 * half, 1)
            target[at * part : at * part + part, :] = value if factor is None else value * factor
    span = 3 * WINDOW
    gap = lax.broadcasted_iota(jnp.int32, (span, 128), 0) - lax.broadcasted_iota(
        jnp.int32, (span, 128), 1
    )
    near = (gap >= 0) & (gap <= 2 * WINDOW)
    for block in range(rows // WINDOW):
        at = block * WINDOW
        same = key_clip[at : at + span] == query_clip[:, at : at + WINDOW]
        bias_ref[block] = jnp.where(near & same, 0.0, -1e30)


def tables_call(info, lengths, rows):
    wide = rows + 2 * WINDOW
    return pl.pallas_call(
        tables_kernel,
        out_shape=(
            jax.ShapeDtypeStruct((wide, 128), F32),
            jax.ShapeDtypeStruct((wide, 128), F32),
            jax.ShapeDtypeStruct((rows // WINDOW, 3 * WINDOW, 128), F32),
        ),
        in_specs=[
            pl.BlockSpec(memory_space=pltpu.SMEM),
            pl.BlockSpec(memory_space=pltpu.SMEM),
        ],
        compiler_params=params(),
        cost_estimate=cost(1e8, 2e6),
        name="tables",
    )(info, lengths)


def project_kernel(x_ref, gain_ref, shift_ref, cos_ref, sin_ref, weight_ref, a1_ref, out_ref):
    chunk = pl.program_id(0)
    rows = x_ref.shape[0]

    @pl.when(chunk == 0)
    def _():
        normed, _unused = norm_stats(x_ref[...].astype(F32))
        a1_ref[...] = (normed * gain_ref[0:1, :] + shift_ref[0:1, :]).astype(BF)

    projected = dot_nn(a1_ref[...], weight_ref[...])
    cosine = cos_ref[WINDOW : WINDOW + rows, :]
    sine = sin_ref[WINDOW : WINDOW + rows, :]

    @pl.when(chunk == 0)
    def _():
        out_ref[...] = (turn(projected, cosine, sine, 1) * HEAD_DIM**-0.5).astype(BF)

    @pl.when(chunk == 1)
    def _():
        out_ref[...] = turn(projected, cosine, sine, 1).astype(BF)

    @pl.when(chunk == 2)
    def _():
        out_ref[...] = projected.astype(BF)


def project_call(x, gains, shifts, cosine, sine, weight):
    rows = x.shape[0]
    wide = cosine.shape[0]
    return pl.pallas_call(
        project_kernel,
        grid=(3,),
        out_shape=(
            jax.ShapeDtypeStruct((rows, D), BF),
            jax.ShapeDtypeStruct((rows, 3 * D), BF),
        ),
        in_specs=[
            whole((rows, D)),
            whole((2, D)),
            whole((2, D)),
            whole((wide, 128)),
            whole((wide, 128)),
            pl.BlockSpec((D, D), lambda c: (0, c)),
        ],
        out_specs=(whole((rows, D)), pl.BlockSpec((rows, D), lambda c: (0, c))),
        compiler_params=params(),
        cost_estimate=cost(2 * rows * D * 3 * D, 12e6),
        name="project",
    )(x, gains, shifts, cosine, sine, weight)


def rim_kernel(
    low_ref, high_ref, gain_ref, shift_ref, cos_ref, sin_ref, weight_ref, a1_ref, out_ref
):
    chunk = pl.program_id(0)
    wide = cos_ref.shape[0]

    @pl.when(chunk == 0)
    def _():
        for at, ref in ((0, low_ref), (WINDOW, high_ref)):
            normed, _unused = norm_stats(ref[...].astype(F32))
            a1_ref[at : at + WINDOW, :] = (
                normed * gain_ref[0:1, :] + shift_ref[0:1, :]
            ).astype(BF)

    projected = dot_nn(a1_ref[...], weight_ref[...])

    @pl.when(chunk == 0)
    def _():
        cosine = jnp.concatenate([cos_ref[:WINDOW, :], cos_ref[wide - WINDOW :, :]], axis=0)
        sine = jnp.concatenate([sin_ref[:WINDOW, :], sin_ref[wide - WINDOW :, :]], axis=0)
        out_ref[...] = turn(projected, cosine, sine, 1).astype(BF)

    @pl.when(chunk == 1)
    def _():
        out_ref[...] = projected.astype(BF)


def rim_call(low, high, gains, shifts, cosine, sine, weight):
    wide = cosine.shape[0]
    return pl.pallas_call(
        rim_kernel,
        grid=(2,),
        out_shape=(
            jax.ShapeDtypeStruct((2 * WINDOW, D), BF),
            jax.ShapeDtypeStruct((2 * WINDOW, 2 * D), BF),
        ),
        in_specs=[
            whole((WINDOW, D)),
            whole((WINDOW, D)),
            whole((2, D)),
            whole((2, D)),
            whole((wide, 128)),
            whole((wide, 128)),
            pl.BlockSpec((D, D), lambda c: (0, c + 1)),
        ],
        out_specs=(whole((2 * WINDOW, D)), pl.BlockSpec((2 * WINDOW, D), lambda c: (0, c))),
        compiler_params=params(),
        cost_estimate=cost(2 * 256 * D * 2 * D, 6e6),
        name="rim",
    )(low, high, gains, shifts, cosine, sine, weight)


def stacked(block):
    owner = lax.broadcasted_iota(jnp.int32, block.shape, 1) // HEAD_DIM
    zero = jnp.zeros_like(block)
    return jnp.concatenate([jnp.where(owner == head, block, zero) for head in range(4)], axis=0)


def attend_kernel(
    q_ref,
    k_ref,
    v_ref,
    rim_k_ref,
    rim_v_ref,
    bias_ref,
    weight_ref,
    x_ref,
    gain_ref,
    shift_ref,
    scale_ref,
    o_ref,
    lse_ref,
    x1_ref,
    attn_ref,
    a2_ref,
    keys,
    values_t,
    mixed_t,
    total,
):
    quad = pl.program_id(0)
    rows = q_ref.shape[0]
    keys[0:WINDOW, :] = rim_k_ref[0:WINDOW, :]
    keys[WINDOW : WINDOW + rows, :] = k_ref[...]
    keys[WINDOW + rows :, :] = rim_k_ref[WINDOW:, :]
    values_t[:, 0:WINDOW] = rim_v_ref[0:WINDOW, :].T
    values_t[:, WINDOW : WINDOW + rows] = v_ref[...].T
    values_t[:, WINDOW + rows :] = rim_v_ref[WINDOW:, :].T
    for block in range(rows // WINDOW):
        at = block * WINDOW
        queries = stacked(q_ref[at : at + WINDOW, :])
        scores = dot_nt(keys[at : at + 3 * WINDOW, :], queries)
        bias = bias_ref[block]
        scores = scores + jnp.concatenate([bias] * 4, axis=1)
        top = jnp.max(scores, axis=0, keepdims=True)
        weights = jnp.exp(scores - top)
        total_row = jnp.sum(weights, axis=0, keepdims=True)
        weights = (weights * (1.0 / total_row)).astype(BF)
        log_row = top + jnp.log(total_row)
        for head in range(4):
            lanes = slice(head * WINDOW, head * WINDOW + WINDOW)
            lse_ref[0, head : head + 1, at : at + WINDOW] = log_row[:, lanes]
            feature = slice(head * HEAD_DIM, head * HEAD_DIM + HEAD_DIM)
            mixed_t[feature, at : at + WINDOW] = dot_nn(
                values_t[feature, at : at + 3 * WINDOW], weights[:, lanes]
            )
    mixed = mixed_t[...].T.astype(BF)
    o_ref[...] = mixed
    branch = dot_nn(mixed, weight_ref[...])

    @pl.when(quad == 0)
    def _():
        total[...] = branch

    @pl.when(quad > 0)
    def _():
        total[...] += branch

    @pl.when(quad == HEADS // 4 - 1)
    def _():
        attn = total[...]
        residual = x_ref[...].astype(F32) + attn * scale_ref[0:1, :]
        normed, _unused = norm_stats(residual)
        x1_ref[...] = residual
        attn_ref[...] = attn.astype(BF)
        a2_ref[...] = (normed * gain_ref[1:2, :] + shift_ref[1:2, :]).astype(BF)


def attend_call(qkv, rim, bias, weight, x, gains, shifts, scales):
    rows = x.shape[0]
    wide = rows + 2 * WINDOW
    row_spec = whole((rows, D))
    return pl.pallas_call(
        attend_kernel,
        grid=(HEADS // 4,),
        out_shape=(
            jax.ShapeDtypeStruct((rows, D), BF),
            jax.ShapeDtypeStruct((HEADS // 4, 8, rows), F32),
            jax.ShapeDtypeStruct((rows, D), F32),
            jax.ShapeDtypeStruct((rows, D), BF),
            jax.ShapeDtypeStruct((rows, D), BF),
        ),
        in_specs=[
            pl.BlockSpec((rows, QUAD), lambda h: (0, h)),
            pl.BlockSpec((rows, QUAD), lambda h: (0, h + 4)),
            pl.BlockSpec((rows, QUAD), lambda h: (0, h + 8)),
            pl.BlockSpec((2 * WINDOW, QUAD), lambda h: (0, h)),
            pl.BlockSpec((2 * WINDOW, QUAD), lambda h: (0, h + 4)),
            whole(bias.shape),
            pl.BlockSpec((QUAD, D), lambda h: (h, 0)),
            row_spec,
            whole((2, D)),
            whole((2, D)),
            whole((2, D)),
        ],
        out_specs=(
            pl.BlockSpec((rows, QUAD), lambda h: (0, h)),
            pl.BlockSpec((1, 8, rows), lambda h: (h, 0, 0)),
            row_spec,
            row_spec,
            row_spec,
        ),
        scratch_shapes=[
            pltpu.VMEM((wide, QUAD), BF),
            pltpu.VMEM((QUAD, wide), BF),
            pltpu.VMEM((QUAD, rows), F32),
            pltpu.VMEM((rows, D), F32),
        ],
        compiler_params=params(),
        cost_estimate=cost(8e9, 14e6, 3e6),
        name="attend",
    )(qkv, qkv, qkv, rim, rim, bias, weight, x, gains, shifts, scales)


def gated(gate, up, grad_hidden):
    sigmoid = 0.5 * jnp.tanh(0.5 * gate) + 0.5
    swish = gate * sigmoid
    hidden = swish * up
    grad_gate = grad_hidden * up * (sigmoid + swish * (1.0 - sigmoid))
    grad_up = grad_hidden * swish
    return (hidden.astype(BF), grad_gate.astype(BF), grad_up.astype(BF))


def feed_kernel(
    a2_ref,
    dy_ref,
    gain_ref,
    scale_ref,
    x1_hbm,
    attn_hbm,
    expand_hbm,
    shrink_hbm,
    act_hbm,
    dx1_ref,
    dattn_ref,
    small_ref,
    expand,
    shrink,
    hidden,
    grads,
    x1,
    attn,
    act,
    sems,
    late_sems,
):
    width = 512
    step = 256
    groups = FF // width
    copies = []
    for group in range(groups):
        at = group * width
        copies.append(
            [
                pltpu.make_async_copy(
                    expand_hbm.at[:, pl.ds(at, width)],
                    expand.at[:, pl.ds(at, width)],
                    sems.at[group, 0],
                ),
                pltpu.make_async_copy(
                    expand_hbm.at[:, pl.ds(FF + at, width)],
                    expand.at[:, pl.ds(FF + at, width)],
                    sems.at[group, 1],
                ),
                pltpu.make_async_copy(
                    shrink_hbm.at[pl.ds(at, width), :],
                    shrink.at[pl.ds(at, width), :],
                    sems.at[group, 2],
                ),
            ]
        )
    late = [
        pltpu.make_async_copy(x1_hbm, x1, late_sems.at[0]),
        pltpu.make_async_copy(attn_hbm, attn, late_sems.at[1]),
    ]
    ahead = 3
    for group in range(ahead):
        for copy in copies[group]:
            copy.start()
    branch_grad = (dy_ref[...].astype(F32) * scale_ref[1:2, :]).astype(BF)
    a2 = a2_ref[...]

    for chunk in range(FF // step):
        at = chunk * step
        if at % width == 0:
            group = at // width
            if group + ahead < groups:
                for copy in copies[group + ahead]:
                    copy.start()
            elif group + ahead == groups:
                for copy in late:
                    copy.start()
            for copy in copies[group]:
                copy.wait()
        gate = dot_nn(a2, expand[:, at : at + step])
        up = dot_nn(a2, expand[:, FF + at : FF + at + step])
        grad_hidden = dot_nt(branch_grad, shrink[at : at + step, :])
        out, grad_gate, grad_up = gated(gate, up, grad_hidden)
        hidden[:, at : at + step] = out
        grads[:, at : at + step] = grad_gate
        grads[:, FF + at : FF + at + step] = grad_up
    branch = dot_nn(hidden[...], shrink[...])
    for copy in late:
        copy.wait()
    residual = x1[...]
    grad_result = dy_ref[...].astype(F32)
    act[...] = (residual + branch * scale_ref[1:2, :]).astype(BF)
    out_copy = pltpu.make_async_copy(act, act_hbm, late_sems.at[2])
    out_copy.start()
    small_ref[0:1, :] = jnp.sum(grad_result * branch, axis=0, keepdims=True)
    grad_normed = dot_nt(grads[...], expand[...])
    normed, inverse = norm_stats(residual)
    small_ref[1:2, :] = jnp.sum(grad_normed * normed, axis=0, keepdims=True)
    small_ref[2:3, :] = jnp.sum(grad_normed, axis=0, keepdims=True)
    grad_residual = grad_result + norm_back(grad_normed, normed, inverse, gain_ref[1:2, :])
    dx1_ref[...] = grad_residual
    small_ref[3:4, :] = jnp.sum(grad_residual * attn[...].astype(F32), axis=0, keepdims=True)
    small_ref[4:8, :] = jnp.zeros((4, D), F32)
    dattn_ref[...] = (grad_residual * scale_ref[0:1, :]).astype(BF)
    out_copy.wait()


def feed_call(a2, dy, x1, attn, gains, scales, expand, shrink):
    rows = a2.shape[0]
    vmem = pl.BlockSpec(memory_space=pltpu.VMEM)
    hbm = pl.BlockSpec(memory_space=pl.ANY)
    return pl.pallas_call(
        feed_kernel,
        out_shape=(
            jax.ShapeDtypeStruct((rows, D), BF),
            jax.ShapeDtypeStruct((rows, D), F32),
            jax.ShapeDtypeStruct((rows, D), BF),
            jax.ShapeDtypeStruct((8, D), F32),
        ),
        in_specs=[vmem] * 4 + [hbm] * 4,
        out_specs=(hbm, vmem, vmem, vmem),
        scratch_shapes=[
            pltpu.VMEM((D, 2 * FF), BF),
            pltpu.VMEM((FF, D), BF),
            pltpu.VMEM((rows, FF), BF),
            pltpu.VMEM((rows, 2 * FF), BF),
            pltpu.VMEM((rows, D), F32),
            pltpu.VMEM((rows, D), BF),
            pltpu.VMEM((rows, D), BF),
            pltpu.SemaphoreType.DMA((FF // 512, 3)),
            pltpu.SemaphoreType.DMA((3,)),
        ],
        compiler_params=params(),
        cost_estimate=cost(2 * rows * D * FF * 6, 36e6, rows * FF),
        name="feed",
    )(a2, dy, gains, scales, x1, attn, expand, shrink)


def slice_kernel(pieces, info_ref, *refs):
    a2_refs = refs[: len(pieces)]
    dy_refs = refs[len(pieces) : 2 * len(pieces)]
    scale_ref, gate_w_ref, up_w_ref, shrink_w_ref = refs[2 * len(pieces) : 2 * len(pieces) + 4]
    pair_send, pair_keep, back_send, back_keep = refs[2 * len(pieces) + 4 :][:4]
    a2_all, dm_all, inner, result, sems = refs[2 * len(pieces) + 8 :]
    size = gate_w_ref.shape[1]
    groups = 1 + max(slot for slot, _, _ in pieces)
    rows = a2_all.shape[0] // groups
    copies = [[] for _ in range(groups)]
    for number, (slot, first, count) in enumerate(pieces):
        for kind, (sources, held) in enumerate(((a2_refs, a2_all), (dy_refs, dm_all))):
            copies[slot].append(
                pltpu.make_async_copy(
                    sources[number],
                    held.at[pl.ds(slot * rows + first, count), :],
                    sems.at[kind, number],
                )
            )
    for slot in range(min(2, groups)):
        for copy in copies[slot]:
            copy.start()
    scale = scale_ref[1:2, :]
    for slot in range(groups):
        if slot + 2 < groups:
            for copy in copies[slot + 2]:
                copy.start()
        for copy in copies[slot]:
            copy.wait()
        span = slice(slot * rows, slot * rows + rows)
        branch_grad = (dm_all[span, :].astype(F32) * scale).astype(BF)
        dm_all[span, :] = branch_grad
        gate = dot_nn(a2_all[span, :], gate_w_ref[...])
        up = dot_nn(a2_all[span, :], up_w_ref[...])
        grad_hidden = dot_nt(branch_grad, shrink_w_ref[...])
        hidden, grad_gate, grad_up = gated(gate, up, grad_hidden)
        inner[span, :size] = grad_gate
        inner[span, size : 2 * size] = grad_up
        inner[span, 2 * size :] = hidden
    result[:, : 2 * size] = dot_tn(a2_all[...], inner[:, : 2 * size]).astype(BF)
    result[:, 2 * size :] = dot_tn(dm_all[...], inner[:, 2 * size :]).astype(BF)
    columns = (slice(0, 2 * size), slice(2 * size, 3 * size))
    for lanes, mine, send_ref, keep_ref in (
        (columns[0], info_ref[1], pair_send, pair_keep),
        (columns[1], info_ref[2], back_send, back_keep),
    ):
        outer, span, _ = send_ref.shape
        for at in range(outer):
            for target, bit in ((send_ref, 1 - mine), (keep_ref, mine)):
                first = pl.multiple_of(at * 2 * span + bit * span, span)
                target[at] = result[pl.ds(first, span), lanes]


def slice_call(info, a2_list, dy_list, scales, expand, shrink, rows, block_rows):
    size = PART
    pieces = []
    slot, first = 0, 0
    for piece in a2_list:
        pieces.append((slot, first, piece.shape[0]))
        first += piece.shape[0]
        if first == rows:
            slot, first = slot + 1, 0
    groups = slot
    hbm = pl.BlockSpec(memory_space=pl.ANY)
    pair_shape = (D // (2 * block_rows), block_rows, 2 * size)
    back_shape = (D // (8 * block_rows), 4 * block_rows, size)
    shapes = (pair_shape, pair_shape, back_shape, back_shape)
    return pl.pallas_call(
        functools.partial(slice_kernel, tuple(pieces)),
        grid_spec=pltpu.PrefetchScalarGridSpec(
            num_scalar_prefetch=1,
            grid=(1,),
            in_specs=[hbm] * (2 * len(pieces))
            + [
                pl.BlockSpec((2, D), lambda i, info: (0, 0)),
                pl.BlockSpec((D, size), lambda i, info: (0, info[0])),
                pl.BlockSpec((D, size), lambda i, info: (0, info[0] + FF // size)),
                pl.BlockSpec((size, D), lambda i, info: (info[0], 0)),
            ],
            out_specs=[pl.BlockSpec(shape, lambda i, info: (0, 0, 0)) for shape in shapes],
            scratch_shapes=[
                pltpu.VMEM((groups * rows, D), BF),
                pltpu.VMEM((groups * rows, D), BF),
                pltpu.VMEM((groups * rows, 3 * size), BF),
                pltpu.VMEM((D, 3 * size), BF),
                pltpu.SemaphoreType.DMA((2, len(pieces))),
            ],
        ),
        out_shape=[jax.ShapeDtypeStruct(shape, BF) for shape in shapes],
        compiler_params=params(),
        cost_estimate=cost(2 * groups * rows * D * size * 6, 22e6, groups * rows * size),
        name="slice_grads",
    )(info, *a2_list, *dy_list, scales, expand, expand, shrink)


def attend_back_kernel(
    last,
    info_ref,
    q_ref,
    k_ref,
    v_ref,
    rim_k_ref,
    rim_v_ref,
    bias_ref,
    cos_ref,
    sin_ref,
    lse_ref,
    dattn_ref,
    dattn_part_ref,
    weight_ref,
    a1_ref,
    a1_rim_ref,
    o_ref,
    *refs,
):
    if last:
        got_ref, *refs = refs
    dq_ref, dk_ref, dv_ref, low_ref, high_ref, *refs = refs
    if last:
        qo_send, qo_keep, kv_send, kv_keep, *refs = refs
    else:
        grads_ref, *refs = refs
    a1, keys, values, keys_t, grad_q_t, grad_k, grad_v, whole_grad = refs
    step = pl.program_id(0)

    def deliver(block, grad):
        if not last:
            grads_ref[block, 0] = grad.astype(BF)
            return
        grad = (grad + got_ref[block, 0].astype(F32)).astype(BF)
        if block < 2:

            @pl.when(step == 0)
            def _():
                qo_send[block] = grad

            @pl.when(step == 1)
            def _():
                qo_keep[block] = grad

            return
        whole_grad[...] = grad
        mine = info_ref[2]
        outer, span = kv_send.shape[2:4]
        for at in range(outer):
            for target, bit in ((kv_send, 1 - mine), (kv_keep, mine)):
                first = pl.multiple_of(at * 2 * span + bit * span, span)
                target[block - 2, 0, at] = whole_grad[pl.ds(first, span), :]

    rows = q_ref.shape[0]
    low, own, high = slice(0, WINDOW), slice(WINDOW, WINDOW + rows), slice(WINDOW + rows, None)

    @pl.when(step == 0)
    def _():
        a1[low, :] = a1_rim_ref[:WINDOW, :]
        a1[own, :] = a1_ref[...]
        a1[high, :] = a1_rim_ref[WINDOW:, :]

    for held, mine, rim in ((keys, k_ref, rim_k_ref), (values, v_ref, rim_v_ref)):
        held[low, :] = rim[:WINDOW, :]
        held[own, :] = mine[...]
        held[high, :] = rim[WINDOW:, :]
    keys_t[...] = keys[...].T
    grad_mixed = dot_nt(dattn_ref[...], weight_ref[...]).astype(BF)
    deliver(1, dot_tn(o_ref[...], dattn_part_ref[...]))
    grad_k[...] = jnp.zeros_like(grad_k)
    grad_v[...] = jnp.zeros_like(grad_v)
    for block in range(rows // WINDOW):
        at = block * WINDOW
        span = slice(at, at + 3 * WINDOW)
        queries = stacked(q_ref[at : at + WINDOW, :])
        grad_out = stacked(grad_mixed[at : at + WINDOW, :])
        scores = dot_nt(keys[span, :], queries)
        log_row = jnp.concatenate(
            [lse_ref[0, head : head + 1, at : at + WINDOW] for head in range(4)], axis=1
        )
        bias = bias_ref[block]
        weights = jnp.exp(scores + jnp.concatenate([bias] * 4, axis=1) - log_row)
        grad_weights = dot_nt(values[span, :], grad_out)
        weighted = weights * grad_weights
        grad_scores = weighted - weights * jnp.sum(weighted, axis=0, keepdims=True)
        grad_scores = grad_scores.astype(BF)
        grad_v[span, :] += dot_nn(weights.astype(BF), grad_out)
        grad_k[span, :] += dot_nn(grad_scores, queries)
        for head in range(4):
            feature = slice(head * HEAD_DIM, head * HEAD_DIM + HEAD_DIM)
            grad_q_t[feature, at : at + WINDOW] = dot_nn(
                keys_t[feature, span], grad_scores[:, head * WINDOW : head * WINDOW + WINDOW]
            )
    cosine, sine = cos_ref[...], sin_ref[...]
    grad_q = turn(grad_q_t[...].T * HEAD_DIM**-0.5, cosine[own, :], sine[own, :], -1).astype(BF)
    turned = turn(grad_k[...], cosine, sine, -1).astype(BF)
    grad_values = grad_v[...].astype(BF)
    deliver(0, dot_tn(a1_ref[...], grad_q))
    deliver(2, dot_tn(a1[...], turned))
    deliver(3, dot_tn(a1[...], grad_values))
    dq_ref[0] = grad_q
    dk_ref[0] = turned[own, :]
    dv_ref[0] = grad_values[own, :]
    low_ref[0, 0] = turned[low, :]
    low_ref[1, 0] = grad_values[low, :]
    high_ref[0, 0] = turned[high, :]
    high_ref[1, 0] = grad_values[high, :]


def attend_back_call(
    info, qkv, rim, bias, cosine, sine, lse, dattn, weight, a1, a1_rim, o, block_rows, got=None
):
    rows = dattn.shape[0]
    wide = rows + 2 * WINDOW
    last = got is not None
    row_shape = jax.ShapeDtypeStruct((2, rows, QUAD), BF)
    rim_shape = jax.ShapeDtypeStruct((2, 2, WINDOW, QUAD), BF)
    row_spec = pl.BlockSpec((1, rows, QUAD), lambda s, info: (s, 0, 0))

    def quad(s, info):
        return 2 * (s ^ (1 - info[1])) + info[0]

    rim_spec = pl.BlockSpec(
        (2, 1, WINDOW, QUAD), lambda s, info: (0, s ^ (1 - info[1]), 0, 0)
    )

    def columns(count, first):
        return pl.BlockSpec((count, QUAD), lambda s, info: (0, first + quad(s, info)))

    grads_spec = pl.BlockSpec((4, 1, D, QUAD), lambda s, info: (0, s, 0, 0))
    if last:
        outer, span = D // (4 * block_rows), 2 * block_rows
        kv_shape = jax.ShapeDtypeStruct((2, 2, outer, span, QUAD), BF)
        kv_spec = pl.BlockSpec(
            (2, 1, outer, span, QUAD), lambda s, info: (0, s, 0, 0, 0)
        )
        qo_shape = jax.ShapeDtypeStruct((2, D, QUAD), BF)
        grad_specs = [whole((2, D, QUAD))] * 2 + [kv_spec] * 2
        grad_shapes = [qo_shape] * 2 + [kv_shape] * 2
    else:
        grad_specs = [grads_spec]
        grad_shapes = [jax.ShapeDtypeStruct((4, 2, D, QUAD), BF)]
    operands = [
        info,
        qkv,
        qkv,
        qkv,
        rim,
        rim,
        bias,
        cosine,
        sine,
        lse,
        dattn,
        dattn,
        weight,
        a1,
        a1_rim,
        o,
    ]
    return pl.pallas_call(
        functools.partial(attend_back_kernel, last),
        grid_spec=pltpu.PrefetchScalarGridSpec(
            num_scalar_prefetch=1,
            grid=(2,),
            in_specs=[
                columns(rows, 0),
                columns(rows, 4),
                columns(rows, 8),
                columns(2 * WINDOW, 0),
                columns(2 * WINDOW, 4),
                whole(bias.shape),
                whole((wide, 128)),
                whole((wide, 128)),
                pl.BlockSpec((1, 8, rows), lambda s, info: (quad(s, info), 0, 0)),
                whole((rows, D)),
                columns(rows, 0),
                pl.BlockSpec((QUAD, D), lambda s, info: (quad(s, info), 0)),
                whole((rows, D)),
                whole((2 * WINDOW, D)),
                whole((rows, D)),
            ]
            + [grads_spec] * last,
            out_specs=[row_spec] * 3 + [rim_spec] * 2 + grad_specs,
            scratch_shapes=[
                pltpu.VMEM((wide, D), BF),
                pltpu.VMEM((wide, QUAD), BF),
                pltpu.VMEM((wide, QUAD), BF),
                pltpu.VMEM((QUAD, wide), BF),
                pltpu.VMEM((QUAD, rows), F32),
                pltpu.VMEM((wide, QUAD), F32),
                pltpu.VMEM((wide, QUAD), F32),
                pltpu.VMEM((D, QUAD), BF),
            ],
        ),
        out_shape=[row_shape] * 3 + [rim_shape] * 2 + grad_shapes,
        compiler_params=params(),
        cost_estimate=cost(1e6, 1e6),
        name="attend_back",
    )(*operands, *([got] if last else []))


def input_back_kernel(
    info_ref,
    keep_q,
    keep_k,
    keep_v,
    send_q,
    send_k,
    send_v,
    low_ref,
    high_ref,
    gain_ref,
    weight_ref,
    x_hbm,
    dx1_hbm,
    grad_ref,
    small_ref,
    part,
    back,
    x,
    dx1,
    sems,
):
    chunk = pl.program_id(0)
    rows = x.shape[0]
    late = [
        pltpu.make_async_copy(x_hbm, x, sems.at[0]),
        pltpu.make_async_copy(dx1_hbm, dx1, sems.at[1]),
    ]

    @pl.when(chunk == 0)
    def _():
        for copy in late:
            copy.start()
        back[...] = jnp.zeros_like(back)

    for kind, pair in enumerate(((keep_q, send_q), (keep_k, send_k), (keep_v, send_v))):

        @pl.when(chunk // 2 == kind)
        def _():
            for core in range(2):

                @pl.when(info_ref[0] == core)
                def _():
                    for at, ref in ((core, pair[0]), (1 - core, pair[1])):
                        lanes = slice(at * QUAD, at * QUAD + QUAD)
                        part[:, lanes] = ref[0]

            if kind > 0:
                for core in range(2):

                    @pl.when(info_ref[0] == core)
                    def _():
                        for at, which in ((core, 1), (1 - core, 0)):
                            lanes = slice(at * QUAD, at * QUAD + QUAD)
                            for first, rim in ((0, low_ref), (rows - WINDOW, high_ref)):
                                span = slice(first, first + WINDOW)
                                part[span, lanes] = (
                                    part[span, lanes].astype(F32)
                                    + rim[which, 0, 0].astype(F32)
                                ).astype(BF)

    back[...] += dot_nt(part[...], weight_ref[...])

    @pl.when(chunk == pl.num_programs(0) - 1)
    def _():
        for copy in late:
            copy.wait()
        grad_normed = back[...]
        normed, inverse = norm_stats(x[...].astype(F32))
        small_ref[0:1, :] = jnp.sum(grad_normed * normed, axis=0, keepdims=True)
        small_ref[1:2, :] = jnp.sum(grad_normed, axis=0, keepdims=True)
        small_ref[2:8, :] = jnp.zeros((6, D), F32)
        grad_ref[...] = (
            dx1[...] + norm_back(grad_normed, normed, inverse, gain_ref[0:1, :])
        ).astype(BF)


def input_back_call(info, keep, send, low, high, x, dx1, gains, weight):
    rows = x.shape[0]

    def own_spec(kind):
        return pl.BlockSpec((1, rows, QUAD), lambda c, info: (c % 2, 0, 0))

    rim_spec = pl.BlockSpec(
        (2, 1, 1, WINDOW, QUAD),
        lambda c, info: (0, jnp.maximum(c // 2 - 1, 0), (c % 2) ^ (1 - info[1]), 0, 0),
    )
    hbm = pl.BlockSpec(memory_space=pl.ANY)
    return pl.pallas_call(
        input_back_kernel,
        grid_spec=pltpu.PrefetchScalarGridSpec(
            num_scalar_prefetch=1,
            grid=(6,),
            in_specs=[own_spec(kind) for kind in range(6)]
            + [
                rim_spec,
                rim_spec,
                whole((2, D)),
                pl.BlockSpec(
                    (D, 2 * QUAD),
                    lambda c, info: (0, c // 2 * 2 + ((c % 2) ^ (1 - info[1]))),
                ),
                hbm,
                hbm,
            ],
            out_specs=(whole((rows, D)), whole((8, D))),
            scratch_shapes=[
                pltpu.VMEM((rows, 2 * QUAD), BF),
                pltpu.VMEM((rows, D), F32),
                pltpu.VMEM((rows, D), BF),
                pltpu.VMEM((rows, D), F32),
                pltpu.SemaphoreType.DMA((2,)),
            ],
        ),
        out_shape=(
            jax.ShapeDtypeStruct((rows, D), BF),
            jax.ShapeDtypeStruct((8, D), F32),
        ),
        compiler_params=params(),
        cost_estimate=cost(1e6, 1e6),
        name="input_back",
    )(info, *keep, *send, low, high, gains, weight, x, dx1)


def place_kernel(starts, count, info_ref, *refs):
    expand_ref, shrink_ref = refs[-2:]
    slot = info_ref[0]
    for number, start in enumerate(starts):
        for flip in range(count):
            ref = refs[number * count + flip]
            size = ref.shape[1] // 3
            at = (slot ^ flip) * PART + start
            expand_ref[:, pl.ds(pl.multiple_of(at, 128), size)] = ref[:, :size].astype(F32)
            expand_ref[:, pl.ds(pl.multiple_of(FF + at, 128), size)] = ref[
                :, size : 2 * size
            ].astype(F32)
            shrink_ref[pl.ds(pl.multiple_of(at, 128), size), :] = ref[:, 2 * size :].astype(F32).T


def place_call(info, starts, pieces):
    rows = pieces[0][0].shape[0]
    vmem = pl.BlockSpec(memory_space=pltpu.VMEM)
    flat = [piece for chunk in pieces for piece in chunk]
    return pl.pallas_call(
        functools.partial(place_kernel, starts, len(pieces[0])),
        in_specs=[pl.BlockSpec(memory_space=pltpu.SMEM)] + [vmem] * len(flat),
        out_shape=(
            jax.ShapeDtypeStruct((rows, 2 * FF), F32),
            jax.ShapeDtypeStruct((FF, rows), F32),
        ),
        compiler_params=params(),
        cost_estimate=cost(1e6, 10e6),
        name="place_feed",
    )(info, *flat)


def place_attend_kernel(count, info_ref, *refs):
    attend_ref, output_ref = refs[count:]
    slot = info_ref[0]
    for flip in range(count):
        at = (slot ^ flip) * QUAD
        for block in range(4):
            value = refs[flip][block].astype(F32)
            if block == 1:
                output_ref[:, pl.ds(pl.multiple_of(at, QUAD), QUAD)] = value
            else:
                column = max(block - 1, 0) * D + at
                attend_ref[:, pl.ds(pl.multiple_of(column, QUAD), QUAD)] = value


def place_attend_call(info, pieces):
    rows = pieces[0].shape[1]
    vmem = pl.BlockSpec(memory_space=pltpu.VMEM)
    return pl.pallas_call(
        functools.partial(place_attend_kernel, len(pieces)),
        in_specs=[pl.BlockSpec(memory_space=pltpu.SMEM)] + [vmem] * len(pieces),
        out_shape=(
            jax.ShapeDtypeStruct((rows, 3 * D), F32),
            jax.ShapeDtypeStruct((rows, D), F32),
        ),
        compiler_params=params(),
        cost_estimate=cost(1e6, 4e6),
        name="place_attend",
    )(info, *pieces)


def add_up(terms):
    total = terms[0].astype(F32)
    for term in terms[1:]:
        total = total + term.astype(F32)
    return total


class Links:
    def __init__(self):
        self.dp_size = lax.axis_size("dp")
        self.seq_size = lax.axis_size("seq")
        self.dp = lax.axis_index("dp")
        self.seq = lax.axis_index("seq")
        self.dp_bits = self.dp_size.bit_length() - 1
        self.seq_bits = self.seq_size.bit_length() - 1

    def swap(self, value, *names):
        flips = {"dp": 0, "seq": 0}
        for axis, bit in names:
            flips[axis] ^= 1 << bit
        pairs = []
        for dp in range(self.dp_size):
            for seq in range(self.seq_size):
                target = (dp ^ flips["dp"]) * self.seq_size + (seq ^ flips["seq"])
                pairs.append((dp * self.seq_size + seq, target))
        return lax.ppermute(value, ("dp", "seq"), pairs)

    def bit(self, name):
        return ((self.dp if name[0] == "dp" else self.seq) >> name[1]) & 1


CORE = ("seq", 0)
X = ("seq", 1)
Y = ("dp", 0)
Z = ("dp", 1)
Q = ("dp", 2)


def pick(value, dim, index):
    return lax.dynamic_index_in_dim(value, index, dim, keepdims=False)


def halve_flow(links, sets, names, order):
    for name in order:
        dim = 1 + names.index(name)
        mine = links.bit(name)
        other = [add_up([pick(term, dim, 1 - mine) for term in terms]) for terms in sets]
        other = other[0] if len(other) == 1 else jnp.concatenate(other, axis=0)
        got = yield links.swap(other.astype(BF), name)
        sets = [[pick(term, dim, mine) for term in terms] for terms in sets]
        first = 0
        for terms in sets:
            count = terms[0].shape[0]
            terms.append(got[first : first + count])
            first += count
        names = names[: dim - 1] + names[dim:]
    return sets


def total_flow(links, sets):
    total = [add_up(terms) for terms in sets]
    total = total[0] if len(total) == 1 else jnp.concatenate(total, axis=0)
    for bit in range(2, links.seq_bits):
        got = yield links.swap(total.astype(BF), ("seq", bit))
        total = total + got.astype(F32)
    return total.astype(BF)


def attend_flow(links, sets, names, order):
    sets = yield from halve_flow(links, sets, names, order)
    total = yield from total_flow(links, sets)
    near, across = yield (links.swap(total, CORE), links.swap(total, X))
    far = yield links.swap(across, CORE)
    return [total, near, across, far]


def pair_flow(links, send, keep, rows):
    got = yield links.swap(send, Y)
    shape = (1,) + (2,) * (links.dp_bits - 1) + (rows, keep.shape[-1])
    names = [("dp", bit) for bit in range(links.dp_bits - 1, 0, -1)]
    order = [("dp", bit) for bit in range(2, links.dp_bits)]
    sets = [[keep.reshape(shape), got.reshape(shape)]]
    return (yield from halve_flow(links, sets, names, order))


def back_flow(links, send, keep, rows):
    got = yield links.swap(send, Q)
    shape = (1,) + (2,) * (links.dp_bits - 1) + (rows, keep.shape[-1])
    names = [("dp", bit) for bit in range(links.dp_bits - 1, -1, -1) if bit != 2]
    order = [Y] + [("dp", bit) for bit in range(3, links.dp_bits)]
    sets = [[keep.reshape(shape), got.reshape(shape)]]
    return (yield from halve_flow(links, sets, names, order))


def spread_flow(links, parts):
    total = jnp.concatenate([add_up([term[0] for term in terms]) for terms in parts], axis=-1)
    for bit in range(2, links.seq_bits):
        got = yield links.swap(total.astype(BF), ("seq", bit))
        total = total + got.astype(F32)
    mine = links.bit(Z)
    own, other = pick(total, 0, mine).astype(BF), pick(total, 0, 1 - mine).astype(BF)
    over_x, over_z, over_both = yield (
        links.swap(own, X),
        links.swap(other, Z),
        links.swap(other, X, Z),
    )
    near = [own, over_x, over_z, over_both]
    far = yield tuple(links.swap(piece, CORE) for piece in near)
    return [(far if flip & 1 else near)[flip >> 1] for flip in range(8)]


def qo_flow(links, send, keep, rows):
    got = yield links.swap(send, X)
    shape = (2,) + (2,) * links.dp_bits + (rows, QUAD)
    names = [("dp", bit) for bit in range(links.dp_bits - 1, -1, -1)]
    sets = [[keep.reshape(shape), got.reshape(shape)]]
    return (yield from halve_flow(links, sets, names, [Z]))


def kv_flow(links, send, keep, rows):
    got = yield links.swap(send, Z)
    terms = [keep, got]
    got = yield links.swap(add_up([term[:, 0] for term in terms]).astype(BF), X)
    terms = [term[:, 1] for term in terms] + [got]
    shape = (2,) + (2,) * (links.dp_bits - 1) + (rows, QUAD)
    return [[term.reshape(shape) for term in terms]]


def gather_flow(links, value):
    half = value.shape[0] // 2
    over_x, over_z, far = yield (
        links.swap(value, X),
        links.swap(value, Z),
        links.swap(value, CORE),
    )
    top = links.swap(over_x[:half], Z)
    bottom = links.swap(over_z[half:], X)
    rest = [links.swap(piece, CORE) for piece in (over_x, over_z)]
    top, bottom, *rest = yield (top, bottom, *rest)
    last = yield tuple(links.swap(piece, CORE) for piece in (top, bottom))
    return [value, over_x, over_z, top, bottom, far, *rest, *last]


def small_flow(links, value):
    groups = [(CORE, X), (Y, Z)]
    groups += [(("seq", bit),) for bit in range(2, links.seq_bits)]
    groups += [(("dp", bit),) for bit in range(2, links.dp_bits)]
    for group in groups:
        flips = [group] if len(group) == 1 else [group[:1], group[1:], group]
        arrived = yield tuple(links.swap(value, *flip) for flip in flips)
        value = value + sum(arrived[1:], arrived[0])
    return value


class Flow:
    def __init__(self, generator):
        self.generator = generator
        self.result = None
        self.waiting = next(generator)

    def resume(self, arrived):
        try:
            self.waiting = self.generator.send(arrived)
        except StopIteration as stop:
            self.waiting = None
            self.result = stop.value


class Fences:
    def __init__(self, token):
        self.token = token

    def __call__(self, flows, values=()):
        flows = [flow for flow in flows if flow.waiting is not None]
        self.token, arrived, values = lax.optimization_barrier(
            (self.token, [flow.waiting for flow in flows], tuple(values))
        )
        for flow, waiting in zip(flows, arrived):
            flow.resume(waiting)
        return values


def body(
    frames,
    cotangent,
    lengths,
    attend_weight,
    output_weight,
    expand_weight,
    shrink_weight,
    norm_gains,
    norm_biases,
    layer_scales,
):
    rows = frames.shape[1]
    links = Links()
    x = frames.reshape(rows, D)
    dy = cotangent.reshape(rows, D)
    member = links.seq & 3
    slot = links.bit(Z) * 4 + member
    block_rows = D // links.dp_size
    fence = Fences(lengths)

    def shifted(value, steps):
        count = links.seq_size
        pairs = [(i, i + steps) for i in range(count) if 0 <= i + steps < count]
        return lax.ppermute(value, "seq", pairs)

    def shift_flow(low_edge, high_edge):
        pair = yield (shifted(high_edge, 1), shifted(low_edge, -1))
        return pair

    dy_flow = Flow(gather_flow(links, dy))
    frames_rim = Flow(shift_flow(x[:WINDOW], x[rows - WINDOW :]))
    table_info = jnp.stack([links.seq, jnp.int32(links.seq_size * rows)]).astype(jnp.int32)
    cosine, sine, bias = tables_call(table_info, lengths, rows)
    a1, qkv = project_call(x, norm_gains, norm_biases, cosine, sine, attend_weight)
    (qkv,) = fence([frames_rim], (qkv,))
    low_frames, high_frames = frames_rim.result
    a1_rim, rim = rim_call(
        low_frames, high_frames, norm_gains, norm_biases, cosine, sine, attend_weight
    )
    (rim,) = fence([dy_flow], (rim,))
    o, lse, x1, attn, a2 = attend_call(
        qkv, rim, bias, output_weight, x, norm_gains, norm_biases, layer_scales
    )
    (a2, x1) = fence([dy_flow], (a2, x1))
    a2_flow = Flow(gather_flow(links, a2))
    act, dx1, dattn, small_feed = feed_call(
        a2, dy, x1, attn, norm_gains, layer_scales, expand_weight, shrink_weight
    )
    (dattn,) = fence([dy_flow, a2_flow], (dattn,))

    core = links.bit(CORE)
    rest_names = [("dp", bit) for bit in range(links.dp_bits - 1, -1, -1) if bit != 1]
    rest_order = rest_names[::-1]

    def heads_back(bit, grad_attn, *got):
        info = jnp.stack([bit, links.bit(X), links.bit(Z)]).astype(jnp.int32)
        return attend_back_call(
            info,
            qkv,
            rim,
            bias,
            cosine,
            sine,
            lse,
            grad_attn,
            output_weight,
            a1,
            a1_rim,
            o,
            block_rows,
            *got,
        )

    def core_flow(send):
        got = yield links.swap(send, CORE)
        return got

    *send_back, send_low, send_high, grad_send = heads_back(1 - core, dattn)
    grad_send, dattn = fence([a2_flow], (grad_send, dattn))
    (dattn, grad_send) = fence([a2_flow], (dattn, grad_send))
    grad_flow = Flow(core_flow(grad_send))
    slice_info = jnp.stack([slot, links.bit(Y), links.bit(Q)]).astype(jnp.int32)
    slice_info, dattn = lax.optimization_barrier((slice_info, dattn))
    pair_send, pair_keep, back_send, back_keep = slice_call(
        slice_info,
        a2_flow.result,
        dy_flow.result,
        layer_scales,
        expand_weight,
        shrink_weight,
        rows,
        block_rows,
    )
    pair_send, back_send, dattn = fence([grad_flow], (pair_send, back_send, dattn))
    pair = Flow(pair_flow(links, pair_send, pair_keep, block_rows))
    back = Flow(back_flow(links, back_send, back_keep, block_rows))
    *keep_back, keep_low, keep_high, qo_send, qo_keep, kv_send, kv_keep = heads_back(
        core, dattn, grad_flow.result
    )
    qo_send, kv_send, keep_low, keep_high = fence(
        [pair, back], (qo_send, kv_send, keep_low, keep_high)
    )
    queries_out = Flow(qo_flow(links, qo_send, qo_keep, block_rows))
    keys_values = Flow(kv_flow(links, kv_send, kv_keep, block_rows))
    rim_flow = Flow(
        shift_flow(jnp.stack([keep_low, send_low]), jnp.stack([keep_high, send_high]))
    )
    (dx1,) = fence([rim_flow, queries_out, keys_values], (dx1,))
    from_low, from_high = rim_flow.result
    input_info = jnp.stack([core, links.bit(X)]).astype(jnp.int32)
    input_gradient, small_first = input_back_call(
        input_info,
        keep_back,
        send_back,
        from_low,
        from_high,
        x,
        dx1,
        norm_gains,
        attend_weight,
    )
    (small_first,) = fence([queries_out, keys_values], (small_first,))
    small = jnp.concatenate([small_feed[:4], small_first[:2], jnp.zeros((2, D), F32)], axis=0)
    small = Flow(small_flow(links, small))
    attends = Flow(
        attend_flow(links, queries_out.result + keys_values.result, rest_names, rest_order)
    )
    while pair.waiting is not None or back.waiting is not None:
        fence([pair, back])
    spread = Flow(spread_flow(links, pair.result + back.result))
    fence([attends, small])
    fence([spread])
    while attends.waiting is not None or spread.waiting is not None or small.waiting is not None:
        fence([attends, small, spread])
    member_info = member.reshape(1).astype(jnp.int32)
    attend_grad, output_grad = place_attend_call(member_info, attends.result)
    expand_grad, shrink_grad = place_call(
        slot.reshape(1).astype(jnp.int32), (0,), [spread.result]
    )
    small = lax.dynamic_slice_in_dim(small.result, links.dp * block_rows, block_rows, axis=1)
    gains_grad = jnp.stack([small[4], small[1]])
    biases_grad = jnp.stack([small[5], small[2]])
    scales_grad = jnp.stack([small[3], small[0]])
    return (
        act.reshape(frames.shape),
        input_gradient.reshape(frames.shape),
        attend_grad,
        output_grad,
        expand_grad,
        shrink_grad,
        gains_grad,
        biases_grad,
        scales_grad,
    )


def solution(mesh):
    in_specs = (
        P("dp", "seq", None),
        P("dp", "seq", None),
        P("dp", None),
        P(),
        P(),
        P(),
        P(),
        P(),
        P(),
        P(),
    )
    out_specs = (
        P("dp", "seq", None),
        P("dp", "seq", None),
        P("dp", None),
        P("dp", None),
        P("dp", None),
        P(None, "dp"),
        P(None, "dp"),
        P(None, "dp"),
        P(None, "dp"),
    )
    return jax.shard_map(body, mesh=mesh, in_specs=in_specs, out_specs=out_specs, check_vma=False)
```

```python
import functools
import math

import jax
import jax.numpy as jnp
from jax import lax
from jax.experimental import pallas as pl
from jax.experimental.pallas import tpu as pltpu
from jax.sharding import PartitionSpec as P

D = 1024
HEADS = 16
HEAD_DIM = 64
FF = 4096
WINDOW = 128
QUAD = 4 * HEAD_DIM
SLICES = 8
PART = FF // SLICES
HALF = PART // 2
EPS = 1e-05
BF = jnp.bfloat16
F32 = jnp.float32
VMEM_BYTES = 58 * 1024 * 1024


def dot_nn(a, b):
    return lax.dot_general(a, b, (((1,), (0,)), ((), ())), preferred_element_type=F32)


def dot_nt(a, b):
    return lax.dot_general(a, b, (((1,), (1,)), ((), ())), preferred_element_type=F32)


def dot_tn(a, b):
    return lax.dot_general(a, b, (((0,), (0,)), ((), ())), preferred_element_type=F32)


def params(**extra):
    return pltpu.CompilerParams(vmem_limit_bytes=VMEM_BYTES, **extra)


def cost(flops, size, transcendentals=0):
    return pl.CostEstimate(
        flops=int(flops), bytes_accessed=int(size), transcendentals=int(transcendentals)
    )


def whole(shape):
    return pl.BlockSpec(shape, lambda *_: (0,) * len(shape))


def norm_stats(values):
    centered = values - jnp.mean(values, axis=-1, keepdims=True)
    inverse = lax.rsqrt(jnp.mean(centered * centered, axis=-1, keepdims=True) + EPS)
    return (centered * inverse, inverse)


def norm_back(gradient, normed, inverse, gain_row):
    scaled = gradient * gain_row
    return inverse * (
        scaled
        - jnp.mean(scaled, axis=-1, keepdims=True)
        - normed * jnp.mean(scaled * normed, axis=-1, keepdims=True)
    )


def turn(values, cosine, sine, sign):
    lane = lax.broadcasted_iota(jnp.int32, (values.shape[0], 128), 1) % HEAD_DIM
    parts = []
    for group in range(values.shape[1] // 128):
        part = values[:, group * 128 : group * 128 + 128]
        swapped = jnp.where(
            lane < HEAD_DIM // 2, pltpu.roll(part, 96, 1), pltpu.roll(part, 32, 1)
        )
        if sign > 0:
            parts.append(part * cosine + swapped * sine)
        else:
            parts.append(part * cosine - swapped * sine)
    return jnp.concatenate(parts, axis=1)


def tables_kernel(info_ref, lengths_ref, cos_ref, sin_ref, bias_ref):
    wide = cos_ref.shape[0]
    rows = wide - 2 * WINDOW
    base = info_ref[0] * rows
    total = info_ref[1]
    frame = base - WINDOW + lax.broadcasted_iota(jnp.int32, (8, wide), 1)

    def step(entry, carry):
        start, clip, begin = carry
        inside = frame >= start
        clip = clip + inside.astype(jnp.int32)
        begin = jnp.where(inside, start, begin)
        return (start + lengths_ref[0, entry], clip, begin)

    _, clip, begin = lax.fori_loop(
        0,
        lengths_ref.shape[1],
        step,
        (jnp.int32(0), jnp.full((8, wide), -1, jnp.int32), jnp.zeros((8, wide), jnp.int32)),
    )
    query_clip = clip[0:1, WINDOW : WINDOW + rows].astype(F32)
    clip = jnp.where((frame >= 0) & (frame < total), clip, -1).astype(F32)
    place = (frame - begin).astype(F32)
    key_clip = jnp.broadcast_to(clip[0:1, :], (128, wide)).T
    half = HEAD_DIM // 2
    pack = 128 // half
    part = wide // pack
    packed = jnp.concatenate(
        [
            jnp.broadcast_to(place[0:1, at * part : at * part + part], (half, part))
            for at in range(pack)
        ],
        axis=0,
    ).T
    lane = lax.broadcasted_iota(jnp.int32, (part, 128), 1)
    frequency = jnp.exp((lane % half).astype(F32) * (-2.0 * math.log(10000.0) / HEAD_DIM))
    angle = packed * frequency
    sine, cosine = jnp.sin(angle), jnp.cos(angle)
    sign = jnp.where(lane % HEAD_DIM < half, -1.0, 1.0)
    for at in range(pack):
        for source, target, factor in ((cosine, cos_ref, None), (sine, sin_ref, sign)):
            value = pltpu.roll(source, (128 - at * half) % 128, 1) if at else source
            value = jnp.where(lane < half, value, 0.0)
            value = value + pltpu.roll(value, half, 1)
            value = value + pltpu.roll(value, 2 * half, 1)
            target[at * part : at * part + part, :] = value if factor is None else value * factor
    span = 3 * WINDOW
    gap = lax.broadcasted_iota(jnp.int32, (span, 128), 0) - lax.broadcasted_iota(
        jnp.int32, (span, 128), 1
    )
    near = (gap >= 0) & (gap <= 2 * WINDOW)
    for block in range(rows // WINDOW):
        at = block * WINDOW
        same = key_clip[at : at + span] == query_clip[:, at : at + WINDOW]
        bias_ref[block] = jnp.where(near & same, 0.0, -1e30)


def tables_call(info, lengths, rows):
    wide = rows + 2 * WINDOW
    return pl.pallas_call(
        tables_kernel,
        out_shape=(
            jax.ShapeDtypeStruct((wide, 128), F32),
            jax.ShapeDtypeStruct((wide, 128), F32),
            jax.ShapeDtypeStruct((rows // WINDOW, 3 * WINDOW, 128), F32),
        ),
        in_specs=[
            pl.BlockSpec(memory_space=pltpu.SMEM),
            pl.BlockSpec(memory_space=pltpu.SMEM),
        ],
        compiler_params=params(),
        cost_estimate=cost(1e8, 2e6),
        name="tables",
    )(info, lengths)


def project_kernel(x_ref, gain_ref, shift_ref, cos_ref, sin_ref, weight_ref, a1_ref, out_ref):
    chunk = pl.program_id(0)
    rows = x_ref.shape[0]

    @pl.when(chunk == 0)
    def _():
        normed, _unused = norm_stats(x_ref[...].astype(F32))
        a1_ref[...] = (normed * gain_ref[0:1, :] + shift_ref[0:1, :]).astype(BF)

    projected = dot_nn(a1_ref[...], weight_ref[...])
    cosine = cos_ref[WINDOW : WINDOW + rows, :]
    sine = sin_ref[WINDOW : WINDOW + rows, :]

    @pl.when(chunk == 0)
    def _():
        out_ref[...] = (turn(projected, cosine, sine, 1) * HEAD_DIM**-0.5).astype(BF)

    @pl.when(chunk == 1)
    def _():
        out_ref[...] = turn(projected, cosine, sine, 1).astype(BF)

    @pl.when(chunk == 2)
    def _():
        out_ref[...] = projected.astype(BF)


def project_call(x, gains, shifts, cosine, sine, weight):
    rows = x.shape[0]
    wide = cosine.shape[0]
    return pl.pallas_call(
        project_kernel,
        grid=(3,),
        out_shape=(
            jax.ShapeDtypeStruct((rows, D), BF),
            jax.ShapeDtypeStruct((rows, 3 * D), BF),
        ),
        in_specs=[
            whole((rows, D)),
            whole((2, D)),
            whole((2, D)),
            whole((wide, 128)),
            whole((wide, 128)),
            pl.BlockSpec((D, D), lambda c: (0, c)),
        ],
        out_specs=(whole((rows, D)), pl.BlockSpec((rows, D), lambda c: (0, c))),
        compiler_params=params(),
        cost_estimate=cost(2 * rows * D * 3 * D, 12e6),
        name="project",
    )(x, gains, shifts, cosine, sine, weight)


def rim_kernel(
    low_ref, high_ref, gain_ref, shift_ref, cos_ref, sin_ref, weight_ref, a1_ref, out_ref
):
    chunk = pl.program_id(0)
    wide = cos_ref.shape[0]

    @pl.when(chunk == 0)
    def _():
        for at, ref in ((0, low_ref), (WINDOW, high_ref)):
            normed, _unused = norm_stats(ref[...].astype(F32))
            a1_ref[at : at + WINDOW, :] = (
                normed * gain_ref[0:1, :] + shift_ref[0:1, :]
            ).astype(BF)

    projected = dot_nn(a1_ref[...], weight_ref[...])

    @pl.when(chunk == 0)
    def _():
        cosine = jnp.concatenate([cos_ref[:WINDOW, :], cos_ref[wide - WINDOW :, :]], axis=0)
        sine = jnp.concatenate([sin_ref[:WINDOW, :], sin_ref[wide - WINDOW :, :]], axis=0)
        out_ref[...] = turn(projected, cosine, sine, 1).astype(BF)

    @pl.when(chunk == 1)
    def _():
        out_ref[...] = projected.astype(BF)


def rim_call(low, high, gains, shifts, cosine, sine, weight):
    wide = cosine.shape[0]
    return pl.pallas_call(
        rim_kernel,
        grid=(2,),
        out_shape=(
            jax.ShapeDtypeStruct((2 * WINDOW, D), BF),
            jax.ShapeDtypeStruct((2 * WINDOW, 2 * D), BF),
        ),
        in_specs=[
            whole((WINDOW, D)),
            whole((WINDOW, D)),
            whole((2, D)),
            whole((2, D)),
            whole((wide, 128)),
            whole((wide, 128)),
            pl.BlockSpec((D, D), lambda c: (0, c + 1)),
        ],
        out_specs=(whole((2 * WINDOW, D)), pl.BlockSpec((2 * WINDOW, D), lambda c: (0, c))),
        compiler_params=params(),
        cost_estimate=cost(2 * 256 * D * 2 * D, 6e6),
        name="rim",
    )(low, high, gains, shifts, cosine, sine, weight)


def stacked(block):
    owner = lax.broadcasted_iota(jnp.int32, block.shape, 1) // HEAD_DIM
    zero = jnp.zeros_like(block)
    return jnp.concatenate([jnp.where(owner == head, block, zero) for head in range(4)], axis=0)


def own_lanes(block):
    rows = block.shape[0] // 4
    owner = lax.broadcasted_iota(jnp.int32, (rows, QUAD), 1) // HEAD_DIM
    total = block[:rows]
    for head in range(1, 4):
        total = jnp.where(owner == head, block[head * rows : head * rows + rows], total)
    return total


def attend_kernel(
    q_ref,
    k_ref,
    v_ref,
    rim_k_ref,
    rim_v_ref,
    bias_ref,
    weight_ref,
    x_ref,
    gain_ref,
    shift_ref,
    scale_ref,
    o_ref,
    lse_ref,
    x1_ref,
    attn_ref,
    a2_ref,
    keys,
    values,
    mixed_all,
    total,
):
    quad = pl.program_id(0)
    rows = q_ref.shape[0]
    keys[0:WINDOW, :] = rim_k_ref[0:WINDOW, :]
    keys[WINDOW : WINDOW + rows, :] = k_ref[...]
    keys[WINDOW + rows :, :] = rim_k_ref[WINDOW:, :]
    values[0:WINDOW, :] = rim_v_ref[0:WINDOW, :]
    values[WINDOW : WINDOW + rows, :] = v_ref[...]
    values[WINDOW + rows :, :] = rim_v_ref[WINDOW:, :]
    for block in range(rows // WINDOW):
        at = block * WINDOW
        queries = stacked(q_ref[at : at + WINDOW, :])
        scores = dot_nt(keys[at : at + 3 * WINDOW, :], queries)
        bias = bias_ref[block]
        scores = scores + jnp.concatenate([bias] * 4, axis=1)
        top = jnp.max(scores, axis=0, keepdims=True)
        weights = jnp.exp(scores - top)
        total_row = jnp.sum(weights, axis=0, keepdims=True)
        weights = (weights * (1.0 / total_row)).astype(BF)
        log_row = top + jnp.log(total_row)
        for head in range(4):
            lanes = slice(head * WINDOW, head * WINDOW + WINDOW)
            lse_ref[0, head : head + 1, at : at + WINDOW] = log_row[:, lanes]
        mixed_all[at : at + WINDOW, :] = own_lanes(
            dot_tn(weights, values[at : at + 3 * WINDOW, :])
        ).astype(BF)
    mixed = mixed_all[...]
    o_ref[...] = mixed
    branch = dot_nn(mixed, weight_ref[...])

    @pl.when(quad == 0)
    def _():
        total[...] = branch

    @pl.when(quad > 0)
    def _():
        total[...] += branch

    @pl.when(quad == HEADS // 4 - 1)
    def _():
        attn = total[...]
        residual = x_ref[...].astype(F32) + attn * scale_ref[0:1, :]
        normed, _unused = norm_stats(residual)
        x1_ref[...] = residual
        attn_ref[...] = attn.astype(BF)
        a2_ref[...] = (normed * gain_ref[1:2, :] + shift_ref[1:2, :]).astype(BF)


def attend_call(qkv, rim, bias, weight, x, gains, shifts, scales):
    rows = x.shape[0]
    wide = rows + 2 * WINDOW
    row_spec = whole((rows, D))
    return pl.pallas_call(
        attend_kernel,
        grid=(HEADS // 4,),
        out_shape=(
            jax.ShapeDtypeStruct((rows, D), BF),
            jax.ShapeDtypeStruct((HEADS // 4, 8, rows), F32),
            jax.ShapeDtypeStruct((rows, D), F32),
            jax.ShapeDtypeStruct((rows, D), BF),
            jax.ShapeDtypeStruct((rows, D), BF),
        ),
        in_specs=[
            pl.BlockSpec((rows, QUAD), lambda h: (0, h)),
            pl.BlockSpec((rows, QUAD), lambda h: (0, h + 4)),
            pl.BlockSpec((rows, QUAD), lambda h: (0, h + 8)),
            pl.BlockSpec((2 * WINDOW, QUAD), lambda h: (0, h)),
            pl.BlockSpec((2 * WINDOW, QUAD), lambda h: (0, h + 4)),
            whole(bias.shape),
            pl.BlockSpec((QUAD, D), lambda h: (h, 0)),
            row_spec,
            whole((2, D)),
            whole((2, D)),
            whole((2, D)),
        ],
        out_specs=(
            pl.BlockSpec((rows, QUAD), lambda h: (0, h)),
            pl.BlockSpec((1, 8, rows), lambda h: (h, 0, 0)),
            row_spec,
            row_spec,
            row_spec,
        ),
        scratch_shapes=[
            pltpu.VMEM((wide, QUAD), BF),
            pltpu.VMEM((wide, QUAD), BF),
            pltpu.VMEM((rows, QUAD), BF),
            pltpu.VMEM((rows, D), F32),
        ],
        compiler_params=params(),
        cost_estimate=cost(8e9, 14e6, 3e6),
        name="attend",
    )(qkv, qkv, qkv, rim, rim, bias, weight, x, gains, shifts, scales)


def gated(gate, up, grad_hidden):
    sigmoid = 0.5 * jnp.tanh(0.5 * gate) + 0.5
    swish = gate * sigmoid
    hidden = swish * up
    grad_gate = grad_hidden * up * (sigmoid + swish * (1.0 - sigmoid))
    grad_up = grad_hidden * swish
    return (hidden.astype(BF), grad_gate.astype(BF), grad_up.astype(BF))


def feed_kernel(
    a2_ref,
    dy_ref,
    gain_ref,
    scale_ref,
    x1_hbm,
    attn_hbm,
    expand_hbm,
    shrink_hbm,
    act_hbm,
    dx1_ref,
    dattn_ref,
    small_ref,
    expand,
    shrink,
    hidden,
    grads,
    x1,
    attn,
    act,
    sems,
    late_sems,
):
    width = 512
    step = 256
    groups = FF // width
    copies = []
    for group in range(groups):
        at = group * width
        copies.append(
            [
                pltpu.make_async_copy(
                    expand_hbm.at[:, pl.ds(at, width)],
                    expand.at[:, pl.ds(at, width)],
                    sems.at[group, 0],
                ),
                pltpu.make_async_copy(
                    expand_hbm.at[:, pl.ds(FF + at, width)],
                    expand.at[:, pl.ds(FF + at, width)],
                    sems.at[group, 1],
                ),
                pltpu.make_async_copy(
                    shrink_hbm.at[pl.ds(at, width), :],
                    shrink.at[pl.ds(at, width), :],
                    sems.at[group, 2],
                ),
            ]
        )
    late = [
        pltpu.make_async_copy(x1_hbm, x1, late_sems.at[0]),
        pltpu.make_async_copy(attn_hbm, attn, late_sems.at[1]),
    ]
    ahead = 3
    for group in range(ahead):
        for copy in copies[group]:
            copy.start()
    branch_grad = (dy_ref[...].astype(F32) * scale_ref[1:2, :]).astype(BF)
    a2 = a2_ref[...]

    for chunk in range(FF // step):
        at = chunk * step
        if at % width == 0:
            group = at // width
            if group + ahead < groups:
                for copy in copies[group + ahead]:
                    copy.start()
            elif group + ahead == groups:
                for copy in late:
                    copy.start()
            for copy in copies[group]:
                copy.wait()
        gate = dot_nn(a2, expand[:, at : at + step])
        up = dot_nn(a2, expand[:, FF + at : FF + at + step])
        grad_hidden = dot_nt(branch_grad, shrink[at : at + step, :])
        out, grad_gate, grad_up = gated(gate, up, grad_hidden)
        hidden[:, at : at + step] = out
        grads[:, at : at + step] = grad_gate
        grads[:, FF + at : FF + at + step] = grad_up
    branch = dot_nn(hidden[...], shrink[...])
    for copy in late:
        copy.wait()
    residual = x1[...]
    grad_result = dy_ref[...].astype(F32)
    act[...] = (residual + branch * scale_ref[1:2, :]).astype(BF)
    out_copy = pltpu.make_async_copy(act, act_hbm, late_sems.at[2])
    out_copy.start()
    small_ref[0:1, :] = jnp.sum(grad_result * branch, axis=0, keepdims=True)
    grad_normed = dot_nt(grads[...], expand[...])
    normed, inverse = norm_stats(residual)
    small_ref[1:2, :] = jnp.sum(grad_normed * normed, axis=0, keepdims=True)
    small_ref[2:3, :] = jnp.sum(grad_normed, axis=0, keepdims=True)
    grad_residual = grad_result + norm_back(grad_normed, normed, inverse, gain_ref[1:2, :])
    dx1_ref[...] = grad_residual
    small_ref[3:4, :] = jnp.sum(grad_residual * attn[...].astype(F32), axis=0, keepdims=True)
    small_ref[4:8, :] = jnp.zeros((4, D), F32)
    dattn_ref[...] = (grad_residual * scale_ref[0:1, :]).astype(BF)
    out_copy.wait()


def feed_call(a2, dy, x1, attn, gains, scales, expand, shrink):
    rows = a2.shape[0]
    vmem = pl.BlockSpec(memory_space=pltpu.VMEM)
    hbm = pl.BlockSpec(memory_space=pl.ANY)
    return pl.pallas_call(
        feed_kernel,
        out_shape=(
            jax.ShapeDtypeStruct((rows, D), BF),
            jax.ShapeDtypeStruct((rows, D), F32),
            jax.ShapeDtypeStruct((rows, D), BF),
            jax.ShapeDtypeStruct((8, D), F32),
        ),
        in_specs=[vmem] * 4 + [hbm] * 4,
        out_specs=(hbm, vmem, vmem, vmem),
        scratch_shapes=[
            pltpu.VMEM((D, 2 * FF), BF),
            pltpu.VMEM((FF, D), BF),
            pltpu.VMEM((rows, FF), BF),
            pltpu.VMEM((rows, 2 * FF), BF),
            pltpu.VMEM((rows, D), F32),
            pltpu.VMEM((rows, D), BF),
            pltpu.VMEM((rows, D), BF),
            pltpu.SemaphoreType.DMA((FF // 512, 3)),
            pltpu.SemaphoreType.DMA((3,)),
        ],
        compiler_params=params(),
        cost_estimate=cost(2 * rows * D * FF * 6, 36e6, rows * FF),
        name="feed",
    )(a2, dy, gains, scales, x1, attn, expand, shrink)


def slice_kernel(pieces, info_ref, *refs):
    a2_refs = refs[: len(pieces)]
    dy_refs = refs[len(pieces) : 2 * len(pieces)]
    scale_ref, gate_w_ref, up_w_ref, shrink_w_ref = refs[2 * len(pieces) : 2 * len(pieces) + 4]
    pair_send, pair_keep, back_send, back_keep = refs[2 * len(pieces) + 4 :][:4]
    a2_all, dm_all, inner, result, sems = refs[2 * len(pieces) + 8 :]
    size = gate_w_ref.shape[1]
    groups = 1 + max(slot for slot, _, _ in pieces)
    rows = a2_all.shape[0] // groups
    copies = [[] for _ in range(groups)]
    for number, (slot, first, count) in enumerate(pieces):
        for kind, (sources, held) in enumerate(((a2_refs, a2_all), (dy_refs, dm_all))):
            copies[slot].append(
                pltpu.make_async_copy(
                    sources[number],
                    held.at[pl.ds(slot * rows + first, count), :],
                    sems.at[kind, number],
                )
            )
    for slot in range(min(2, groups)):
        for copy in copies[slot]:
            copy.start()
    scale = scale_ref[1:2, :]
    for slot in range(groups):
        if slot + 2 < groups:
            for copy in copies[slot + 2]:
                copy.start()
        for copy in copies[slot]:
            copy.wait()
        span = slice(slot * rows, slot * rows + rows)
        branch_grad = (dm_all[span, :].astype(F32) * scale).astype(BF)
        dm_all[span, :] = branch_grad
        gate = dot_nn(a2_all[span, :], gate_w_ref[...])
        up = dot_nn(a2_all[span, :], up_w_ref[...])
        grad_hidden = dot_nt(branch_grad, shrink_w_ref[...])
        hidden, grad_gate, grad_up = gated(gate, up, grad_hidden)
        inner[span, :size] = grad_gate
        inner[span, size : 2 * size] = grad_up
        inner[span, 2 * size :] = hidden
    result[:, : 2 * size] = dot_tn(a2_all[...], inner[:, : 2 * size]).astype(BF)
    result[:, 2 * size :] = dot_tn(dm_all[...], inner[:, 2 * size :]).astype(BF)
    columns = (slice(0, 2 * size), slice(2 * size, 3 * size))
    for lanes, mine, send_ref, keep_ref in (
        (columns[0], info_ref[1], pair_send, pair_keep),
        (columns[1], info_ref[2], back_send, back_keep),
    ):
        outer, span, _ = send_ref.shape
        for at in range(outer):
            for target, bit in ((send_ref, 1 - mine), (keep_ref, mine)):
                first = pl.multiple_of(at * 2 * span + bit * span, span)
                target[at] = result[pl.ds(first, span), lanes]


def slice_call(info, a2_list, dy_list, scales, expand, shrink, rows, block_rows):
    size = PART
    pieces = []
    slot, first = 0, 0
    for piece in a2_list:
        pieces.append((slot, first, piece.shape[0]))
        first += piece.shape[0]
        if first == rows:
            slot, first = slot + 1, 0
    groups = slot
    hbm = pl.BlockSpec(memory_space=pl.ANY)
    pair_shape = (D // (2 * block_rows), block_rows, 2 * size)
    back_shape = (D // (8 * block_rows), 4 * block_rows, size)
    shapes = (pair_shape, pair_shape, back_shape, back_shape)
    return pl.pallas_call(
        functools.partial(slice_kernel, tuple(pieces)),
        grid_spec=pltpu.PrefetchScalarGridSpec(
            num_scalar_prefetch=1,
            grid=(1,),
            in_specs=[hbm] * (2 * len(pieces))
            + [
                pl.BlockSpec((2, D), lambda i, info: (0, 0)),
                pl.BlockSpec((D, size), lambda i, info: (0, info[0])),
                pl.BlockSpec((D, size), lambda i, info: (0, info[0] + FF // size)),
                pl.BlockSpec((size, D), lambda i, info: (info[0], 0)),
            ],
            out_specs=[pl.BlockSpec(shape, lambda i, info: (0, 0, 0)) for shape in shapes],
            scratch_shapes=[
                pltpu.VMEM((groups * rows, D), BF),
                pltpu.VMEM((groups * rows, D), BF),
                pltpu.VMEM((groups * rows, 3 * size), BF),
                pltpu.VMEM((D, 3 * size), BF),
                pltpu.SemaphoreType.DMA((2, len(pieces))),
            ],
        ),
        out_shape=[jax.ShapeDtypeStruct(shape, BF) for shape in shapes],
        compiler_params=params(),
        cost_estimate=cost(2 * groups * rows * D * size * 6, 22e6, groups * rows * size),
        name="slice_grads",
    )(info, *a2_list, *dy_list, scales, expand, expand, shrink)


def attend_back_kernel(
    last,
    info_ref,
    q_ref,
    k_ref,
    v_ref,
    rim_k_ref,
    rim_v_ref,
    bias_ref,
    cos_ref,
    sin_ref,
    lse_ref,
    dattn_ref,
    dattn_part_ref,
    weight_ref,
    a1_ref,
    a1_rim_ref,
    o_ref,
    *refs,
):
    if last:
        other_low, other_high, *refs = refs
    dq_ref, dk_ref, dv_ref, low_ref, high_ref, *refs = refs
    qo_ref, kv_ref, *refs = refs
    a1, keys, values, keys_t, grad_q_t, grad_k, grad_v = refs
    step = pl.program_id(0)

    def deliver(block, grad):
        if block < 2:
            qo_ref[0, block] = grad.astype(BF)
            return
        kv_ref[0, block - 2] = grad.astype(BF)

    rows = q_ref.shape[0]
    low, own, high = slice(0, WINDOW), slice(WINDOW, WINDOW + rows), slice(WINDOW + rows, None)

    @pl.when(step == 0)
    def _():
        a1[low, :] = a1_rim_ref[:WINDOW, :]
        a1[own, :] = a1_ref[...]
        a1[high, :] = a1_rim_ref[WINDOW:, :]

    for held, mine, rim in ((keys, k_ref, rim_k_ref), (values, v_ref, rim_v_ref)):
        held[low, :] = rim[:WINDOW, :]
        held[own, :] = mine[...]
        held[high, :] = rim[WINDOW:, :]
    keys_t[...] = keys[...].T
    grad_mixed = dot_nt(dattn_ref[...], weight_ref[...]).astype(BF)
    deliver(1, dot_tn(o_ref[...], dattn_part_ref[...]))
    grad_k[...] = jnp.zeros_like(grad_k)
    grad_v[...] = jnp.zeros_like(grad_v)
    for block in range(rows // WINDOW):
        at = block * WINDOW
        span = slice(at, at + 3 * WINDOW)
        queries = stacked(q_ref[at : at + WINDOW, :])
        grad_out = stacked(grad_mixed[at : at + WINDOW, :])
        scores = dot_nt(keys[span, :], queries)
        log_row = jnp.concatenate(
            [lse_ref[0, head : head + 1, at : at + WINDOW] for head in range(4)], axis=1
        )
        bias = bias_ref[block]
        weights = jnp.exp(scores + jnp.concatenate([bias] * 4, axis=1) - log_row)
        grad_weights = dot_nt(values[span, :], grad_out)
        weighted = weights * grad_weights
        grad_scores = weighted - weights * jnp.sum(weighted, axis=0, keepdims=True)
        grad_scores = grad_scores.astype(BF)
        grad_v[span, :] += dot_nn(weights.astype(BF), grad_out)
        grad_k[span, :] += dot_nn(grad_scores, queries)
        for head in range(4):
            feature = slice(head * HEAD_DIM, head * HEAD_DIM + HEAD_DIM)
            grad_q_t[feature, at : at + WINDOW] = dot_nn(
                keys_t[feature, span], grad_scores[:, head * WINDOW : head * WINDOW + WINDOW]
            )
    cosine, sine = cos_ref[...], sin_ref[...]
    grad_q = turn(grad_q_t[...].T * HEAD_DIM**-0.5, cosine[own, :], sine[own, :], -1).astype(BF)
    turned = turn(grad_k[...], cosine, sine, -1).astype(BF)
    grad_values = grad_v[...].astype(BF)
    deliver(0, dot_tn(a1_ref[...], grad_q))
    deliver(2, dot_tn(a1[...], turned))
    deliver(3, dot_tn(a1[...], grad_values))
    dq_ref[0] = grad_q
    dk_ref[0] = turned[own, :]
    dv_ref[0] = grad_values[own, :]
    for target, span in ((low_ref, low), (high_ref, high)):
        target[0, 0, 0] = turned[span, :]
        target[0, 1, 0] = grad_values[span, :]
    if last:
        low_ref[1] = other_low[0]
        high_ref[1] = other_high[0]


def attend_back_call(
    info, qkv, rim, bias, cosine, sine, lse, dattn, weight, a1, a1_rim, o, *other_rims
):
    rows = dattn.shape[0]
    wide = rows + 2 * WINDOW
    last = len(other_rims) > 0
    row_shape = jax.ShapeDtypeStruct((2, rows, QUAD), BF)
    sides = 2 if last else 1
    rim_shape = jax.ShapeDtypeStruct((sides, 2, 2, WINDOW, QUAD), BF)
    row_spec = pl.BlockSpec((1, rows, QUAD), lambda s, info: (s, 0, 0))

    def quad(s, info):
        return 2 * (s ^ (1 - info[1])) + info[0]

    def rim_spec(count):
        return pl.BlockSpec(
            (count, 2, 1, WINDOW, QUAD), lambda s, info: (0, 0, s ^ (1 - info[1]), 0, 0)
        )


    def columns(count, first):
        return pl.BlockSpec((count, QUAD), lambda s, info: (0, first + quad(s, info)))

    kv_shape = jax.ShapeDtypeStruct((2, 2, D, QUAD), BF)
    kv_spec = pl.BlockSpec((1, 2, D, QUAD), lambda s, info: (s, 0, 0, 0))
    operands = [
        info,
        qkv,
        qkv,
        qkv,
        rim,
        rim,
        bias,
        cosine,
        sine,
        lse,
        dattn,
        dattn,
        weight,
        a1,
        a1_rim,
        o,
    ]
    return pl.pallas_call(
        functools.partial(attend_back_kernel, last),
        grid_spec=pltpu.PrefetchScalarGridSpec(
            num_scalar_prefetch=1,
            grid=(2,),
            in_specs=[
                columns(rows, 0),
                columns(rows, 4),
                columns(rows, 8),
                columns(2 * WINDOW, 0),
                columns(2 * WINDOW, 4),
                whole(bias.shape),
                whole((wide, 128)),
                whole((wide, 128)),
                pl.BlockSpec((1, 8, rows), lambda s, info: (quad(s, info), 0, 0)),
                whole((rows, D)),
                columns(rows, 0),
                pl.BlockSpec((QUAD, D), lambda s, info: (quad(s, info), 0)),
                whole((rows, D)),
                whole((2 * WINDOW, D)),
                whole((rows, D)),
            ]
            + [rim_spec(1)] * len(other_rims),
            out_specs=[row_spec] * 3 + [rim_spec(sides)] * 2 + [kv_spec] * 2,
            scratch_shapes=[
                pltpu.VMEM((wide, D), BF),
                pltpu.VMEM((wide, QUAD), BF),
                pltpu.VMEM((wide, QUAD), BF),
                pltpu.VMEM((QUAD, wide), BF),
                pltpu.VMEM((QUAD, rows), F32),
                pltpu.VMEM((wide, QUAD), F32),
                pltpu.VMEM((wide, QUAD), F32),
            ],
        ),
        out_shape=[row_shape] * 3
        + [rim_shape] * 2
        + [kv_shape] * 2,
        compiler_params=params(),
        cost_estimate=cost(1e6, 1e6),
        name="attend_back",
    )(*operands, *other_rims)


def input_back_kernel(
    info_ref,
    keep_q,
    keep_k,
    keep_v,
    send_q,
    send_k,
    send_v,
    low_ref,
    high_ref,
    gain_ref,
    weight_ref,
    x_hbm,
    dx1_hbm,
    grad_ref,
    small_ref,
    part,
    back,
    x,
    dx1,
    sems,
):
    chunk = pl.program_id(0)
    rows = x.shape[0]
    late = [
        pltpu.make_async_copy(x_hbm, x, sems.at[0]),
        pltpu.make_async_copy(dx1_hbm, dx1, sems.at[1]),
    ]

    @pl.when(chunk == 0)
    def _():
        for copy in late:
            copy.start()
        back[...] = jnp.zeros_like(back)

    for kind, pair in enumerate(((keep_q, send_q), (keep_k, send_k), (keep_v, send_v))):

        @pl.when(chunk // 2 == kind)
        def _():
            for core in range(2):

                @pl.when(info_ref[0] == core)
                def _():
                    for at, ref in ((core, pair[0]), (1 - core, pair[1])):
                        lanes = slice(at * QUAD, at * QUAD + QUAD)
                        part[:, lanes] = ref[0]

            if kind > 0:
                for core in range(2):

                    @pl.when(info_ref[0] == core)
                    def _():
                        for at, which in ((core, 1), (1 - core, 0)):
                            lanes = slice(at * QUAD, at * QUAD + QUAD)
                            for first, rim in ((0, low_ref), (rows - WINDOW, high_ref)):
                                span = slice(first, first + WINDOW)
                                part[span, lanes] = (
                                    part[span, lanes].astype(F32)
                                    + rim[which, 0, 0].astype(F32)
                                ).astype(BF)

    back[...] += dot_nt(part[...], weight_ref[...])

    @pl.when(chunk == pl.num_programs(0) - 1)
    def _():
        for copy in late:
            copy.wait()
        grad_normed = back[...]
        normed, inverse = norm_stats(x[...].astype(F32))
        small_ref[0:1, :] = jnp.sum(grad_normed * normed, axis=0, keepdims=True)
        small_ref[1:2, :] = jnp.sum(grad_normed, axis=0, keepdims=True)
        small_ref[2:8, :] = jnp.zeros((6, D), F32)
        grad_ref[...] = (
            dx1[...] + norm_back(grad_normed, normed, inverse, gain_ref[0:1, :])
        ).astype(BF)


def input_back_call(info, keep, send, low, high, x, dx1, gains, weight):
    rows = x.shape[0]

    def own_spec(kind):
        return pl.BlockSpec((1, rows, QUAD), lambda c, info: (c % 2, 0, 0))

    rim_spec = pl.BlockSpec(
        (2, 1, 1, WINDOW, QUAD),
        lambda c, info: (0, jnp.maximum(c // 2 - 1, 0), (c % 2) ^ (1 - info[1]), 0, 0),
    )
    hbm = pl.BlockSpec(memory_space=pl.ANY)
    return pl.pallas_call(
        input_back_kernel,
        grid_spec=pltpu.PrefetchScalarGridSpec(
            num_scalar_prefetch=1,
            grid=(6,),
            in_specs=[own_spec(kind) for kind in range(6)]
            + [
                rim_spec,
                rim_spec,
                whole((2, D)),
                pl.BlockSpec(
                    (D, 2 * QUAD),
                    lambda c, info: (0, c // 2 * 2 + ((c % 2) ^ (1 - info[1]))),
                ),
                hbm,
                hbm,
            ],
            out_specs=(whole((rows, D)), whole((8, D))),
            scratch_shapes=[
                pltpu.VMEM((rows, 2 * QUAD), BF),
                pltpu.VMEM((rows, D), F32),
                pltpu.VMEM((rows, D), BF),
                pltpu.VMEM((rows, D), F32),
                pltpu.SemaphoreType.DMA((2,)),
            ],
        ),
        out_shape=(
            jax.ShapeDtypeStruct((rows, D), BF),
            jax.ShapeDtypeStruct((8, D), F32),
        ),
        compiler_params=params(),
        cost_estimate=cost(1e6, 1e6),
        name="input_back",
    )(info, *keep, *send, low, high, gains, weight, x, dx1)


def place_kernel(info_ref, near_ref, far_ref, expand_ref, shrink_ref):
    for core, ref in enumerate((near_ref, far_ref)):
        for at in range(4):
            flip = 4 * (at >> 1) + 2 * (at & 1) + core
            first = pl.multiple_of((info_ref[0] ^ flip) * PART, PART)
            expand_ref[:, pl.ds(first, PART)] = ref[at, :, :PART].astype(F32)
            expand_ref[:, pl.ds(pl.multiple_of(FF + first, PART), PART)] = ref[
                at, :, PART : 2 * PART
            ].astype(F32)
            shrink_ref[pl.ds(first, PART), :] = ref[at, :, 2 * PART :].astype(F32).T


def place_call(info, near, far):
    rows = near.shape[1]
    vmem = pl.BlockSpec(memory_space=pltpu.VMEM)
    return pl.pallas_call(
        place_kernel,
        in_specs=[pl.BlockSpec(memory_space=pltpu.SMEM), vmem, vmem],
        out_shape=(
            jax.ShapeDtypeStruct((rows, 2 * FF), F32),
            jax.ShapeDtypeStruct((FF, rows), F32),
        ),
        compiler_params=params(),
        cost_estimate=cost(1e6, 10e6),
        name="place_feed",
    )(info, near, far)


def place_attend_kernel(count, info_ref, *refs):
    attend_ref, output_ref = refs[count:]
    slot = info_ref[0]
    for flip in range(count):
        at = (slot ^ flip) * QUAD
        for block in range(4):
            value = refs[flip][block].astype(F32)
            if block == 1:
                output_ref[:, pl.ds(pl.multiple_of(at, QUAD), QUAD)] = value
            else:
                column = max(block - 1, 0) * D + at
                attend_ref[:, pl.ds(pl.multiple_of(column, QUAD), QUAD)] = value


def place_attend_call(info, pieces):
    rows = pieces[0].shape[1]
    vmem = pl.BlockSpec(memory_space=pltpu.VMEM)
    return pl.pallas_call(
        functools.partial(place_attend_kernel, len(pieces)),
        in_specs=[pl.BlockSpec(memory_space=pltpu.SMEM)] + [vmem] * len(pieces),
        out_shape=(
            jax.ShapeDtypeStruct((rows, 3 * D), F32),
            jax.ShapeDtypeStruct((rows, D), F32),
        ),
        compiler_params=params(),
        cost_estimate=cost(1e6, 4e6),
        name="place_attend",
    )(info, *pieces)


def add_up(terms):
    total = terms[0].astype(F32)
    for term in terms[1:]:
        total = total + term.astype(F32)
    return total


class Links:
    def __init__(self):
        self.dp_size = lax.axis_size("dp")
        self.seq_size = lax.axis_size("seq")
        self.dp = lax.axis_index("dp")
        self.seq = lax.axis_index("seq")
        self.dp_bits = self.dp_size.bit_length() - 1
        self.seq_bits = self.seq_size.bit_length() - 1

    def swap(self, value, *names):
        flips = {"dp": 0, "seq": 0}
        for axis, bit in names:
            flips[axis] ^= 1 << bit
        pairs = []
        for dp in range(self.dp_size):
            for seq in range(self.seq_size):
                target = (dp ^ flips["dp"]) * self.seq_size + (seq ^ flips["seq"])
                pairs.append((dp * self.seq_size + seq, target))
        return lax.ppermute(value, ("dp", "seq"), pairs)

    def bit(self, name):
        return ((self.dp if name[0] == "dp" else self.seq) >> name[1]) & 1


CORE = ("seq", 0)
X = ("seq", 1)
Y = ("dp", 0)
Z = ("dp", 1)
Q = ("dp", 2)


def pick(value, dim, index):
    return lax.dynamic_index_in_dim(value, index, dim, keepdims=False)


def halve_flow(links, sets, names, order):
    for name in order:
        dim = 1 + names.index(name)
        mine = links.bit(name)
        other = [add_up([pick(term, dim, 1 - mine) for term in terms]) for terms in sets]
        other = other[0] if len(other) == 1 else jnp.concatenate(other, axis=0)
        got = yield links.swap(other.astype(BF), name)
        sets = [[pick(term, dim, mine) for term in terms] for terms in sets]
        first = 0
        for terms in sets:
            count = terms[0].shape[0]
            terms.append(got[first : first + count])
            first += count
        names = names[: dim - 1] + names[dim:]
    return sets


def total_flow(links, sets):
    total = [add_up(terms) for terms in sets]
    total = total[0] if len(total) == 1 else jnp.concatenate(total, axis=0)
    for bit in range(2, links.seq_bits):
        got = yield links.swap(total.astype(BF), ("seq", bit))
        total = total + got.astype(F32)
    return total.astype(BF)


def attend_flow(links, sets, names, order):
    sets = yield from halve_flow(links, sets, names, order)
    total = yield from total_flow(links, sets)
    near, across = yield (links.swap(total, CORE), links.swap(total, X))
    far = yield links.swap(across, CORE)
    return [total, near, across, far]


def pair_flow(links, send, keep, rows):
    got = yield links.swap(send, Y)
    shape = (1,) + (2,) * (links.dp_bits - 1) + (rows, keep.shape[-1])
    names = [("dp", bit) for bit in range(links.dp_bits - 1, 0, -1)]
    order = [("dp", bit) for bit in range(2, links.dp_bits)]
    sets = [[keep.reshape(shape), got.reshape(shape)]]
    return (yield from halve_flow(links, sets, names, order))


def back_flow(links, send, keep, rows):
    got = yield links.swap(send, Q)
    shape = (1,) + (2,) * (links.dp_bits - 1) + (rows, keep.shape[-1])
    names = [("dp", bit) for bit in range(links.dp_bits - 1, -1, -1) if bit != 2]
    order = [Y] + [("dp", bit) for bit in range(3, links.dp_bits)]
    sets = [[keep.reshape(shape), got.reshape(shape)]]
    return (yield from halve_flow(links, sets, names, order))


def spread_flow(links, parts):
    total = jnp.concatenate([add_up([term[0] for term in terms]) for terms in parts], axis=-1)
    for bit in range(2, links.seq_bits):
        got = yield links.swap(total.astype(BF), ("seq", bit))
        total = total + got.astype(F32)
    mine = links.bit(Z)
    own, other = pick(total, 0, mine).astype(BF), pick(total, 0, 1 - mine).astype(BF)
    over_x, over_z, over_both = yield (
        links.swap(own, X),
        links.swap(other, Z),
        links.swap(other, X, Z),
    )
    near = jnp.stack([own, over_x, over_z, over_both])
    far = yield links.swap(near, CORE)
    return [near, far]


def qo_flow(links, terms, rows):
    got = yield links.swap(add_up([term[0] for term in terms]).astype(BF), X)
    shape = (2,) + (2,) * links.dp_bits + (rows, QUAD)
    names = [("dp", bit) for bit in range(links.dp_bits - 1, -1, -1)]
    terms = [term.reshape(shape) for term in (*[term[1] for term in terms], got)]
    return (yield from halve_flow(links, [terms], names, [Z, Y]))


def kv_flow(links, terms, rows):
    shape = (2, 2) + (2,) * links.dp_bits + (rows, QUAD)
    mine = links.bit(Y)
    dim = 1 + links.dp_bits
    terms = [term.reshape(shape) for term in terms]
    other = add_up([pick(term, dim, 1 - mine) for term in terms]).astype(BF)
    got = yield links.swap(other, Y)
    terms = [pick(term, dim, mine) for term in terms] + [got]
    got = yield links.swap(add_up([term[0] for term in terms]).astype(BF), X)
    terms = [term[1] for term in terms] + [got]
    names = [("dp", bit) for bit in range(links.dp_bits - 1, 0, -1)]
    return (yield from halve_flow(links, [terms], names, [Z]))


def gather_flow(links, value):
    half = value.shape[0] // 2
    over_x, over_z, far = yield (
        links.swap(value, X),
        links.swap(value, Z),
        links.swap(value, CORE),
    )
    top = links.swap(over_x[:half], Z)
    bottom = links.swap(over_z[half:], X)
    rest = [links.swap(piece, CORE) for piece in (over_x, over_z)]
    top, bottom, *rest = yield (top, bottom, *rest)
    last = yield tuple(links.swap(piece, CORE) for piece in (top, bottom))
    return [value, over_x, over_z, top, bottom, far, *rest, *last]


def small_flow(links, value):
    for axis, count in (("seq", links.seq_bits), ("dp", links.dp_bits)):
        for bit in range(count):
            got = yield links.swap(value, (axis, bit))
            value = value + got
    return value


class Flow:
    def __init__(self, generator):
        self.generator = generator
        self.result = None
        self.waiting = next(generator)

    def resume(self, arrived):
        try:
            self.waiting = self.generator.send(arrived)
        except StopIteration as stop:
            self.waiting = None
            self.result = stop.value


class Fences:
    def __init__(self, token):
        self.token = token

    def __call__(self, flows, values=()):
        flows = [flow for flow in flows if flow.waiting is not None]
        self.token, arrived, values = lax.optimization_barrier(
            (self.token, [flow.waiting for flow in flows], tuple(values))
        )
        for flow, waiting in zip(flows, arrived):
            flow.resume(waiting)
        return values


def body(
    frames,
    cotangent,
    lengths,
    attend_weight,
    output_weight,
    expand_weight,
    shrink_weight,
    norm_gains,
    norm_biases,
    layer_scales,
):
    rows = frames.shape[1]
    links = Links()
    x = frames.reshape(rows, D)
    dy = cotangent.reshape(rows, D)
    member = links.seq & 3
    slot = links.bit(Z) * 4 + member
    block_rows = D // links.dp_size
    fence = Fences(lengths)

    def shifted(value, steps):
        count = links.seq_size
        pairs = [(i, i + steps) for i in range(count) if 0 <= i + steps < count]
        return lax.ppermute(value, "seq", pairs)

    def shift_flow(low_edge, high_edge):
        pair = yield (shifted(high_edge, 1), shifted(low_edge, -1))
        return pair

    dy_flow = Flow(gather_flow(links, dy))
    frames_rim = Flow(shift_flow(x[:WINDOW], x[rows - WINDOW :]))
    table_info = jnp.stack([links.seq, jnp.int32(links.seq_size * rows)]).astype(jnp.int32)
    cosine, sine, bias = tables_call(table_info, lengths, rows)
    a1, qkv = project_call(x, norm_gains, norm_biases, cosine, sine, attend_weight)
    (qkv,) = fence([frames_rim], (qkv,))
    low_frames, high_frames = frames_rim.result
    a1_rim, rim = rim_call(
        low_frames, high_frames, norm_gains, norm_biases, cosine, sine, attend_weight
    )
    (rim,) = fence([dy_flow], (rim,))
    o, lse, x1, attn, a2 = attend_call(
        qkv, rim, bias, output_weight, x, norm_gains, norm_biases, layer_scales
    )
    (a2, x1) = fence([dy_flow], (a2, x1))
    a2_flow = Flow(gather_flow(links, a2))
    act, dx1, dattn, small_feed = feed_call(
        a2, dy, x1, attn, norm_gains, layer_scales, expand_weight, shrink_weight
    )
    (dattn,) = fence([dy_flow, a2_flow], (dattn,))

    core = links.bit(CORE)
    rest_names = [("dp", bit) for bit in range(links.dp_bits - 1, -1, -1) if bit > 1]
    rest_order = rest_names[::-1]

    def heads_back(bit, grad_attn, *other_rims):
        info = jnp.stack([bit, links.bit(X)]).astype(jnp.int32)
        return attend_back_call(
            info,
            qkv,
            rim,
            bias,
            cosine,
            sine,
            lse,
            grad_attn,
            output_weight,
            a1,
            a1_rim,
            o,
            *other_rims,
        )

    def core_flow(*sends):
        got = yield tuple(links.swap(send, CORE) for send in sends)
        return got

    *send_back, send_low, send_high, qo_far, kv_far = heads_back(
        1 - core, dattn
    )
    qo_far, kv_far, dattn = fence([a2_flow], (qo_far, kv_far, dattn))
    first_flow = Flow(core_flow(qo_far, kv_far))
    *keep_back, low, high, qo_own, kv_own = heads_back(
        core, dattn, send_low, send_high
    )
    qo_own, kv_own, low, high = fence([a2_flow, first_flow], (qo_own, kv_own, low, high))
    qo_got, kv_got = first_flow.result
    rim_flow = Flow(shift_flow(low, high))
    queries_out = Flow(qo_flow(links, [qo_own, qo_got], block_rows))
    keys_values = Flow(kv_flow(links, [kv_own, kv_got], block_rows))
    slice_info = jnp.stack([slot, links.bit(Y), links.bit(Q)]).astype(jnp.int32)
    slice_info, dx1 = lax.optimization_barrier((slice_info, dx1))
    pair_send, pair_keep, back_send, back_keep = slice_call(
        slice_info,
        a2_flow.result,
        dy_flow.result,
        layer_scales,
        expand_weight,
        shrink_weight,
        rows,
        block_rows,
    )
    pair_send, back_send, dx1 = fence([rim_flow], (pair_send, back_send, dx1))
    pair = Flow(pair_flow(links, pair_send, pair_keep, block_rows))
    back = Flow(back_flow(links, back_send, back_keep, block_rows))
    from_low, from_high = rim_flow.result
    input_info = jnp.stack([core, links.bit(X)]).astype(jnp.int32)
    input_gradient, small_first = input_back_call(
        input_info,
        keep_back,
        send_back,
        from_low,
        from_high,
        x,
        dx1,
        norm_gains,
        attend_weight,
    )
    (small_first,) = fence([pair, back], (small_first,))
    small = jnp.concatenate([small_feed[:4], small_first[:2], jnp.zeros((2, D), F32)], axis=0)
    fence([queries_out, keys_values])
    small = Flow(small_flow(links, small))
    fence([queries_out, keys_values, back, small])
    fence([queries_out, keys_values, small])
    while pair.waiting is not None or back.waiting is not None:
        fence([pair, back])
    spread = Flow(spread_flow(links, pair.result + back.result))
    attends = Flow(
        attend_flow(links, queries_out.result + keys_values.result, rest_names, rest_order)
    )
    fence([attends, small])
    while attends.waiting is not None or spread.waiting is not None or small.waiting is not None:
        fence([attends, small, spread])
    member_info = member.reshape(1).astype(jnp.int32)
    attend_grad, output_grad = place_attend_call(member_info, attends.result)
    expand_grad, shrink_grad = place_call(
        slot.reshape(1).astype(jnp.int32), *spread.result
    )
    small = lax.dynamic_slice_in_dim(small.result, links.dp * block_rows, block_rows, axis=1)
    gains_grad = jnp.stack([small[4], small[1]])
    biases_grad = jnp.stack([small[5], small[2]])
    scales_grad = jnp.stack([small[3], small[0]])
    return (
        act.reshape(frames.shape),
        input_gradient.reshape(frames.shape),
        attend_grad,
        output_grad,
        expand_grad,
        shrink_grad,
        gains_grad,
        biases_grad,
        scales_grad,
    )


def solution(mesh):
    in_specs = (
        P("dp", "seq", None),
        P("dp", "seq", None),
        P("dp", None),
        P(),
        P(),
        P(),
        P(),
        P(),
        P(),
        P(),
    )
    out_specs = (
        P("dp", "seq", None),
        P("dp", "seq", None),
        P("dp", None),
        P("dp", None),
        P("dp", None),
        P(None, "dp"),
        P(None, "dp"),
        P(None, "dp"),
        P(None, "dp"),
    )
    return jax.shard_map(body, mesh=mesh, in_specs=in_specs, out_specs=out_specs, check_vma=False)
```

```python
import functools
import math

import jax
import jax.numpy as jnp
from jax import lax
from jax.experimental import pallas as pl
from jax.experimental.pallas import tpu as pltpu
from jax.sharding import PartitionSpec as P

D = 1024
HEADS = 16
HEAD_DIM = 64
FF = 4096
WINDOW = 128
QUAD = 4 * HEAD_DIM
SLICES = 8
PART = FF // SLICES
HALF = PART // 2
EPS = 1e-05
BF = jnp.bfloat16
F32 = jnp.float32
VMEM_BYTES = 58 * 1024 * 1024


def dot_nn(a, b):
    return lax.dot_general(a, b, (((1,), (0,)), ((), ())), preferred_element_type=F32)


def dot_nt(a, b):
    return lax.dot_general(a, b, (((1,), (1,)), ((), ())), preferred_element_type=F32)


def dot_tn(a, b):
    return lax.dot_general(a, b, (((0,), (0,)), ((), ())), preferred_element_type=F32)


def params(**extra):
    return pltpu.CompilerParams(vmem_limit_bytes=VMEM_BYTES, **extra)


def cost(flops, size, transcendentals=0):
    return pl.CostEstimate(
        flops=int(flops), bytes_accessed=int(size), transcendentals=int(transcendentals)
    )


def whole(shape):
    return pl.BlockSpec(shape, lambda *_: (0,) * len(shape))


def norm_stats(values):
    centered = values - jnp.mean(values, axis=-1, keepdims=True)
    inverse = lax.rsqrt(jnp.mean(centered * centered, axis=-1, keepdims=True) + EPS)
    return (centered * inverse, inverse)


def norm_back(gradient, normed, inverse, gain_row):
    scaled = gradient * gain_row
    return inverse * (
        scaled
        - jnp.mean(scaled, axis=-1, keepdims=True)
        - normed * jnp.mean(scaled * normed, axis=-1, keepdims=True)
    )


def turn(values, cosine, sine, sign):
    lane = lax.broadcasted_iota(jnp.int32, (values.shape[0], 128), 1) % HEAD_DIM
    parts = []
    for group in range(values.shape[1] // 128):
        part = values[:, group * 128 : group * 128 + 128]
        swapped = jnp.where(
            lane < HEAD_DIM // 2, pltpu.roll(part, 96, 1), pltpu.roll(part, 32, 1)
        )
        if sign > 0:
            parts.append(part * cosine + swapped * sine)
        else:
            parts.append(part * cosine - swapped * sine)
    return jnp.concatenate(parts, axis=1)


def tables_kernel(info_ref, lengths_ref, cos_ref, sin_ref, bias_ref):
    wide = cos_ref.shape[0]
    rows = wide - 2 * WINDOW
    base = info_ref[0] * rows
    total = info_ref[1]
    frame = base - WINDOW + lax.broadcasted_iota(jnp.int32, (8, wide), 1)

    def step(entry, carry):
        start, clip, begin = carry
        inside = frame >= start
        clip = clip + inside.astype(jnp.int32)
        begin = jnp.where(inside, start, begin)
        return (start + lengths_ref[0, entry], clip, begin)

    _, clip, begin = lax.fori_loop(
        0,
        lengths_ref.shape[1],
        step,
        (jnp.int32(0), jnp.full((8, wide), -1, jnp.int32), jnp.zeros((8, wide), jnp.int32)),
    )
    query_clip = clip[0:1, WINDOW : WINDOW + rows].astype(F32)
    clip = jnp.where((frame >= 0) & (frame < total), clip, -1).astype(F32)
    place = (frame - begin).astype(F32)
    key_clip = jnp.broadcast_to(clip[0:1, :], (128, wide)).T
    half = HEAD_DIM // 2
    pack = 128 // half
    part = wide // pack
    packed = jnp.concatenate(
        [
            jnp.broadcast_to(place[0:1, at * part : at * part + part], (half, part))
            for at in range(pack)
        ],
        axis=0,
    ).T
    lane = lax.broadcasted_iota(jnp.int32, (part, 128), 1)
    frequency = jnp.exp((lane % half).astype(F32) * (-2.0 * math.log(10000.0) / HEAD_DIM))
    angle = packed * frequency
    sine, cosine = jnp.sin(angle), jnp.cos(angle)
    sign = jnp.where(lane % HEAD_DIM < half, -1.0, 1.0)
    for at in range(pack):
        for source, target, factor in ((cosine, cos_ref, None), (sine, sin_ref, sign)):
            value = pltpu.roll(source, (128 - at * half) % 128, 1) if at else source
            value = jnp.where(lane < half, value, 0.0)
            value = value + pltpu.roll(value, half, 1)
            value = value + pltpu.roll(value, 2 * half, 1)
            target[at * part : at * part + part, :] = value if factor is None else value * factor
    span = 3 * WINDOW
    gap = lax.broadcasted_iota(jnp.int32, (span, 128), 0) - lax.broadcasted_iota(
        jnp.int32, (span, 128), 1
    )
    near = (gap >= 0) & (gap <= 2 * WINDOW)
    for block in range(rows // WINDOW):
        at = block * WINDOW
        same = key_clip[at : at + span] == query_clip[:, at : at + WINDOW]
        bias_ref[block] = jnp.where(near & same, 0.0, -1e30)


def tables_call(info, lengths, rows):
    wide = rows + 2 * WINDOW
    return pl.pallas_call(
        tables_kernel,
        out_shape=(
            jax.ShapeDtypeStruct((wide, 128), F32),
            jax.ShapeDtypeStruct((wide, 128), F32),
            jax.ShapeDtypeStruct((rows // WINDOW, 3 * WINDOW, 128), F32),
        ),
        in_specs=[
            pl.BlockSpec(memory_space=pltpu.SMEM),
            pl.BlockSpec(memory_space=pltpu.SMEM),
        ],
        compiler_params=params(),
        cost_estimate=cost(1e8, 2e6),
        name="tables",
    )(info, lengths)


def project_kernel(x_ref, gain_ref, shift_ref, cos_ref, sin_ref, weight_ref, a1_ref, out_ref):
    chunk = pl.program_id(0)
    rows = x_ref.shape[0]

    @pl.when(chunk == 0)
    def _():
        normed, _unused = norm_stats(x_ref[...].astype(F32))
        a1_ref[...] = (normed * gain_ref[0:1, :] + shift_ref[0:1, :]).astype(BF)

    projected = dot_nn(a1_ref[...], weight_ref[...])
    cosine = cos_ref[WINDOW : WINDOW + rows, :]
    sine = sin_ref[WINDOW : WINDOW + rows, :]

    @pl.when(chunk == 0)
    def _():
        out_ref[...] = (turn(projected, cosine, sine, 1) * HEAD_DIM**-0.5).astype(BF)

    @pl.when(chunk == 1)
    def _():
        out_ref[...] = turn(projected, cosine, sine, 1).astype(BF)

    @pl.when(chunk == 2)
    def _():
        out_ref[...] = projected.astype(BF)


def project_call(x, gains, shifts, cosine, sine, weight):
    rows = x.shape[0]
    wide = cosine.shape[0]
    return pl.pallas_call(
        project_kernel,
        grid=(3,),
        out_shape=(
            jax.ShapeDtypeStruct((rows, D), BF),
            jax.ShapeDtypeStruct((rows, 3 * D), BF),
        ),
        in_specs=[
            whole((rows, D)),
            whole((2, D)),
            whole((2, D)),
            whole((wide, 128)),
            whole((wide, 128)),
            pl.BlockSpec((D, D), lambda c: (0, c)),
        ],
        out_specs=(whole((rows, D)), pl.BlockSpec((rows, D), lambda c: (0, c))),
        compiler_params=params(),
        cost_estimate=cost(2 * rows * D * 3 * D, 12e6),
        name="project",
    )(x, gains, shifts, cosine, sine, weight)


def rim_kernel(
    low_ref, high_ref, gain_ref, shift_ref, cos_ref, sin_ref, weight_ref, a1_ref, out_ref
):
    chunk = pl.program_id(0)
    wide = cos_ref.shape[0]

    @pl.when(chunk == 0)
    def _():
        for at, ref in ((0, low_ref), (WINDOW, high_ref)):
            normed, _unused = norm_stats(ref[...].astype(F32))
            a1_ref[at : at + WINDOW, :] = (
                normed * gain_ref[0:1, :] + shift_ref[0:1, :]
            ).astype(BF)

    projected = dot_nn(a1_ref[...], weight_ref[...])

    @pl.when(chunk == 0)
    def _():
        cosine = jnp.concatenate([cos_ref[:WINDOW, :], cos_ref[wide - WINDOW :, :]], axis=0)
        sine = jnp.concatenate([sin_ref[:WINDOW, :], sin_ref[wide - WINDOW :, :]], axis=0)
        out_ref[...] = turn(projected, cosine, sine, 1).astype(BF)

    @pl.when(chunk == 1)
    def _():
        out_ref[...] = projected.astype(BF)


def rim_call(low, high, gains, shifts, cosine, sine, weight):
    wide = cosine.shape[0]
    return pl.pallas_call(
        rim_kernel,
        grid=(2,),
        out_shape=(
            jax.ShapeDtypeStruct((2 * WINDOW, D), BF),
            jax.ShapeDtypeStruct((2 * WINDOW, 2 * D), BF),
        ),
        in_specs=[
            whole((WINDOW, D)),
            whole((WINDOW, D)),
            whole((2, D)),
            whole((2, D)),
            whole((wide, 128)),
            whole((wide, 128)),
            pl.BlockSpec((D, D), lambda c: (0, c + 1)),
        ],
        out_specs=(whole((2 * WINDOW, D)), pl.BlockSpec((2 * WINDOW, D), lambda c: (0, c))),
        compiler_params=params(),
        cost_estimate=cost(2 * 256 * D * 2 * D, 6e6),
        name="rim",
    )(low, high, gains, shifts, cosine, sine, weight)


def stacked(block):
    owner = lax.broadcasted_iota(jnp.int32, block.shape, 1) // HEAD_DIM
    zero = jnp.zeros_like(block)
    return jnp.concatenate([jnp.where(owner == head, block, zero) for head in range(4)], axis=0)


def own_lanes(block):
    rows = block.shape[0] // 4
    owner = lax.broadcasted_iota(jnp.int32, (rows, QUAD), 1) // HEAD_DIM
    total = block[:rows]
    for head in range(1, 4):
        total = jnp.where(owner == head, block[head * rows : head * rows + rows], total)
    return total


def attend_kernel(
    q_ref,
    k_ref,
    v_ref,
    rim_k_ref,
    rim_v_ref,
    bias_ref,
    weight_ref,
    x_ref,
    gain_ref,
    shift_ref,
    scale_ref,
    o_ref,
    lse_ref,
    x1_ref,
    attn_ref,
    a2_ref,
    keys,
    values,
    mixed_all,
    total,
):
    quad = pl.program_id(0)
    rows = q_ref.shape[0]
    keys[0:WINDOW, :] = rim_k_ref[0:WINDOW, :]
    keys[WINDOW : WINDOW + rows, :] = k_ref[...]
    keys[WINDOW + rows :, :] = rim_k_ref[WINDOW:, :]
    values[0:WINDOW, :] = rim_v_ref[0:WINDOW, :]
    values[WINDOW : WINDOW + rows, :] = v_ref[...]
    values[WINDOW + rows :, :] = rim_v_ref[WINDOW:, :]
    for block in range(rows // WINDOW):
        at = block * WINDOW
        queries = stacked(q_ref[at : at + WINDOW, :])
        scores = dot_nt(keys[at : at + 3 * WINDOW, :], queries)
        bias = bias_ref[block]
        scores = scores + jnp.concatenate([bias] * 4, axis=1)
        top = jnp.max(scores, axis=0, keepdims=True)
        weights = jnp.exp(scores - top)
        total_row = jnp.sum(weights, axis=0, keepdims=True)
        weights = (weights * (1.0 / total_row)).astype(BF)
        log_row = top + jnp.log(total_row)
        for head in range(4):
            lanes = slice(head * WINDOW, head * WINDOW + WINDOW)
            lse_ref[0, head : head + 1, at : at + WINDOW] = log_row[:, lanes]
        mixed_all[at : at + WINDOW, :] = own_lanes(
            dot_tn(weights, values[at : at + 3 * WINDOW, :])
        ).astype(BF)
    mixed = mixed_all[...]
    o_ref[...] = mixed
    branch = dot_nn(mixed, weight_ref[...])

    @pl.when(quad == 0)
    def _():
        total[...] = branch

    @pl.when(quad > 0)
    def _():
        total[...] += branch

    @pl.when(quad == HEADS // 4 - 1)
    def _():
        attn = total[...]
        residual = x_ref[...].astype(F32) + attn * scale_ref[0:1, :]
        normed, _unused = norm_stats(residual)
        x1_ref[...] = residual
        attn_ref[...] = attn.astype(BF)
        a2_ref[...] = (normed * gain_ref[1:2, :] + shift_ref[1:2, :]).astype(BF)


def attend_call(qkv, rim, bias, weight, x, gains, shifts, scales):
    rows = x.shape[0]
    wide = rows + 2 * WINDOW
    row_spec = whole((rows, D))
    return pl.pallas_call(
        attend_kernel,
        grid=(HEADS // 4,),
        out_shape=(
            jax.ShapeDtypeStruct((rows, D), BF),
            jax.ShapeDtypeStruct((HEADS // 4, 8, rows), F32),
            jax.ShapeDtypeStruct((rows, D), F32),
            jax.ShapeDtypeStruct((rows, D), BF),
            jax.ShapeDtypeStruct((rows, D), BF),
        ),
        in_specs=[
            pl.BlockSpec((rows, QUAD), lambda h: (0, h)),
            pl.BlockSpec((rows, QUAD), lambda h: (0, h + 4)),
            pl.BlockSpec((rows, QUAD), lambda h: (0, h + 8)),
            pl.BlockSpec((2 * WINDOW, QUAD), lambda h: (0, h)),
            pl.BlockSpec((2 * WINDOW, QUAD), lambda h: (0, h + 4)),
            whole(bias.shape),
            pl.BlockSpec((QUAD, D), lambda h: (h, 0)),
            row_spec,
            whole((2, D)),
            whole((2, D)),
            whole((2, D)),
        ],
        out_specs=(
            pl.BlockSpec((rows, QUAD), lambda h: (0, h)),
            pl.BlockSpec((1, 8, rows), lambda h: (h, 0, 0)),
            row_spec,
            row_spec,
            row_spec,
        ),
        scratch_shapes=[
            pltpu.VMEM((wide, QUAD), BF),
            pltpu.VMEM((wide, QUAD), BF),
            pltpu.VMEM((rows, QUAD), BF),
            pltpu.VMEM((rows, D), F32),
        ],
        compiler_params=params(),
        cost_estimate=cost(8e9, 14e6, 3e6),
        name="attend",
    )(qkv, qkv, qkv, rim, rim, bias, weight, x, gains, shifts, scales)


def gated(gate, up, grad_hidden):
    sigmoid = 0.5 * jnp.tanh(0.5 * gate) + 0.5
    swish = gate * sigmoid
    hidden = swish * up
    grad_gate = grad_hidden * up * (sigmoid + swish * (1.0 - sigmoid))
    grad_up = grad_hidden * swish
    return (hidden.astype(BF), grad_gate.astype(BF), grad_up.astype(BF))


def feed_kernel(
    a2_ref,
    dy_ref,
    gain_ref,
    scale_ref,
    x1_hbm,
    attn_hbm,
    expand_hbm,
    shrink_hbm,
    act_hbm,
    dx1_ref,
    dattn_ref,
    small_ref,
    expand,
    shrink,
    hidden,
    grads,
    x1,
    attn,
    act,
    sems,
    late_sems,
):
    width = 512
    step = 256
    groups = FF // width
    copies = []
    for group in range(groups):
        at = group * width
        copies.append(
            [
                pltpu.make_async_copy(
                    expand_hbm.at[:, pl.ds(at, width)],
                    expand.at[:, pl.ds(at, width)],
                    sems.at[group, 0],
                ),
                pltpu.make_async_copy(
                    expand_hbm.at[:, pl.ds(FF + at, width)],
                    expand.at[:, pl.ds(FF + at, width)],
                    sems.at[group, 1],
                ),
                pltpu.make_async_copy(
                    shrink_hbm.at[pl.ds(at, width), :],
                    shrink.at[pl.ds(at, width), :],
                    sems.at[group, 2],
                ),
            ]
        )
    late = [
        pltpu.make_async_copy(x1_hbm, x1, late_sems.at[0]),
        pltpu.make_async_copy(attn_hbm, attn, late_sems.at[1]),
    ]
    ahead = 3
    for group in range(ahead):
        for copy in copies[group]:
            copy.start()
    branch_grad = (dy_ref[...].astype(F32) * scale_ref[1:2, :]).astype(BF)
    a2 = a2_ref[...]

    for chunk in range(FF // step):
        at = chunk * step
        if at % width == 0:
            group = at // width
            if group + ahead < groups:
                for copy in copies[group + ahead]:
                    copy.start()
            elif group + ahead == groups:
                for copy in late:
                    copy.start()
            for copy in copies[group]:
                copy.wait()
        gate = dot_nn(a2, expand[:, at : at + step])
        up = dot_nn(a2, expand[:, FF + at : FF + at + step])
        grad_hidden = dot_nt(branch_grad, shrink[at : at + step, :])
        out, grad_gate, grad_up = gated(gate, up, grad_hidden)
        hidden[:, at : at + step] = out
        grads[:, at : at + step] = grad_gate
        grads[:, FF + at : FF + at + step] = grad_up
    branch = dot_nn(hidden[...], shrink[...])
    for copy in late:
        copy.wait()
    residual = x1[...]
    grad_result = dy_ref[...].astype(F32)
    act[...] = (residual + branch * scale_ref[1:2, :]).astype(BF)
    out_copy = pltpu.make_async_copy(act, act_hbm, late_sems.at[2])
    out_copy.start()
    small_ref[0:1, :] = jnp.sum(grad_result * branch, axis=0, keepdims=True)
    grad_normed = dot_nt(grads[...], expand[...])
    normed, inverse = norm_stats(residual)
    small_ref[1:2, :] = jnp.sum(grad_normed * normed, axis=0, keepdims=True)
    small_ref[2:3, :] = jnp.sum(grad_normed, axis=0, keepdims=True)
    grad_residual = grad_result + norm_back(grad_normed, normed, inverse, gain_ref[1:2, :])
    dx1_ref[...] = grad_residual
    small_ref[3:4, :] = jnp.sum(grad_residual * attn[...].astype(F32), axis=0, keepdims=True)
    small_ref[4:8, :] = jnp.zeros((4, D), F32)
    dattn_ref[...] = (grad_residual * scale_ref[0:1, :]).astype(BF)
    out_copy.wait()


def feed_call(a2, dy, x1, attn, gains, scales, expand, shrink):
    rows = a2.shape[0]
    vmem = pl.BlockSpec(memory_space=pltpu.VMEM)
    hbm = pl.BlockSpec(memory_space=pl.ANY)
    return pl.pallas_call(
        feed_kernel,
        out_shape=(
            jax.ShapeDtypeStruct((rows, D), BF),
            jax.ShapeDtypeStruct((rows, D), F32),
            jax.ShapeDtypeStruct((rows, D), BF),
            jax.ShapeDtypeStruct((8, D), F32),
        ),
        in_specs=[vmem] * 4 + [hbm] * 4,
        out_specs=(hbm, vmem, vmem, vmem),
        scratch_shapes=[
            pltpu.VMEM((D, 2 * FF), BF),
            pltpu.VMEM((FF, D), BF),
            pltpu.VMEM((rows, FF), BF),
            pltpu.VMEM((rows, 2 * FF), BF),
            pltpu.VMEM((rows, D), F32),
            pltpu.VMEM((rows, D), BF),
            pltpu.VMEM((rows, D), BF),
            pltpu.SemaphoreType.DMA((FF // 512, 3)),
            pltpu.SemaphoreType.DMA((3,)),
        ],
        compiler_params=params(),
        cost_estimate=cost(2 * rows * D * FF * 6, 36e6, rows * FF),
        name="feed",
    )(a2, dy, gains, scales, x1, attn, expand, shrink)


def slice_kernel(pieces, info_ref, *refs):
    a2_refs = refs[: len(pieces)]
    dy_refs = refs[len(pieces) : 2 * len(pieces)]
    scale_ref, gate_w_ref, up_w_ref, shrink_w_ref = refs[2 * len(pieces) : 2 * len(pieces) + 4]
    pair_send, pair_keep, back_send, back_keep = refs[2 * len(pieces) + 4 :][:4]
    a2_all, dm_all, inner, result, sems = refs[2 * len(pieces) + 8 :]
    size = gate_w_ref.shape[1]
    groups = 1 + max(slot for slot, _, _ in pieces)
    rows = a2_all.shape[0] // groups
    copies = [[] for _ in range(groups)]
    for number, (slot, first, count) in enumerate(pieces):
        for kind, (sources, held) in enumerate(((a2_refs, a2_all), (dy_refs, dm_all))):
            copies[slot].append(
                pltpu.make_async_copy(
                    sources[number],
                    held.at[pl.ds(slot * rows + first, count), :],
                    sems.at[kind, number],
                )
            )
    for slot in range(min(2, groups)):
        for copy in copies[slot]:
            copy.start()
    scale = scale_ref[1:2, :]
    for slot in range(groups):
        if slot + 2 < groups:
            for copy in copies[slot + 2]:
                copy.start()
        for copy in copies[slot]:
            copy.wait()
        span = slice(slot * rows, slot * rows + rows)
        branch_grad = (dm_all[span, :].astype(F32) * scale).astype(BF)
        dm_all[span, :] = branch_grad
        gate = dot_nn(a2_all[span, :], gate_w_ref[...])
        up = dot_nn(a2_all[span, :], up_w_ref[...])
        grad_hidden = dot_nt(branch_grad, shrink_w_ref[...])
        hidden, grad_gate, grad_up = gated(gate, up, grad_hidden)
        inner[span, :size] = grad_gate
        inner[span, size : 2 * size] = grad_up
        inner[span, 2 * size :] = hidden
    result[:, : 2 * size] = dot_tn(a2_all[...], inner[:, : 2 * size]).astype(BF)
    result[:, 2 * size :] = dot_tn(dm_all[...], inner[:, 2 * size :]).astype(BF)
    columns = (slice(0, 2 * size), slice(2 * size, 3 * size))
    for lanes, mine, send_ref, keep_ref in (
        (columns[0], info_ref[1], pair_send, pair_keep),
        (columns[1], info_ref[2], back_send, back_keep),
    ):
        outer, span, _ = send_ref.shape
        for at in range(outer):
            for target, bit in ((send_ref, 1 - mine), (keep_ref, mine)):
                first = pl.multiple_of(at * 2 * span + bit * span, span)
                target[at] = result[pl.ds(first, span), lanes]


def slice_call(info, a2_list, dy_list, scales, expand, shrink, rows, block_rows):
    size = PART
    pieces = []
    slot, first = 0, 0
    for piece in a2_list:
        pieces.append((slot, first, piece.shape[0]))
        first += piece.shape[0]
        if first == rows:
            slot, first = slot + 1, 0
    groups = slot
    hbm = pl.BlockSpec(memory_space=pl.ANY)
    pair_shape = (D // (2 * block_rows), block_rows, 2 * size)
    back_shape = (D // (8 * block_rows), 4 * block_rows, size)
    shapes = (pair_shape, pair_shape, back_shape, back_shape)
    return pl.pallas_call(
        functools.partial(slice_kernel, tuple(pieces)),
        grid_spec=pltpu.PrefetchScalarGridSpec(
            num_scalar_prefetch=1,
            grid=(1,),
            in_specs=[hbm] * (2 * len(pieces))
            + [
                pl.BlockSpec((2, D), lambda i, info: (0, 0)),
                pl.BlockSpec((D, size), lambda i, info: (0, info[0])),
                pl.BlockSpec((D, size), lambda i, info: (0, info[0] + FF // size)),
                pl.BlockSpec((size, D), lambda i, info: (info[0], 0)),
            ],
            out_specs=[pl.BlockSpec(shape, lambda i, info: (0, 0, 0)) for shape in shapes],
            scratch_shapes=[
                pltpu.VMEM((groups * rows, D), BF),
                pltpu.VMEM((groups * rows, D), BF),
                pltpu.VMEM((groups * rows, 3 * size), BF),
                pltpu.VMEM((D, 3 * size), BF),
                pltpu.SemaphoreType.DMA((2, len(pieces))),
            ],
        ),
        out_shape=[jax.ShapeDtypeStruct(shape, BF) for shape in shapes],
        compiler_params=params(),
        cost_estimate=cost(2 * groups * rows * D * size * 6, 22e6, groups * rows * size),
        name="slice_grads",
    )(info, *a2_list, *dy_list, scales, expand, expand, shrink)


def attend_back_kernel(
    last,
    info_ref,
    q_ref,
    k_ref,
    v_ref,
    rim_k_ref,
    rim_v_ref,
    bias_ref,
    cos_ref,
    sin_ref,
    lse_ref,
    dattn_ref,
    dattn_part_ref,
    weight_ref,
    a1_ref,
    a1_rim_ref,
    o_ref,
    *refs,
):
    if last:
        other_low, other_high, *refs = refs
    dq_ref, dk_ref, dv_ref, low_ref, high_ref, *refs = refs
    qo_ref, kv_ref, *refs = refs
    a1, keys, values, keys_t, grad_q_t, grad_k, grad_v = refs
    step = pl.program_id(0)

    def deliver(block, grad):
        if block < 2:
            qo_ref[0, block] = grad.astype(BF)
            return
        kv_ref[0, block - 2] = grad.astype(BF)

    rows = q_ref.shape[0]
    low, own, high = slice(0, WINDOW), slice(WINDOW, WINDOW + rows), slice(WINDOW + rows, None)

    @pl.when(step == 0)
    def _():
        a1[low, :] = a1_rim_ref[:WINDOW, :]
        a1[own, :] = a1_ref[...]
        a1[high, :] = a1_rim_ref[WINDOW:, :]

    for held, mine, rim in ((keys, k_ref, rim_k_ref), (values, v_ref, rim_v_ref)):
        held[low, :] = rim[:WINDOW, :]
        held[own, :] = mine[...]
        held[high, :] = rim[WINDOW:, :]
    keys_t[...] = keys[...].T
    grad_mixed = dot_nt(dattn_ref[...], weight_ref[...]).astype(BF)
    deliver(1, dot_tn(o_ref[...], dattn_part_ref[...]))
    grad_k[...] = jnp.zeros_like(grad_k)
    grad_v[...] = jnp.zeros_like(grad_v)
    for block in range(rows // WINDOW):
        at = block * WINDOW
        span = slice(at, at + 3 * WINDOW)
        queries = stacked(q_ref[at : at + WINDOW, :])
        grad_out = stacked(grad_mixed[at : at + WINDOW, :])
        scores = dot_nt(keys[span, :], queries)
        log_row = jnp.concatenate(
            [lse_ref[0, head : head + 1, at : at + WINDOW] for head in range(4)], axis=1
        )
        bias = bias_ref[block]
        weights = jnp.exp(scores + jnp.concatenate([bias] * 4, axis=1) - log_row)
        grad_weights = dot_nt(values[span, :], grad_out)
        weighted = weights * grad_weights
        grad_scores = weighted - weights * jnp.sum(weighted, axis=0, keepdims=True)
        grad_scores = grad_scores.astype(BF)
        grad_v[span, :] += dot_nn(weights.astype(BF), grad_out)
        grad_k[span, :] += dot_nn(grad_scores, queries)
        for head in range(4):
            feature = slice(head * HEAD_DIM, head * HEAD_DIM + HEAD_DIM)
            grad_q_t[feature, at : at + WINDOW] = dot_nn(
                keys_t[feature, span], grad_scores[:, head * WINDOW : head * WINDOW + WINDOW]
            )
    cosine, sine = cos_ref[...], sin_ref[...]
    grad_q = turn(grad_q_t[...].T * HEAD_DIM**-0.5, cosine[own, :], sine[own, :], -1).astype(BF)
    turned = turn(grad_k[...], cosine, sine, -1).astype(BF)
    grad_values = grad_v[...].astype(BF)
    deliver(0, dot_tn(a1_ref[...], grad_q))
    deliver(2, dot_tn(a1[...], turned))
    deliver(3, dot_tn(a1[...], grad_values))
    dq_ref[0] = grad_q
    dk_ref[0] = turned[own, :]
    dv_ref[0] = grad_values[own, :]
    for target, span in ((low_ref, low), (high_ref, high)):
        target[0, 0, 0] = turned[span, :]
        target[0, 1, 0] = grad_values[span, :]
    if last:
        low_ref[1] = other_low[0]
        high_ref[1] = other_high[0]


def attend_back_call(
    info, qkv, rim, bias, cosine, sine, lse, dattn, weight, a1, a1_rim, o, *other_rims
):
    rows = dattn.shape[0]
    wide = rows + 2 * WINDOW
    last = len(other_rims) > 0
    row_shape = jax.ShapeDtypeStruct((2, rows, QUAD), BF)
    sides = 2 if last else 1
    rim_shape = jax.ShapeDtypeStruct((sides, 2, 2, WINDOW, QUAD), BF)
    row_spec = pl.BlockSpec((1, rows, QUAD), lambda s, info: (s, 0, 0))

    def quad(s, info):
        return 2 * (s ^ (1 - info[1])) + info[0]

    def rim_spec(count):
        return pl.BlockSpec(
            (count, 2, 1, WINDOW, QUAD), lambda s, info: (0, 0, s ^ (1 - info[1]), 0, 0)
        )


    def columns(count, first):
        return pl.BlockSpec((count, QUAD), lambda s, info: (0, first + quad(s, info)))

    kv_shape = jax.ShapeDtypeStruct((2, 2, D, QUAD), BF)
    kv_spec = pl.BlockSpec((1, 2, D, QUAD), lambda s, info: (s, 0, 0, 0))
    operands = [
        info,
        qkv,
        qkv,
        qkv,
        rim,
        rim,
        bias,
        cosine,
        sine,
        lse,
        dattn,
        dattn,
        weight,
        a1,
        a1_rim,
        o,
    ]
    return pl.pallas_call(
        functools.partial(attend_back_kernel, last),
        grid_spec=pltpu.PrefetchScalarGridSpec(
            num_scalar_prefetch=1,
            grid=(2,),
            in_specs=[
                columns(rows, 0),
                columns(rows, 4),
                columns(rows, 8),
                columns(2 * WINDOW, 0),
                columns(2 * WINDOW, 4),
                whole(bias.shape),
                whole((wide, 128)),
                whole((wide, 128)),
                pl.BlockSpec((1, 8, rows), lambda s, info: (quad(s, info), 0, 0)),
                whole((rows, D)),
                columns(rows, 0),
                pl.BlockSpec((QUAD, D), lambda s, info: (quad(s, info), 0)),
                whole((rows, D)),
                whole((2 * WINDOW, D)),
                whole((rows, D)),
            ]
            + [rim_spec(1)] * len(other_rims),
            out_specs=[row_spec] * 3 + [rim_spec(sides)] * 2 + [kv_spec] * 2,
            scratch_shapes=[
                pltpu.VMEM((wide, D), BF),
                pltpu.VMEM((wide, QUAD), BF),
                pltpu.VMEM((wide, QUAD), BF),
                pltpu.VMEM((QUAD, wide), BF),
                pltpu.VMEM((QUAD, rows), F32),
                pltpu.VMEM((wide, QUAD), F32),
                pltpu.VMEM((wide, QUAD), F32),
            ],
        ),
        out_shape=[row_shape] * 3
        + [rim_shape] * 2
        + [kv_shape] * 2,
        compiler_params=params(),
        cost_estimate=cost(1e6, 1e6),
        name="attend_back",
    )(*operands, *other_rims)


def input_back_kernel(
    info_ref,
    keep_q,
    keep_k,
    keep_v,
    send_q,
    send_k,
    send_v,
    low_ref,
    high_ref,
    gain_ref,
    weight_ref,
    x_hbm,
    dx1_hbm,
    grad_ref,
    small_ref,
    part,
    back,
    x,
    dx1,
    sems,
):
    chunk = pl.program_id(0)
    rows = x.shape[0]
    late = [
        pltpu.make_async_copy(x_hbm, x, sems.at[0]),
        pltpu.make_async_copy(dx1_hbm, dx1, sems.at[1]),
    ]

    @pl.when(chunk == 0)
    def _():
        for copy in late:
            copy.start()
        back[...] = jnp.zeros_like(back)

    for kind, pair in enumerate(((keep_q, send_q), (keep_k, send_k), (keep_v, send_v))):

        @pl.when(chunk // 2 == kind)
        def _():
            for core in range(2):

                @pl.when(info_ref[0] == core)
                def _():
                    for at, ref in ((core, pair[0]), (1 - core, pair[1])):
                        lanes = slice(at * QUAD, at * QUAD + QUAD)
                        part[:, lanes] = ref[0]

            if kind > 0:
                for core in range(2):

                    @pl.when(info_ref[0] == core)
                    def _():
                        for at, which in ((core, 1), (1 - core, 0)):
                            lanes = slice(at * QUAD, at * QUAD + QUAD)
                            for first, rim in ((0, low_ref), (rows - WINDOW, high_ref)):
                                span = slice(first, first + WINDOW)
                                part[span, lanes] = (
                                    part[span, lanes].astype(F32)
                                    + rim[which, 0, 0].astype(F32)
                                ).astype(BF)

    back[...] += dot_nt(part[...], weight_ref[...])

    @pl.when(chunk == pl.num_programs(0) - 1)
    def _():
        for copy in late:
            copy.wait()
        grad_normed = back[...]
        normed, inverse = norm_stats(x[...].astype(F32))
        small_ref[0:1, :] = jnp.sum(grad_normed * normed, axis=0, keepdims=True)
        small_ref[1:2, :] = jnp.sum(grad_normed, axis=0, keepdims=True)
        small_ref[2:8, :] = jnp.zeros((6, D), F32)
        grad_ref[...] = (
            dx1[...] + norm_back(grad_normed, normed, inverse, gain_ref[0:1, :])
        ).astype(BF)


def input_back_call(info, keep, send, low, high, x, dx1, gains, weight):
    rows = x.shape[0]

    def own_spec(kind):
        return pl.BlockSpec((1, rows, QUAD), lambda c, info: (c % 2, 0, 0))

    rim_spec = pl.BlockSpec(
        (2, 1, 1, WINDOW, QUAD),
        lambda c, info: (0, jnp.maximum(c // 2 - 1, 0), (c % 2) ^ (1 - info[1]), 0, 0),
    )
    hbm = pl.BlockSpec(memory_space=pl.ANY)
    return pl.pallas_call(
        input_back_kernel,
        grid_spec=pltpu.PrefetchScalarGridSpec(
            num_scalar_prefetch=1,
            grid=(6,),
            in_specs=[own_spec(kind) for kind in range(6)]
            + [
                rim_spec,
                rim_spec,
                whole((2, D)),
                pl.BlockSpec(
                    (D, 2 * QUAD),
                    lambda c, info: (0, c // 2 * 2 + ((c % 2) ^ (1 - info[1]))),
                ),
                hbm,
                hbm,
            ],
            out_specs=(whole((rows, D)), whole((8, D))),
            scratch_shapes=[
                pltpu.VMEM((rows, 2 * QUAD), BF),
                pltpu.VMEM((rows, D), F32),
                pltpu.VMEM((rows, D), BF),
                pltpu.VMEM((rows, D), F32),
                pltpu.SemaphoreType.DMA((2,)),
            ],
        ),
        out_shape=(
            jax.ShapeDtypeStruct((rows, D), BF),
            jax.ShapeDtypeStruct((8, D), F32),
        ),
        compiler_params=params(),
        cost_estimate=cost(1e6, 1e6),
        name="input_back",
    )(info, *keep, *send, low, high, gains, weight, x, dx1)


def place_kernel(info_ref, near_ref, far_ref, expand_ref, shrink_ref):
    for core, ref in enumerate((near_ref, far_ref)):
        for at in range(4):
            flip = 4 * (at >> 1) + 2 * (at & 1) + core
            first = pl.multiple_of((info_ref[0] ^ flip) * PART, PART)
            expand_ref[:, pl.ds(first, PART)] = ref[at, :, :PART].astype(F32)
            expand_ref[:, pl.ds(pl.multiple_of(FF + first, PART), PART)] = ref[
                at, :, PART : 2 * PART
            ].astype(F32)
            shrink_ref[pl.ds(first, PART), :] = ref[at, :, 2 * PART :].astype(F32).T


def place_call(info, near, far):
    rows = near.shape[1]
    vmem = pl.BlockSpec(memory_space=pltpu.VMEM)
    return pl.pallas_call(
        place_kernel,
        in_specs=[pl.BlockSpec(memory_space=pltpu.SMEM), vmem, vmem],
        out_shape=(
            jax.ShapeDtypeStruct((rows, 2 * FF), F32),
            jax.ShapeDtypeStruct((FF, rows), F32),
        ),
        compiler_params=params(),
        cost_estimate=cost(1e6, 10e6),
        name="place_feed",
    )(info, near, far)


def place_attend_kernel(count, info_ref, *refs):
    attend_ref, output_ref = refs[count:]
    slot = info_ref[0]
    for flip in range(count):
        at = (slot ^ flip) * QUAD
        for block in range(4):
            value = refs[flip][block].astype(F32)
            if block == 1:
                output_ref[:, pl.ds(pl.multiple_of(at, QUAD), QUAD)] = value
            else:
                column = max(block - 1, 0) * D + at
                attend_ref[:, pl.ds(pl.multiple_of(column, QUAD), QUAD)] = value


def place_attend_call(info, pieces):
    rows = pieces[0].shape[1]
    vmem = pl.BlockSpec(memory_space=pltpu.VMEM)
    return pl.pallas_call(
        functools.partial(place_attend_kernel, len(pieces)),
        in_specs=[pl.BlockSpec(memory_space=pltpu.SMEM)] + [vmem] * len(pieces),
        out_shape=(
            jax.ShapeDtypeStruct((rows, 3 * D), F32),
            jax.ShapeDtypeStruct((rows, D), F32),
        ),
        compiler_params=params(),
        cost_estimate=cost(1e6, 4e6),
        name="place_attend",
    )(info, *pieces)


def add_up(terms):
    total = terms[0].astype(F32)
    for term in terms[1:]:
        total = total + term.astype(F32)
    return total


class Links:
    def __init__(self):
        self.dp_size = lax.axis_size("dp")
        self.seq_size = lax.axis_size("seq")
        self.dp = lax.axis_index("dp")
        self.seq = lax.axis_index("seq")
        self.dp_bits = self.dp_size.bit_length() - 1
        self.seq_bits = self.seq_size.bit_length() - 1

    def swap(self, value, *names):
        flips = {"dp": 0, "seq": 0}
        for axis, bit in names:
            flips[axis] ^= 1 << bit
        pairs = []
        for dp in range(self.dp_size):
            for seq in range(self.seq_size):
                target = (dp ^ flips["dp"]) * self.seq_size + (seq ^ flips["seq"])
                pairs.append((dp * self.seq_size + seq, target))
        return lax.ppermute(value, ("dp", "seq"), pairs)

    def bit(self, name):
        return ((self.dp if name[0] == "dp" else self.seq) >> name[1]) & 1


CORE = ("seq", 0)
X = ("seq", 1)
Y = ("dp", 0)
Z = ("dp", 1)
Q = ("dp", 2)


def pick(value, dim, index):
    return lax.dynamic_index_in_dim(value, index, dim, keepdims=False)


def halve_flow(links, sets, names, order):
    for name in order:
        dim = 1 + names.index(name)
        mine = links.bit(name)
        other = [add_up([pick(term, dim, 1 - mine) for term in terms]) for terms in sets]
        other = other[0] if len(other) == 1 else jnp.concatenate(other, axis=0)
        got = yield links.swap(other.astype(BF), name)
        sets = [[pick(term, dim, mine) for term in terms] for terms in sets]
        first = 0
        for terms in sets:
            count = terms[0].shape[0]
            terms.append(got[first : first + count])
            first += count
        names = names[: dim - 1] + names[dim:]
    return sets


def total_flow(links, sets):
    total = [add_up(terms) for terms in sets]
    total = total[0] if len(total) == 1 else jnp.concatenate(total, axis=0)
    for bit in range(2, links.seq_bits):
        got = yield links.swap(total.astype(BF), ("seq", bit))
        total = total + got.astype(F32)
    return total.astype(BF)


def attend_flow(links, sets, names, order):
    sets = yield from halve_flow(links, sets, names, order)
    total = yield from total_flow(links, sets)
    near, across = yield (links.swap(total, CORE), links.swap(total, X))
    far = yield links.swap(across, CORE)
    return [total, near, across, far]


def pair_flow(links, send, keep, rows):
    got = yield links.swap(send, Y)
    shape = (1,) + (2,) * (links.dp_bits - 1) + (rows, keep.shape[-1])
    names = [("dp", bit) for bit in range(links.dp_bits - 1, 0, -1)]
    order = [("dp", bit) for bit in range(2, links.dp_bits)]
    sets = [[keep.reshape(shape), got.reshape(shape)]]
    return (yield from halve_flow(links, sets, names, order))


def back_flow(links, send, keep, rows):
    got = yield links.swap(send, Q)
    shape = (1,) + (2,) * (links.dp_bits - 1) + (rows, keep.shape[-1])
    names = [("dp", bit) for bit in range(links.dp_bits - 1, -1, -1) if bit != 2]
    order = [Y] + [("dp", bit) for bit in range(3, links.dp_bits)]
    sets = [[keep.reshape(shape), got.reshape(shape)]]
    return (yield from halve_flow(links, sets, names, order))


def spread_flow(links, parts):
    total = jnp.concatenate([add_up([term[0] for term in terms]) for terms in parts], axis=-1)
    for bit in range(2, links.seq_bits):
        got = yield links.swap(total.astype(BF), ("seq", bit))
        total = total + got.astype(F32)
    mine = links.bit(Z)
    own, other = pick(total, 0, mine).astype(BF), pick(total, 0, 1 - mine).astype(BF)
    over_x, over_z, over_both = yield (
        links.swap(own, X),
        links.swap(other, Z),
        links.swap(other, X, Z),
    )
    near = jnp.stack([own, over_x, over_z, over_both])
    far = yield links.swap(near, CORE)
    return [near, far]


def qo_flow(links, terms, rows):
    got = yield links.swap(add_up([term[0] for term in terms]).astype(BF), X)
    shape = (2,) + (2,) * links.dp_bits + (rows, QUAD)
    names = [("dp", bit) for bit in range(links.dp_bits - 1, -1, -1)]
    terms = [term.reshape(shape) for term in (*[term[1] for term in terms], got)]
    return (yield from halve_flow(links, [terms], names, [Z, Y]))


def kv_flow(links, terms, rows):
    shape = (2, 2) + (2,) * links.dp_bits + (rows, QUAD)
    mine = links.bit(Y)
    dim = 1 + links.dp_bits
    terms = [term.reshape(shape) for term in terms]
    other = add_up([pick(term, dim, 1 - mine) for term in terms]).astype(BF)
    got = yield links.swap(other, Y)
    terms = [pick(term, dim, mine) for term in terms] + [got]
    got = yield links.swap(add_up([term[0] for term in terms]).astype(BF), X)
    terms = [term[1] for term in terms] + [got]
    names = [("dp", bit) for bit in range(links.dp_bits - 1, 0, -1)]
    return (yield from halve_flow(links, [terms], names, [Z]))


def gather_flow(links, value):
    half = value.shape[0] // 2
    over_x, over_z, far = yield (
        links.swap(value, X),
        links.swap(value, Z),
        links.swap(value, CORE),
    )
    top = links.swap(over_x[:half], Z)
    bottom = links.swap(over_z[half:], X)
    rest = [links.swap(piece, CORE) for piece in (over_x, over_z)]
    top, bottom, *rest = yield (top, bottom, *rest)
    last = yield tuple(links.swap(piece, CORE) for piece in (top, bottom))
    return [value, over_x, over_z, top, bottom, far, *rest, *last]


def small_flow(links, value):
    for axis, count in (("seq", links.seq_bits), ("dp", links.dp_bits)):
        for bit in range(count):
            got = yield links.swap(value, (axis, bit))
            value = value + got
    return value


class Flow:
    def __init__(self, generator):
        self.generator = generator
        self.result = None
        self.waiting = next(generator)

    def resume(self, arrived):
        try:
            self.waiting = self.generator.send(arrived)
        except StopIteration as stop:
            self.waiting = None
            self.result = stop.value


class Fences:
    def __init__(self, token):
        self.token = token

    def __call__(self, flows, values=()):
        flows = [flow for flow in flows if flow.waiting is not None]
        self.token, arrived, values = lax.optimization_barrier(
            (self.token, [flow.waiting for flow in flows], tuple(values))
        )
        for flow, waiting in zip(flows, arrived):
            flow.resume(waiting)
        return values


def body(
    frames,
    cotangent,
    lengths,
    attend_weight,
    output_weight,
    expand_weight,
    shrink_weight,
    norm_gains,
    norm_biases,
    layer_scales,
):
    rows = frames.shape[1]
    links = Links()
    x = frames.reshape(rows, D)
    dy = cotangent.reshape(rows, D)
    member = links.seq & 3
    slot = links.bit(Z) * 4 + member
    block_rows = D // links.dp_size
    fence = Fences(lengths)

    def shifted(value, steps):
        count = links.seq_size
        pairs = [(i, i + steps) for i in range(count) if 0 <= i + steps < count]
        return lax.ppermute(value, "seq", pairs)

    def shift_flow(low_edge, high_edge):
        pair = yield (shifted(high_edge, 1), shifted(low_edge, -1))
        return pair

    dy_flow = Flow(gather_flow(links, dy))
    frames_rim = Flow(shift_flow(x[:WINDOW], x[rows - WINDOW :]))
    table_info = jnp.stack([links.seq, jnp.int32(links.seq_size * rows)]).astype(jnp.int32)
    cosine, sine, bias = tables_call(table_info, lengths, rows)
    a1, qkv = project_call(x, norm_gains, norm_biases, cosine, sine, attend_weight)
    (qkv,) = fence([frames_rim], (qkv,))
    low_frames, high_frames = frames_rim.result
    a1_rim, rim = rim_call(
        low_frames, high_frames, norm_gains, norm_biases, cosine, sine, attend_weight
    )
    (rim,) = fence([dy_flow], (rim,))
    o, lse, x1, attn, a2 = attend_call(
        qkv, rim, bias, output_weight, x, norm_gains, norm_biases, layer_scales
    )
    (a2, x1) = fence([dy_flow], (a2, x1))
    a2_flow = Flow(gather_flow(links, a2))
    act, dx1, dattn, small_feed = feed_call(
        a2, dy, x1, attn, norm_gains, layer_scales, expand_weight, shrink_weight
    )
    (dattn,) = fence([dy_flow, a2_flow], (dattn,))

    core = links.bit(CORE)
    rest_names = [("dp", bit) for bit in range(links.dp_bits - 1, -1, -1) if bit > 1]
    rest_order = rest_names[::-1]

    def heads_back(bit, grad_attn, *other_rims):
        info = jnp.stack([bit, links.bit(X)]).astype(jnp.int32)
        return attend_back_call(
            info,
            qkv,
            rim,
            bias,
            cosine,
            sine,
            lse,
            grad_attn,
            output_weight,
            a1,
            a1_rim,
            o,
            *other_rims,
        )

    def core_flow(*sends):
        got = yield tuple(links.swap(send, CORE) for send in sends)
        return got

    *send_back, send_low, send_high, qo_far, kv_far = heads_back(
        1 - core, dattn
    )
    qo_far, kv_far, dattn = fence([a2_flow], (qo_far, kv_far, dattn))
    first_flow = Flow(core_flow(qo_far, kv_far))
    *keep_back, low, high, qo_own, kv_own = heads_back(
        core, dattn, send_low, send_high
    )
    qo_own, kv_own, low, high = fence([a2_flow, first_flow], (qo_own, kv_own, low, high))
    qo_got, kv_got = first_flow.result
    rim_flow = Flow(shift_flow(low, high))
    queries_out = Flow(qo_flow(links, [qo_own, qo_got], block_rows))
    keys_values = Flow(kv_flow(links, [kv_own, kv_got], block_rows))
    slice_info = jnp.stack([slot, links.bit(Y), links.bit(Q)]).astype(jnp.int32)
    slice_info, dx1 = lax.optimization_barrier((slice_info, dx1))
    pair_send, pair_keep, back_send, back_keep = slice_call(
        slice_info,
        a2_flow.result,
        dy_flow.result,
        layer_scales,
        expand_weight,
        shrink_weight,
        rows,
        block_rows,
    )
    pair_send, back_send, dx1 = fence([rim_flow], (pair_send, back_send, dx1))
    pair = Flow(pair_flow(links, pair_send, pair_keep, block_rows))
    back = Flow(back_flow(links, back_send, back_keep, block_rows))
    from_low, from_high = rim_flow.result
    input_info = jnp.stack([core, links.bit(X)]).astype(jnp.int32)
    input_gradient, small_first = input_back_call(
        input_info,
        keep_back,
        send_back,
        from_low,
        from_high,
        x,
        dx1,
        norm_gains,
        attend_weight,
    )
    (small_first,) = fence([pair, back], (small_first,))
    small = jnp.concatenate([small_feed[:4], small_first[:2], jnp.zeros((2, D), F32)], axis=0)
    fence([queries_out, keys_values])
    small = Flow(small_flow(links, small))
    fence([queries_out, keys_values, back, small])
    fence([queries_out, keys_values, small])
    while pair.waiting is not None or back.waiting is not None:
        fence([pair, back])
    spread = Flow(spread_flow(links, pair.result + back.result))
    attends = Flow(
        attend_flow(links, queries_out.result + keys_values.result, rest_names, rest_order)
    )
    fence([attends, small])
    while attends.waiting is not None or spread.waiting is not None or small.waiting is not None:
        fence([attends, small, spread])
    member_info = member.reshape(1).astype(jnp.int32)
    attend_grad, output_grad = place_attend_call(member_info, attends.result)
    near, far = spread.result
    far, attend_grad, output_grad = lax.optimization_barrier((far, attend_grad, output_grad))
    expand_grad, shrink_grad = place_call(
        slot.reshape(1).astype(jnp.int32), near, far
    )
    small = lax.dynamic_slice_in_dim(small.result, links.dp * block_rows, block_rows, axis=1)
    gains_grad = jnp.stack([small[4], small[1]])
    biases_grad = jnp.stack([small[5], small[2]])
    scales_grad = jnp.stack([small[3], small[0]])
    return (
        act.reshape(frames.shape),
        input_gradient.reshape(frames.shape),
        attend_grad,
        output_grad,
        expand_grad,
        shrink_grad,
        gains_grad,
        biases_grad,
        scales_grad,
    )


def solution(mesh):
    in_specs = (
        P("dp", "seq", None),
        P("dp", "seq", None),
        P("dp", None),
        P(),
        P(),
        P(),
        P(),
        P(),
        P(),
        P(),
    )
    out_specs = (
        P("dp", "seq", None),
        P("dp", "seq", None),
        P("dp", None),
        P("dp", None),
        P("dp", None),
        P(None, "dp"),
        P(None, "dp"),
        P(None, "dp"),
        P(None, "dp"),
    )
    return jax.shard_map(body, mesh=mesh, in_specs=in_specs, out_specs=out_specs, check_vma=False)
```
